32 devices in a mesh: dp: 4 (over x, core), seq: 8 (over z, y).
Axes of the slice: x: 2, y: 2, z: 4, core: 2. Of those that a mesh axis runs over, the one named last changes fastest.
Arguments:
- inputs: bfloat16 [4, 1024, 2048], P('dp', 'seq'), may hold values from -6 to 6
- doc_lengths: int32 [4, 8], P('dp'), may hold values from 1 to 960, 1024 in all within a row
- w_query: bfloat16 [2048, 2048], P(('dp', 'seq')), may hold values from -0.125 to 0.125
- w_key: bfloat16 [2048, 2048], P(('dp', 'seq')), may hold values from -0.125 to 0.125
- w_value: bfloat16 [2048, 2048], P(('dp', 'seq')), may hold values from -0.125 to 0.125
- w_out: bfloat16 [2048, 2048], P(('dp', 'seq')), may hold values from -0.125 to 0.125
- gain_query: bfloat16 [2048], P(('dp', 'seq')), may hold values from 0.25 to 1.75
- gain_key: bfloat16 [2048], P(('dp', 'seq')), may hold values from 0.25 to 1.75
- gain_attn: bfloat16 [2048], P(('dp', 'seq')), may hold values from 0.25 to 1.75
- w_gate: bfloat16 [2048, 8192], P(('dp', 'seq')), may hold values from -0.125 to 0.125
- w_up: bfloat16 [2048, 8192], P(('dp', 'seq')), may hold values from -0.125 to 0.125
- w_down: bfloat16 [8192, 2048], P(None, ('dp', 'seq')), may hold values from -0.0625 to 0.0625
- gain_ffn: bfloat16 [2048], P(('dp', 'seq')), may hold values from 0.25 to 1.75
- cotangent: bfloat16 [4, 1024, 2048], P('dp', 'seq'), may hold values from -6 to 6
Outputs:
- out: bfloat16 [4, 1024, 2048], P('dp', 'seq')
- grad_inputs: float32 [4, 1024, 2048], P('dp', 'seq')
- grad_w_query: float32 [2048, 2048], P(('dp', 'seq'))
- grad_w_key: float32 [2048, 2048], P(('dp', 'seq'))
- grad_w_value: float32 [2048, 2048], P(('dp', 'seq'))
- grad_w_out: float32 [2048, 2048], P(('dp', 'seq'))
- grad_gain_query: float32 [2048], P(('dp', 'seq'))
- grad_gain_key: float32 [2048], P(('dp', 'seq'))
- grad_gain_attn: float32 [2048], P(('dp', 'seq'))
- grad_w_gate: float32 [2048, 8192], P(('dp', 'seq'))
- grad_w_up: float32 [2048, 8192], P(('dp', 'seq'))
- grad_w_down: float32 [8192, 2048], P(None, ('dp', 'seq'))
- grad_gain_ffn: float32 [2048], P(('dp', 'seq'))
The draws below stay inside these ranges and needn't reach their ends.
Inputs may be any that keep to these rules, and one draw needn't show every extreme that they name: `doc_lengths`: each row's lengths sum to 1024, and one of them is 960.
All inputs are finite; a program needn't handle non-finite values.
Results may differ from the reference program's by a relative error of at most 0.019.
Values may be sent and summed in bfloat16 or wider, within the bound.
No kernel may reach another device: no remote copies, remote signals or barrier semaphores. Data moves between devices by JAX's collectives and lax.ppermute only.
A program may use at most 832 MiB of HBM per device.

```python
import math
import jax
import jax.numpy as jnp
import numpy as np
from jax import lax

D = 2048
HEADS = 16
HEAD_DIM = 128
FF = 8192
TOK_DEV = 128
DOCS = 8
LENGTH = 1024
ROWS_ALL = 4


def steps_of(stream_key, dims, pieces, least, top_value):
    loudness = 1.0
    for axis_at, parts in pieces:
        steps = jax.random.uniform(jax.random.fold_in(jax.random.fold_in(stream_key, 6), axis_at), (parts,), jnp.float32, least / len(pieces), top_value / len(pieces))
        loudness = loudness * jnp.repeat(jnp.exp(steps), dims[axis_at] // parts).reshape((-1,) + (1,) * (len(dims) - 1 - axis_at))
    return loudness


def split_up(number_of, total, reach, skew):
    portions = [(1 << 20) // math.isqrt(grade ** skew) + 1 for grade in range(2, number_of + 1)]
    spare, given = total - reach - (number_of - 1), [1] * (number_of - 1)
    while spare > 0:
        free = [i for i in range(number_of - 1) if given[i] < reach]
        pool, remaining = sum([portions[i] for i in free]), spare
        for i in free:
            more = min(reach - given[i], max(1, remaining * portions[i] // pool), spare)
            given[i] = given[i] + more
            spare = spare - more
    return np.array([reach] + given)


def ragged(rng, number_of, total, limit, skew):
    if number_of == 2:
        one = jax.random.randint(rng, (), max(1, total - limit), min(limit, total - 1) + 1)
        return jnp.stack([one, total - one])
    tallies = jnp.asarray(split_up(number_of, total, limit, skew), jnp.int32)
    pairs = (number_of - 1) // 2
    source_of, receiver = tallies[1:1 + 2 * pairs:2], tallies[2:2 + 2 * pairs:2]
    slack = jnp.minimum(source_of - 1, limit - receiver)
    passed = jax.random.randint(jax.random.fold_in(rng, 1), (pairs,), 0, 1 << 20) % (slack + 1)
    tallies = tallies.at[1:1 + 2 * pairs:2].set(source_of - passed).at[2:2 + 2 * pairs:2].set(receiver + passed)
    return tallies[jax.random.permutation(jax.random.fold_in(rng, 2), number_of)]


def bell_draw(stream_key, shape, scale, limit, cuts=(), dtype=jnp.bfloat16):
    values = jax.random.normal(stream_key, shape, jnp.float32) * scale
    if len(cuts) > 0:
        values = steps_of(stream_key, shape, cuts, -0.22, 0.18) * values
    return jnp.clip(values, min=-limit, max=limit).astype(dtype)


def setup_inputs(seed: int = 0) -> dict:
    keys = jax.random.split(jax.random.key(seed), 15)
    inputs = bell_draw(keys[0], (ROWS_ALL, LENGTH, D), 1.0, 6.0, ((0, 4), (1, 8)))
    doc_lengths = jax.vmap(lambda own: ragged(own, DOCS, LENGTH, LENGTH - TOK_DEV // 2, 2))(jax.random.split(keys[1], ROWS_ALL)).reshape((ROWS_ALL, DOCS)).astype(jnp.int32)
    w_query = bell_draw(keys[2], (D, D), D ** -0.5, 0.125, ((0, 32),))
    w_key = bell_draw(keys[3], (D, D), D ** -0.5, 0.125, ((0, 32),))
    w_value = bell_draw(keys[4], (D, D), D ** -0.5, 0.125, ((0, 32),))
    w_out = bell_draw(keys[5], (D, D), D ** -0.5, 0.125, ((0, 32),))
    gain_query = jnp.clip(1.0 + 0.15 * jax.random.normal(keys[6], (D,), jnp.float32), 0.25, 1.75).astype(jnp.bfloat16)
    gain_key = jnp.clip(1.0 + 0.15 * jax.random.normal(keys[7], (D,), jnp.float32), 0.25, 1.75).astype(jnp.bfloat16)
    gain_attn = jnp.clip(1.0 + 0.15 * jax.random.normal(keys[8], (D,), jnp.float32), 0.25, 1.75).astype(jnp.bfloat16)
    w_gate = bell_draw(keys[9], (D, FF), D ** -0.5, 0.125, ((0, 32),))
    w_up = bell_draw(keys[10], (D, FF), D ** -0.5, 0.125, ((0, 32),))
    w_down = bell_draw(keys[11], (FF, D), FF ** -0.5, 0.0625, ((1, 32),))
    gain_ffn = jnp.clip(1.0 + 0.15 * jax.random.normal(keys[12], (D,), jnp.float32), 0.25, 1.75).astype(jnp.bfloat16)
    cotangent = bell_draw(keys[13], (ROWS_ALL, LENGTH, D), 1.0, 6.0, ((0, 4), (1, 8)))
    return dict(inputs=inputs, doc_lengths=doc_lengths, w_query=w_query, w_key=w_key, w_value=w_value, w_out=w_out, gain_query=gain_query, gain_key=gain_key, gain_attn=gain_attn, w_gate=w_gate, w_up=w_up, w_down=w_down, gain_ffn=gain_ffn, cotangent=cotangent)


NORM_EPS = 1e-06
ROPE_BASE = 500000.0
MASK_FILL = -1e+30
FULL_PRECISION = lax.Precision.HIGHEST

@jax.custom_vjp
def low(v):
    return lax.optimization_barrier(v.astype(jnp.bfloat16)).astype(jnp.float32)

@jax.custom_vjp
def low_back(v):
    return v

def low_keep(v):
    return (low(v), None)

def low_pass(kept, grad):
    return (grad,)

def back_keep(v):
    return (v, None)

def back_low(kept, grad):
    return (low(grad),)
low.defvjp(low_keep, low_pass)
low_back.defvjp(back_keep, back_low)

def matmul(left_mat, right_mat):
    return jnp.dot(left_mat, right_mat, precision=FULL_PRECISION, preferred_element_type=jnp.float32)

def rms_norm(array_in, gain_vec):
    return array_in * lax.rsqrt(lax.optimization_barrier(jnp.mean(array_in * array_in, axis=-1, keepdims=True)) + NORM_EPS) * gain_vec

def rotate(array_in, cosine, sine_t):
    half_dim = array_in.shape[-1] // 2
    first_half = array_in[..., :half_dim]
    second_half = array_in[..., half_dim:]
    return jnp.concatenate([first_half * cosine - second_half * sine_t, second_half * cosine + first_half * sine_t], axis=-1)

def tables():
    half_dim = HEAD_DIM // 2
    position = jnp.arange(LENGTH).astype(jnp.float32)
    inverse = jnp.exp(-(jnp.arange(half_dim).astype(jnp.float32) / half_dim) * math.log(ROPE_BASE))
    angles = position[:, None] * inverse[None, :]
    return (jnp.cos(angles)[:, None, :], jnp.sin(angles)[:, None, :])

def row_forward(row_input, lengths, weights):
    w_query, w_key, w_value, w_out, gain_query, gain_key, gain_attn, w_gate, w_up, w_down, gain_ffn = weights
    cosine, sine_t = tables()
    score_scale = 1.0 / math.sqrt(HEAD_DIM)
    q_lin = low_back(matmul(row_input, w_query))
    k_lin = low_back(matmul(row_input, w_key))
    v_lin = low_back(matmul(row_input, w_value))
    queries = low(rotate(rms_norm(q_lin, gain_query).reshape(LENGTH, HEADS, HEAD_DIM), cosine, sine_t))
    key_rows = low(rotate(rms_norm(k_lin, gain_key).reshape(LENGTH, HEADS, HEAD_DIM), cosine, sine_t))
    values = low(v_lin).reshape(LENGTH, HEADS, HEAD_DIM)
    position = jnp.arange(LENGTH).astype(jnp.int32)
    doc_ends = jnp.cumsum(lengths).astype(jnp.int32)
    doc_ids = lax.optimization_barrier(jnp.sum((position[:, None] >= doc_ends[None, :]).astype(jnp.int32), axis=1))
    block_rows = min(512, LENGTH)
    block_count = LENGTH // block_rows

    def attend(block_item):
        q_block, q_pos, q_doc = block_item
        scores = jnp.einsum('qhd,khd->hqk', q_block, key_rows, precision=FULL_PRECISION) * score_scale
        scores = low_back(scores)
        allowed = (position[None, :] <= q_pos[:, None]) & (doc_ids[None, :] == q_doc[:, None])
        scores = jnp.where(allowed[None], scores, MASK_FILL)
        row_max = lax.optimization_barrier(jnp.max(scores, axis=-1, keepdims=True))
        row_total = row_max + jnp.log(lax.optimization_barrier(jnp.sum(jnp.exp(scores - row_max), axis=-1, keepdims=True)))
        attn_probs = low(jnp.exp(scores - row_total))
        return jnp.einsum('hqk,khd->qhd', attn_probs, values, precision=FULL_PRECISION)
    attn_mixed = lax.map(jax.checkpoint(attend), (queries.reshape(block_count, block_rows, HEADS, HEAD_DIM), position.reshape(block_count, block_rows), doc_ids.reshape(block_count, block_rows)))
    attended = low_back(low(attn_mixed.reshape(LENGTH, HEADS * HEAD_DIM)))
    branch = low_back(matmul(attended, w_out))
    hidden = row_input + rms_norm(branch, gain_attn)
    hidden_low = low(hidden)
    gate_act = low_back(matmul(hidden_low, w_gate))
    upward = low_back(matmul(hidden_low, w_up))
    active = low(jax.nn.silu(gate_act) * upward)
    result = low_back(matmul(active, w_down))
    return hidden + rms_norm(result, gain_ffn)

def reference(inputs, doc_lengths, w_query, w_key, w_value, w_out, gain_query, gain_key, gain_attn, w_gate, w_up, w_down, gain_ffn, cotangent):
    float_weights = tuple((weight.astype(jnp.float32) for weight in (w_query, w_key, w_value, w_out, gain_query, gain_key, gain_attn, w_gate, w_up, w_down, gain_ffn)))

    def layer_fn(layer_inputs, *weights):

        def one_row(row_item):
            return row_forward(row_item[0], row_item[1], weights)
        return lax.map(one_row, (layer_inputs, doc_lengths))
    output, pullback = jax.vjp(layer_fn, inputs.astype(jnp.float32), *float_weights)
    all_grads = pullback(cotangent.astype(jnp.float32))
    return (output.astype(jnp.bfloat16), all_grads[0], all_grads[1], all_grads[2], all_grads[3], all_grads[4], all_grads[5], all_grads[6], all_grads[7], all_grads[8], all_grads[9], all_grads[10], all_grads[11])
```

```python
import math

import jax
import jax.numpy as jnp
from jax import lax
from jax.sharding import Mesh
from jax.sharding import PartitionSpec as P

HEADS = 16
HEAD_DIM = 128


NORM_EPS = 1e-06
ROPE_BASE = 500000.0
MASK_FILL = -1e30

SEQ = ("z", "y")
DP = ("x", "core")
FEED = ("core", "z")
REST = ("x", "y")
ALL = ("x", "core", "z", "y")
SWAP = [(0, 1), (1, 0)]
F32 = jnp.float32
BF16 = jnp.bfloat16


def matmul(left_mat, right_mat):
    return jnp.dot(left_mat, right_mat, preferred_element_type=F32)


def dot_right_t(left_mat, right_mat):
    return lax.dot_general(
        left_mat, right_mat, (((1,), (1,)), ((), ())), preferred_element_type=F32
    )


def dot_left_t(left_mat, right_mat):
    return lax.dot_general(
        left_mat, right_mat, (((0,), (0,)), ((), ())), preferred_element_type=F32
    )


def norm_apply(array_in, gain_vec):
    factor = lax.rsqrt(jnp.mean(array_in * array_in, axis=-1, keepdims=True) + NORM_EPS)
    return (array_in * factor * gain_vec, factor)


def norm_back(array_in, factor, gain_vec, grad_in):
    gain_term = jnp.sum(grad_in * array_in * factor, axis=0)
    scaled = grad_in * gain_vec
    grad_out = factor * scaled - array_in * (factor * factor * factor) * jnp.mean(
        scaled * array_in, axis=-1, keepdims=True
    )
    return (grad_out, gain_term)


def rotation(first_pos, tok_count):
    half_dim = HEAD_DIM // 2
    position = (first_pos + jnp.arange(tok_count)).astype(F32)
    inverse = jnp.exp(-(jnp.arange(half_dim).astype(F32) / half_dim) * math.log(ROPE_BASE))
    angles = position[:, None] * inverse[None, :]
    return (jnp.cos(angles)[:, None, :], jnp.sin(angles)[:, None, :])


def rotate(array_in, cosine, sine_t, turn_sign):
    half_dim = array_in.shape[-1] // 2
    first_half = array_in[..., :half_dim]
    second_half = array_in[..., half_dim:]
    return jnp.concatenate(
        [
            first_half * cosine - turn_sign * second_half * sine_t,
            second_half * cosine + turn_sign * first_half * sine_t,
        ],
        axis=-1,
    )


def exchange(array_in, axes):
    return lax.all_to_all(array_in, axes, split_axis=0, concat_axis=0, tiled=True)


def spread(array_in, axes):
    count = lax.axis_size(axes)
    return exchange(jnp.broadcast_to(array_in[None], (count,) + array_in.shape), axes)


def ring_pairs(count):
    order = [0] + list(range(1, count, 2)) + [v for v in range(count - 1, 0, -1) if v % 2 == 0]
    return [(order[i], order[(i + 1) % count]) for i in range(count)]


def core_swap(array_in):
    return lax.ppermute(array_in, "core", SWAP)


def body(
    inputs,
    doc_lengths,
    w_query,
    w_key,
    w_value,
    w_out,
    gain_query,
    gain_key,
    gain_attn,
    w_gate,
    w_up,
    w_down,
    gain_ffn,
    cotangent,
):
    _, tok_count, model_width = inputs.shape
    n_x, n_core, n_z, n_y = (lax.axis_size(a) for a in ALL)
    n_seq, n_dp, n_all = n_z * n_y, n_x * n_core, n_x * n_core * n_z * n_y
    seq_at = lax.axis_index(SEQ)
    length = tok_count * n_seq
    score_scale = 1.0 / math.sqrt(HEAD_DIM)
    own_rows = w_query.shape[0]
    own_width = model_width // n_seq
    own_heads = own_width // HEAD_DIM
    feed_width = w_gate.shape[1]
    n_feed = n_core * n_z
    own_feed = feed_width // n_feed
    ring = ring_pairs(n_z)
    tokens = inputs[0]

    gains = spread(jnp.stack([gain_query, gain_key, gain_attn, gain_ffn]), ALL)
    gains = gains.transpose(1, 0, 2).reshape(4, model_width).astype(F32)
    my_gq = lax.dynamic_slice_in_dim(gains[0], seq_at * own_width, own_width)
    my_gk = lax.dynamic_slice_in_dim(gains[1], seq_at * own_width, own_width)
    gain_a, gain_f = gains[2], gains[3]

    w_heads = jnp.stack([w_query, w_key, w_value])
    w_heads = w_heads.reshape(3, own_rows, n_seq, own_width).transpose(2, 1, 0, 3)
    w_heads = exchange(w_heads.reshape(n_seq, own_rows, 3 * own_width), SEQ)
    w_heads = lax.all_gather(w_heads, DP, axis=0, tiled=True).reshape(model_width, 3 * own_width)
    x_row = lax.all_gather(tokens, SEQ, axis=0, tiled=True)
    full_o = lax.all_gather(w_out, ALL, axis=0, tiled=True)

    w_feed = jnp.stack([w_gate, w_up, w_down.T])
    w_feed = w_feed.reshape(3, own_rows, n_feed, own_feed).transpose(2, 0, 1, 3)
    w_feed = exchange(w_feed, FEED)
    w_feed = lax.all_gather(w_feed, REST, axis=0, tiled=False)
    w_feed = w_feed.reshape(n_x, n_y, n_core, n_z, 3, own_rows, own_feed)
    w_feed = w_feed.transpose(4, 0, 2, 3, 1, 5, 6).reshape(3, model_width, own_feed)
    w_g, w_u, w_d = w_feed[0], w_feed[1], w_feed[2]

    qkv = matmul(x_row, w_heads)
    q_lin, k_lin, v_lin = (
        qkv[:, :own_width],
        qkv[:, own_width : 2 * own_width],
        qkv[:, 2 * own_width :],
    )
    squares = jnp.stack([jnp.sum(q_lin * q_lin, axis=1), jnp.sum(k_lin * k_lin, axis=1)])
    squares = jnp.sum(spread(squares, SEQ), axis=0) / model_width
    factors = lax.rsqrt(squares + NORM_EPS)
    q_factor, k_factor = factors[0][:, None], factors[1][:, None]
    cosine, sine_t = rotation(0, length)

    def to_heads(array_in, turn_sign):
        heads = rotate(array_in.reshape(length, own_heads, HEAD_DIM), cosine, sine_t, turn_sign)
        return heads.astype(BF16).transpose(1, 0, 2)

    def from_heads(array_in):
        return array_in.transpose(1, 0, 2).reshape(length, own_width)

    queries = to_heads(q_lin * q_factor * my_gq, 1.0)
    keys = to_heads(k_lin * k_factor * my_gk, 1.0)
    values = v_lin.astype(BF16).reshape(length, own_heads, HEAD_DIM).transpose(1, 0, 2)

    position = jnp.arange(length)
    doc_ends = jnp.cumsum(doc_lengths[0])
    doc_ids = jnp.sum((position[:, None] >= doc_ends[None, :]).astype(jnp.int32), axis=1)
    allowed = (position[None, :] <= position[:, None]) & (doc_ids[None, :] == doc_ids[:, None])
    scores = jnp.einsum("htd,hkd->htk", queries, keys, preferred_element_type=F32) * score_scale
    scores = jnp.where(allowed[None], scores, MASK_FILL)
    row_max = jnp.max(scores, axis=-1, keepdims=True)
    totals = row_max + jnp.log(jnp.sum(jnp.exp(scores - row_max), axis=-1, keepdims=True))
    prob_full = jnp.exp(scores - totals)
    probs = prob_full.astype(BF16)
    mixed = jnp.einsum("htk,hkd->htd", probs, values, preferred_element_type=F32)
    attended = from_heads(mixed).astype(BF16)

    att_tok = exchange(attended.reshape(n_seq, tok_count, own_width), SEQ)
    att_tok = att_tok.transpose(1, 0, 2).reshape(tok_count, model_width)
    branch = matmul(att_tok, full_o)
    branch_norm, branch_factor = norm_apply(branch, gain_a)
    hidden = tokens.astype(F32) + branch_norm
    hidden_low = hidden.astype(BF16)

    def ring_gather(own):
        held = [own]
        for _ in range(n_z - 1):
            held.append(lax.ppermute(held[-1], "z", ring))
        return [jnp.concatenate([part, core_swap(part)], axis=0) for part in held]

    def ring_sum(parts):
        total = None
        for step in list(range(1, n_z)) + [0]:
            part = parts[step]
            mine = part[:tok_count] + core_swap(part[tok_count:].astype(BF16)).astype(F32)
            if total is not None:
                mine = mine + lax.ppermute(total.astype(BF16), "z", ring).astype(F32)
            total = mine
        return total

    hid = ring_gather(hidden_low)
    gate = [matmul(part, w_g) for part in hid]
    upward = [matmul(part, w_u) for part in hid]
    sig = [jax.nn.sigmoid(part) for part in gate]
    active = [(g * s * u).astype(BF16) for g, s, u in zip(gate, sig, upward)]
    result = ring_sum([dot_right_t(part, w_d) for part in active])
    result_norm, result_factor = norm_apply(result, gain_f)
    output = (hidden + result_norm).astype(BF16)

    grad_top = cotangent[0].astype(F32)
    grad_result, ffn_gain_term = norm_back(result, result_factor, gain_f, grad_top)
    g_res = ring_gather(grad_result.astype(BF16))
    g_act = [matmul(part, w_d) for part in g_res]
    g_gate = [
        (a * u * s * (1.0 + g * (1.0 - s))).astype(BF16)
        for a, u, s, g in zip(g_act, upward, sig, gate)
    ]
    g_up = [(a * g * s).astype(BF16) for a, g, s in zip(g_act, gate, sig)]
    grad_hidden = grad_top + ring_sum(
        [dot_right_t(a, w_g) + dot_right_t(b, w_u) for a, b in zip(g_gate, g_up)]
    )

    def feed_grad(left, right):
        term = dot_left_t(jnp.concatenate(left, axis=0), jnp.concatenate(right, axis=0))
        term = term.astype(BF16).reshape(n_x, n_core, n_z, n_y, own_rows, own_feed)
        term = term.transpose(0, 3, 1, 2, 4, 5).reshape(n_x * n_y, n_feed, own_rows, own_feed)
        term = jnp.sum(exchange(term, REST).astype(F32), axis=0)
        term = exchange(term.astype(BF16), FEED)
        return term.transpose(1, 0, 2).reshape(own_rows, feed_width).astype(F32)

    grad_w_down = feed_grad(g_res, active).T
    grad_w_gate = feed_grad(hid, g_gate)
    grad_w_up = feed_grad(hid, g_up)

    grad_branch, attn_gain_term = norm_back(branch, branch_factor, gain_a, grad_hidden)
    grad_branch = grad_branch.astype(BF16)
    grad_attended = dot_right_t(grad_branch, full_o).astype(BF16)
    g_att = grad_attended.reshape(tok_count, n_seq, own_width).transpose(1, 0, 2)
    g_att = exchange(g_att, SEQ).reshape(length, own_heads, HEAD_DIM).transpose(1, 0, 2)

    branch_row = lax.all_gather(grad_branch, SEQ, axis=0, tiled=True)
    grad_w_out = dot_left_t(attended, branch_row).astype(BF16)
    grad_w_out = grad_w_out.reshape(n_dp, own_rows, model_width)
    grad_w_out = jnp.sum(exchange(grad_w_out, DP).astype(F32), axis=0)
    home = [(d * n_seq + s, s * n_dp + d) for d in range(n_dp) for s in range(n_seq)]
    grad_w_out = lax.ppermute(grad_w_out.astype(BF16), ALL, home).astype(F32)

    grad_probs = jnp.einsum("htd,hkd->htk", g_att, values, preferred_element_type=F32)
    offsets = jnp.sum(prob_full * grad_probs, axis=-1, keepdims=True)
    grad_scores = (prob_full * (grad_probs - offsets)).astype(BF16)
    grad_q = (
        jnp.einsum("htk,hkd->htd", grad_scores, keys, preferred_element_type=F32) * score_scale
    )
    grad_k = (
        jnp.einsum("htk,htd->hkd", grad_scores, queries, preferred_element_type=F32) * score_scale
    )
    grad_v = jnp.einsum("htk,htd->hkd", probs, g_att, preferred_element_type=F32)

    def turn_back(array_in):
        heads = rotate(array_in.transpose(1, 0, 2), cosine, sine_t, -1.0)
        return heads.reshape(length, own_width)

    grad_q, grad_k = turn_back(grad_q), turn_back(grad_k)
    dots = jnp.stack(
        [jnp.sum(grad_q * my_gq * q_lin, axis=1), jnp.sum(grad_k * my_gk * k_lin, axis=1)]
    )
    dots = jnp.sum(spread(dots, SEQ), axis=0) / model_width

    def lin_back(grad_in, lin, factor, gain_vec, mean_dot):
        gain_term = jnp.sum(grad_in * lin * factor, axis=0)
        grad_out = factor * (grad_in * gain_vec) - lin * (factor * factor * factor) * mean_dot
        return grad_out.astype(BF16), gain_term

    grad_q_lin, query_gain_term = lin_back(grad_q, q_lin, q_factor, my_gq, dots[0][:, None])
    grad_k_lin, key_gain_term = lin_back(grad_k, k_lin, k_factor, my_gk, dots[1][:, None])
    grad_lin = jnp.concatenate([grad_q_lin, grad_k_lin, from_heads(grad_v).astype(BF16)], axis=1)

    grad_row = dot_right_t(grad_lin, w_heads).astype(BF16)
    grad_input = grad_hidden + lax.psum_scatter(
        grad_row, SEQ, scatter_dimension=0, tiled=True
    ).astype(F32)

    grad_heads = dot_left_t(x_row, grad_lin).astype(BF16)
    grad_heads = grad_heads.reshape(n_dp, n_seq * own_rows, 3 * own_width)
    grad_heads = jnp.sum(exchange(grad_heads, DP).astype(F32), axis=0).astype(BF16)
    grad_heads = exchange(grad_heads.reshape(n_seq, own_rows, 3 * own_width), SEQ)
    grad_heads = grad_heads.reshape(n_seq, own_rows, 3, own_width).transpose(2, 1, 0, 3)
    grad_heads = grad_heads.reshape(3, own_rows, model_width).astype(F32)

    def place(term):
        return lax.dynamic_update_slice(
            jnp.zeros((model_width,), F32), term, (seq_at * own_width,)
        )

    gain_terms = jnp.stack(
        [place(query_gain_term), place(key_gain_term), attn_gain_term, ffn_gain_term]
    )
    gain_terms = gain_terms.reshape(4, n_all, own_rows).transpose(1, 0, 2)
    gain_grads = jnp.sum(exchange(gain_terms, ALL), axis=0)

    return (
        output[None],
        grad_input[None],
        grad_heads[0],
        grad_heads[1],
        grad_heads[2],
        grad_w_out,
        gain_grads[0],
        gain_grads[1],
        gain_grads[2],
        grad_w_gate,
        grad_w_up,
        grad_w_down,
        gain_grads[3],
    )


def plain_rotation(first_pos, tok_count):
    half_dim = HEAD_DIM // 2
    position = (first_pos + jnp.arange(tok_count)).astype(jnp.float32)
    inverse = jnp.exp(-(jnp.arange(half_dim).astype(jnp.float32) / half_dim) * math.log(ROPE_BASE))
    angles = position[:, None] * inverse[None, :]
    return (jnp.cos(angles)[None, :, None, :], jnp.sin(angles)[None, :, None, :])


def plain_body(
    inputs,
    doc_lengths,
    w_query,
    w_key,
    w_value,
    w_out,
    gain_query,
    gain_key,
    gain_attn,
    w_gate,
    w_up,
    w_down,
    gain_ffn,
    cotangent,
):
    row_count, tok_count, model_width = inputs.shape
    length = tok_count * lax.axis_size("seq")
    first_pos = lax.axis_index("seq") * tok_count
    score_scale = 1.0 / math.sqrt(HEAD_DIM)
    tokens = inputs.reshape(row_count * tok_count, model_width)

    def heads_first(array_in):
        return array_in.reshape(row_count, tok_count, HEADS, HEAD_DIM).transpose(2, 0, 1, 3)

    def heads_last(array_in):
        return array_in.transpose(1, 2, 0, 3).reshape(row_count * tok_count, HEADS * HEAD_DIM)

    full_q, full_k, full_v, full_o, full_gq, full_gk, full_ga = (
        lax.all_gather(w_query, ("dp", "seq"), axis=0, tiled=True),
        lax.all_gather(w_key, ("dp", "seq"), axis=0, tiled=True),
        lax.all_gather(w_value, ("dp", "seq"), axis=0, tiled=True),
        lax.all_gather(w_out, ("dp", "seq"), axis=0, tiled=True),
        lax.all_gather(gain_query, ("dp", "seq"), axis=0, tiled=True),
        lax.all_gather(gain_key, ("dp", "seq"), axis=0, tiled=True),
        lax.all_gather(gain_attn, ("dp", "seq"), axis=0, tiled=True),
    )
    cosine, sine_t = plain_rotation(first_pos, tok_count)
    q_lin = matmul(tokens, full_q)
    k_lin = matmul(tokens, full_k)
    v_lin = matmul(tokens, full_v)
    q_norm, q_factor = norm_apply(q_lin, full_gq.astype(jnp.float32))
    k_norm, k_factor = norm_apply(k_lin, full_gk.astype(jnp.float32))
    queries = (
        rotate(q_norm.reshape(row_count, tok_count, HEADS, HEAD_DIM), cosine, sine_t, 1.0)
        .astype(jnp.bfloat16)
        .transpose(2, 0, 1, 3)
    )
    keys_mine = (
        rotate(k_norm.reshape(row_count, tok_count, HEADS, HEAD_DIM), cosine, sine_t, 1.0)
        .astype(jnp.bfloat16)
        .transpose(2, 0, 1, 3)
    )
    values_mine = heads_first(v_lin.astype(jnp.bfloat16))
    keys_all, values_all = (
        lax.all_gather(keys_mine, "seq", axis=2, tiled=True),
        lax.all_gather(values_mine, "seq", axis=2, tiled=True),
    )
    doc_ends = jnp.cumsum(doc_lengths, axis=1)
    position = jnp.arange(length)
    doc_ids = jnp.sum((position[None, :, None] >= doc_ends[:, None, :]).astype(jnp.int32), axis=2)
    my_pos = first_pos + jnp.arange(tok_count)
    docs_mine = lax.dynamic_slice_in_dim(doc_ids, first_pos, tok_count, 1)
    allowed = (position[None, None, :] <= my_pos[None, :, None]) & (
        doc_ids[:, None, :] == docs_mine[:, :, None]
    )

    def scores_of(q_head, k_head):
        raw_scores = (
            jnp.einsum("rtd,rkd->rtk", q_head, k_head, preferred_element_type=jnp.float32)
            * score_scale
        )
        return jnp.where(allowed, raw_scores, MASK_FILL)

    def attend(head_item):
        q_head, k_head, v_head = head_item
        scores = scores_of(q_head, k_head)
        row_max = jnp.max(scores, axis=-1, keepdims=True)
        row_total = row_max + jnp.log(jnp.sum(jnp.exp(scores - row_max), axis=-1, keepdims=True))
        attn_probs = jnp.exp(scores - row_total).astype(jnp.bfloat16)
        head_out = jnp.einsum(
            "rtk,rkd->rtd", attn_probs, v_head, preferred_element_type=jnp.float32
        )
        return (head_out, row_total[..., 0])

    attn_mixed, totals = lax.map(attend, (queries, keys_all, values_all))
    attended = heads_last(attn_mixed.astype(jnp.bfloat16))
    branch = matmul(attended, full_o)
    branch_norm, branch_factor = norm_apply(branch, full_ga.astype(jnp.float32))
    hidden = tokens.astype(jnp.float32) + branch_norm
    hidden_low = hidden.astype(jnp.bfloat16)
    gate_full, up_full, down_full, ffn_gain_full = (
        lax.all_gather(w_gate, ("dp", "seq"), axis=0, tiled=True),
        lax.all_gather(w_up, ("dp", "seq"), axis=0, tiled=True),
        lax.all_gather(w_down, ("dp", "seq"), axis=1, tiled=True),
        lax.all_gather(gain_ffn, ("dp", "seq"), axis=0, tiled=True),
    )
    gate_act = matmul(hidden_low, gate_full)
    upward = matmul(hidden_low, up_full)
    gate_sig = jax.nn.sigmoid(gate_act)
    active = (gate_act * gate_sig * upward).astype(jnp.bfloat16)
    result = matmul(active, down_full)
    result_norm, result_factor = norm_apply(result, ffn_gain_full.astype(jnp.float32))
    output = (hidden + result_norm).astype(jnp.bfloat16).reshape(row_count, tok_count, model_width)
    grad_top = cotangent.reshape(row_count * tok_count, model_width).astype(jnp.float32)
    grad_result, ffn_gain_term = norm_back(
        result, result_factor, ffn_gain_full.astype(jnp.float32), grad_top
    )
    grad_result = grad_result.astype(jnp.bfloat16)
    grad_active = dot_right_t(grad_result, down_full)
    grad_gate = (grad_active * upward * gate_sig * (1.0 + gate_act * (1.0 - gate_sig))).astype(
        jnp.bfloat16
    )
    grad_up = (grad_active * gate_act * gate_sig).astype(jnp.bfloat16)
    grad_hidden = grad_top + dot_right_t(grad_gate, gate_full) + dot_right_t(grad_up, up_full)
    feedforward_grads = lax.psum_scatter(
        jnp.concatenate(
            [
                dot_left_t(hidden_low, grad_gate),
                dot_left_t(hidden_low, grad_up),
                dot_left_t(grad_result, active),
            ],
            axis=1,
        ),
        ("dp", "seq"),
        scatter_dimension=0,
        tiled=True,
    )
    grad_branch, attn_gain_term = norm_back(
        branch, branch_factor, full_ga.astype(jnp.float32), grad_hidden
    )
    grad_branch = grad_branch.astype(jnp.bfloat16)
    back_q, back_k, back_v, back_o, back_gq, back_gk = (
        lax.all_gather(w_query, ("dp", "seq"), axis=0, tiled=True),
        lax.all_gather(w_key, ("dp", "seq"), axis=0, tiled=True),
        lax.all_gather(w_value, ("dp", "seq"), axis=0, tiled=True),
        lax.all_gather(w_out, ("dp", "seq"), axis=0, tiled=True),
        lax.all_gather(gain_query, ("dp", "seq"), axis=0, tiled=True),
        lax.all_gather(gain_key, ("dp", "seq"), axis=0, tiled=True),
    )
    grad_attended = dot_right_t(grad_branch, back_o).astype(jnp.bfloat16)
    grad_w_out_term = dot_left_t(attended, grad_branch)
    grad_mixed = heads_first(grad_attended)

    def head_back(head_item):
        q_head, k_head, v_head, g_head, t_head = head_item
        prob_full = jnp.exp(scores_of(q_head, k_head) - t_head[..., None])
        grad_probs = jnp.einsum("rtd,rkd->rtk", g_head, v_head, preferred_element_type=jnp.float32)
        offsets = jnp.sum(prob_full * grad_probs, axis=-1, keepdims=True)
        grad_scores = (prob_full * (grad_probs - offsets)).astype(jnp.bfloat16)
        grad_q = (
            jnp.einsum("rtk,rkd->rtd", grad_scores, k_head, preferred_element_type=jnp.float32)
            * score_scale
        )
        grad_k = (
            jnp.einsum("rtk,rtd->rkd", grad_scores, q_head, preferred_element_type=jnp.float32)
            * score_scale
        )
        grad_v = jnp.einsum(
            "rtk,rtd->rkd",
            prob_full.astype(jnp.bfloat16),
            g_head,
            preferred_element_type=jnp.float32,
        )
        return (grad_q, grad_k, grad_v)

    grad_queries, key_terms, value_terms = lax.map(
        head_back, (queries, keys_all, values_all, grad_mixed, totals)
    )
    grad_keys, grad_values = (
        lax.psum_scatter(
            key_terms.astype(jnp.bfloat16), "seq", scatter_dimension=2, tiled=True
        ).astype(jnp.float32),
        lax.psum_scatter(
            value_terms.astype(jnp.bfloat16), "seq", scatter_dimension=2, tiled=True
        ).astype(jnp.float32),
    )
    grad_q_norm = rotate(grad_queries.transpose(1, 2, 0, 3), cosine, sine_t, -1.0).reshape(
        row_count * tok_count, model_width
    )
    grad_k_norm = rotate(grad_keys.transpose(1, 2, 0, 3), cosine, sine_t, -1.0).reshape(
        row_count * tok_count, model_width
    )
    grad_q_lin, query_gain_term = norm_back(
        q_lin, q_factor, back_gq.astype(jnp.float32), grad_q_norm
    )
    grad_k_lin, key_gain_term = norm_back(k_lin, k_factor, back_gk.astype(jnp.float32), grad_k_norm)
    grad_q_lin = grad_q_lin.astype(jnp.bfloat16)
    grad_k_lin = grad_k_lin.astype(jnp.bfloat16)
    grad_v_lin = heads_last(grad_values).astype(jnp.bfloat16)
    grad_input = (
        grad_hidden
        + dot_right_t(grad_q_lin, back_q)
        + dot_right_t(grad_k_lin, back_k)
        + dot_right_t(grad_v_lin, back_v)
    )
    attention_grads = (
        lax.psum_scatter(
            dot_left_t(tokens, grad_q_lin), ("dp", "seq"), scatter_dimension=0, tiled=True
        ),
        lax.psum_scatter(
            dot_left_t(tokens, grad_k_lin), ("dp", "seq"), scatter_dimension=0, tiled=True
        ),
        lax.psum_scatter(
            dot_left_t(tokens, grad_v_lin), ("dp", "seq"), scatter_dimension=0, tiled=True
        ),
        lax.psum_scatter(grad_w_out_term, ("dp", "seq"), scatter_dimension=0, tiled=True),
        lax.psum_scatter(query_gain_term, ("dp", "seq"), scatter_dimension=0, tiled=True),
        lax.psum_scatter(key_gain_term, ("dp", "seq"), scatter_dimension=0, tiled=True),
        lax.psum_scatter(attn_gain_term, ("dp", "seq"), scatter_dimension=0, tiled=True),
        lax.psum_scatter(ffn_gain_term, ("dp", "seq"), scatter_dimension=0, tiled=True),
    )
    feed_width = w_gate.shape[1]
    grad_w_gate = feedforward_grads[:, :feed_width]
    grad_w_up = feedforward_grads[:, feed_width : 2 * feed_width]
    grad_w_down = feedforward_grads[:, 2 * feed_width :].T
    return (
        output,
        grad_input.reshape(row_count, tok_count, model_width),
        attention_grads[0],
        attention_grads[1],
        attention_grads[2],
        attention_grads[3],
        attention_grads[4],
        attention_grads[5],
        attention_grads[6],
        grad_w_gate,
        grad_w_up,
        grad_w_down,
        attention_grads[7],
    )


def solution(mesh):
    n_dp, n_seq = mesh.shape["dp"], mesh.shape["seq"]
    if HEADS % n_seq == 0 and n_dp % 2 == 0 and n_seq % 2 == 0:
        grid = Mesh(mesh.devices.reshape(n_dp // 2, 2, n_seq // 2, 2), ALL)
        layer, dp, seq = body, DP, SEQ
    else:
        grid, layer, dp, seq = mesh, plain_body, ("dp",), ("seq",)
    rows = P(dp, seq, None)
    split = P(dp + seq, None)
    vector = P(dp + seq)
    down = P(None, dp + seq)
    return jax.shard_map(
        layer,
        mesh=grid,
        in_specs=(rows, P(dp, None))
        + (split,) * 4
        + (vector,) * 3
        + (split, split, down, vector, rows),
        out_specs=(rows, rows) + (split,) * 4 + (vector,) * 3 + (split, split, down, vector),
        check_vma=False,
    )
```

```python
import math

import jax
import jax.numpy as jnp
from jax import lax
from jax.experimental import pallas as pl
from jax.experimental.pallas import tpu as pltpu
from jax.sharding import Mesh
from jax.sharding import PartitionSpec as P

HEADS = 16
HEAD_DIM = 128


NORM_EPS = 1e-06
ROPE_BASE = 500000.0
MASK_FILL = -1e30

SEQ = ("z", "y")
DP = ("x", "core")
FEED = ("z", "core")
REST = ("x", "y")
ALL = ("x", "core", "z", "y")
SWAP = [(0, 1), (1, 0)]
F32 = jnp.float32
BF16 = jnp.bfloat16


def matmul(left_mat, right_mat):
    return jnp.dot(left_mat, right_mat, preferred_element_type=F32)


def dot_right_t(left_mat, right_mat):
    return lax.dot_general(
        left_mat, right_mat, (((1,), (1,)), ((), ())), preferred_element_type=F32
    )


def dot_left_t(left_mat, right_mat):
    return lax.dot_general(
        left_mat, right_mat, (((0,), (0,)), ((), ())), preferred_element_type=F32
    )


def norm_apply(array_in, gain_vec):
    factor = lax.rsqrt(jnp.mean(array_in * array_in, axis=-1, keepdims=True) + NORM_EPS)
    return (array_in * factor * gain_vec, factor)


def norm_back(array_in, factor, gain_vec, grad_in):
    gain_term = jnp.sum(grad_in * array_in * factor, axis=0)
    scaled = grad_in * gain_vec
    grad_out = factor * scaled - array_in * (factor * factor * factor) * jnp.mean(
        scaled * array_in, axis=-1, keepdims=True
    )
    return (grad_out, gain_term)


def turn_tables(tok_count):
    half_dim = HEAD_DIM // 2
    position = jnp.arange(tok_count).astype(F32)
    inverse = jnp.exp(-(jnp.arange(half_dim).astype(F32) / half_dim) * math.log(ROPE_BASE))
    angles = position[:, None] * inverse[None, :]
    cosine, sine_t = jnp.cos(angles), jnp.sin(angles)
    return (
        jnp.concatenate([cosine, cosine], axis=1),
        jnp.concatenate([-sine_t, sine_t], axis=1),
    )


def rotate(array_in, cosine, sine_t):
    return array_in * cosine + pltpu.roll(array_in, HEAD_DIM // 2, 1) * sine_t


def rotate_back(array_in, cosine, sine_t):
    return array_in * cosine - pltpu.roll(array_in, HEAD_DIM // 2, 1) * sine_t


def exchange(array_in, axes):
    return lax.all_to_all(array_in, axes, split_axis=0, concat_axis=0, tiled=True)


def spread(array_in, axes):
    count = lax.axis_size(axes)
    return exchange(jnp.broadcast_to(array_in[None], (count,) + array_in.shape), axes)


def tie(value, *earlier):
    return lax.optimization_barrier((value,) + earlier)[0]


def ring_order(count):
    return [0] + list(range(1, count, 2)) + [v for v in range(count - 1, 0, -1) if v % 2 == 0]


def core_swap(array_in):
    return lax.ppermute(array_in, "core", SWAP)


def pick(array_in, at, axis=0):
    return lax.dynamic_index_in_dim(array_in, at, axis, keepdims=False)


def visible(doc_col, doc_row, first, rows, width):
    at = first + lax.broadcasted_iota(jnp.int32, (rows, width), 0)
    of = lax.broadcasted_iota(jnp.int32, (rows, width), 1)
    return (of <= at) & (doc_col == doc_row)


def attend_kernel(
    step,
    q_lin,
    k_lin,
    v_lin,
    factors,
    gain_q,
    gain_k,
    cosine,
    sine_t,
    doc_col,
    doc_row,
    queries,
    keys,
    values,
    totals,
    attended,
):
    cos, sin = cosine[...], sine_t[...]
    queries[...] = rotate(q_lin[...] * factors[:, 0:1] * gain_q[...], cos, sin).astype(BF16)
    keys[...] = rotate(k_lin[...] * factors[:, 1:2] * gain_k[...], cos, sin).astype(BF16)
    values[...] = v_lin[...].astype(BF16)
    scale = 1.0 / math.sqrt(HEAD_DIM)
    for first in range(0, queries.shape[0], step):
        width = first + step
        mine = pl.ds(first, step)
        scores = dot_right_t(queries[mine, :], keys[0:width, :]) * scale
        seen = visible(doc_col[mine, :], doc_row[:, 0:width], first, step, width)
        scores = jnp.where(seen, scores, MASK_FILL)
        row_max = jnp.max(scores, axis=1, keepdims=True)
        row_sum = jnp.sum(jnp.exp(scores - row_max), axis=1, keepdims=True)
        total = row_max + jnp.log(row_sum)
        probs = jnp.exp(scores - total).astype(BF16)
        totals[0, mine, :] = total
        attended[mine, :] = matmul(probs, values[0:width, :]).astype(BF16)


def attend_back_kernel(
    step,
    queries,
    keys,
    values,
    totals,
    g_att,
    q_lin,
    k_lin,
    gain_q,
    gain_k,
    cosine,
    sine_t,
    doc_col,
    doc_row,
    grad_q,
    grad_k,
    grad_v,
    dot_q,
    dot_k,
    k_sum,
    v_sum,
):
    scale = 1.0 / math.sqrt(HEAD_DIM)
    k_sum[...] = jnp.zeros_like(k_sum)
    v_sum[...] = jnp.zeros_like(v_sum)
    for first in range(0, queries.shape[0], step):
        width = first + step
        mine, upto = pl.ds(first, step), pl.ds(0, width)
        scores = dot_right_t(queries[mine, :], keys[upto, :]) * scale
        seen = visible(doc_col[mine, :], doc_row[:, 0:width], first, step, width)
        scores = jnp.where(seen, scores, MASK_FILL)
        prob_full = jnp.exp(scores - totals[0, mine, :])
        grad_probs = dot_right_t(g_att[mine, :], values[upto, :])
        offsets = jnp.sum(prob_full * grad_probs, axis=1, keepdims=True)
        grad_scores = (prob_full * (grad_probs - offsets)).astype(BF16)
        back = matmul(grad_scores, keys[upto, :]) * scale
        back = rotate_back(back, cosine[mine, :], sine_t[mine, :])
        grad_q[mine, :] = back
        dot_q[0, mine, :] = jnp.sum(back * gain_q[...] * q_lin[mine, :], axis=1, keepdims=True)
        k_sum[upto, :] += dot_left_t(grad_scores, queries[mine, :])
        v_sum[upto, :] += dot_left_t(prob_full.astype(BF16), g_att[mine, :])
    back = rotate_back(k_sum[...] * scale, cosine[...], sine_t[...])
    grad_k[...] = back
    dot_k[0] = jnp.sum(back * gain_k[...] * k_lin[...], axis=1, keepdims=True)
    grad_v[...] = v_sum[...].astype(BF16)


def head_specs(length, heads):
    def part(offset):
        return pl.BlockSpec((length, HEAD_DIM), lambda h: (0, h + offset))

    def gain():
        return pl.BlockSpec((1, HEAD_DIM), lambda h: (0, h))

    def whole(shape):
        return pl.BlockSpec(shape, lambda h: (0, 0))

    each = pl.BlockSpec((1, length, 1), lambda h: (h, 0, 0))
    table = whole((length, HEAD_DIM))
    docs = [whole((length, 1)), whole((1, length))]
    return part, gain, whole, each, table, docs


def attend(qkv, factors, gain_q, gain_k, tables, docs, heads):
    length = qkv.shape[0]
    part, gain, whole, each, table, doc_specs = head_specs(length, heads)
    low = jax.ShapeDtypeStruct((length, heads * HEAD_DIM), BF16)
    step = min(256, length)
    pairs = heads * length * length * HEAD_DIM
    return pl.pallas_call(
        lambda *refs: attend_kernel(step, *refs),
        grid=(heads,),
        in_specs=[part(0), part(heads), part(2 * heads), whole((length, 2)), gain(), gain()]
        + [table, table]
        + doc_specs,
        out_specs=[part(0), part(0), part(0), each, part(0)],
        out_shape=[low, low, low, jax.ShapeDtypeStruct((heads, length, 1), F32), low],
        compiler_params=pltpu.CompilerParams(vmem_limit_bytes=24 * 1024 * 1024),
        cost_estimate=pl.CostEstimate(
            flops=3 * pairs, bytes_accessed=qkv.size * 6, transcendentals=heads * length * length
        ),
    )(qkv, qkv, qkv, factors, gain_q, gain_k, *tables, *docs)


def attend_back(saved, g_att, qkv, gain_q, gain_k, tables, docs, heads):
    queries, keys, values, totals = saved
    length = qkv.shape[0]
    part, gain, whole, each, table, doc_specs = head_specs(length, heads)
    flat = jax.ShapeDtypeStruct((length, heads * HEAD_DIM), F32)
    low = jax.ShapeDtypeStruct((length, heads * HEAD_DIM), BF16)
    line = jax.ShapeDtypeStruct((heads, length, 1), F32)
    step = min(256, length)
    pairs = heads * length * length * HEAD_DIM
    return pl.pallas_call(
        lambda *refs: attend_back_kernel(step, *refs),
        grid=(heads,),
        in_specs=[part(0), part(0), part(0), each, part(0), part(0), part(heads), gain(), gain()]
        + [table, table]
        + doc_specs,
        out_specs=[part(0), part(0), part(0), each, each],
        out_shape=[flat, flat, low, line, line],
        scratch_shapes=[pltpu.VMEM((length, HEAD_DIM), F32)] * 2,
        compiler_params=pltpu.CompilerParams(vmem_limit_bytes=24 * 1024 * 1024),
        cost_estimate=pl.CostEstimate(
            flops=7 * pairs, bytes_accessed=qkv.size * 8, transcendentals=heads * length * length
        ),
    )(queries, keys, values, totals, g_att, qkv, qkv, gain_q, gain_k, *tables, *docs)


def feed_kernel(part, other, w_g, w_u, w_d, *refs):
    hid, gate, upward, active, mine, away, total = refs[-7:]
    block, tokens = pl.program_id(0), part.shape[0]

    @pl.when(block == 0)
    def _():
        hid[:tokens, :] = part[...]
        hid[tokens:, :] = other[...]

    g = matmul(hid[...], w_g[...])
    u = matmul(hid[...], w_u[...])
    a = (g * (1.0 / (1.0 + jnp.exp(-g))) * u).astype(BF16)
    gate[...], upward[...], active[...] = g, u, a
    term = dot_right_t(a, w_d[...])

    @pl.when(block == 0)
    def _():
        total[...] = term

    @pl.when(block > 0)
    def _():
        total[...] += term

    @pl.when(block == pl.num_programs(0) - 1)
    def _():
        mine[...] = total[:tokens, :]
        away[...] = total[tokens:, :].astype(BF16)


def feed_back_kernel(part, other, w_g, w_u, w_d, gate, upward, *refs):
    g_res, g_gate, g_up, mine, away, total = refs[-6:]
    block, tokens = pl.program_id(0), part.shape[0]

    @pl.when(block == 0)
    def _():
        g_res[:tokens, :] = part[...]
        g_res[tokens:, :] = other[...]

    a = matmul(g_res[...], w_d[...])
    g, u = gate[...], upward[...]
    s = 1.0 / (1.0 + jnp.exp(-g))
    gg = (a * u * s * (1.0 + g * (1.0 - s))).astype(BF16)
    gu = (a * g * s).astype(BF16)
    g_gate[...], g_up[...] = gg, gu
    term = dot_right_t(gg, w_g[...]) + dot_right_t(gu, w_u[...])

    @pl.when(block == 0)
    def _():
        total[...] = term

    @pl.when(block > 0)
    def _():
        total[...] += term

    @pl.when(block == pl.num_programs(0) - 1)
    def _():
        mine[...] = total[:tokens, :]
        away[...] = total[tokens:, :].astype(BF16)


def feed_step(at, count, pair, weights, saved, held, kernel, dtypes):
    tokens, width = pair[0].shape
    feed = weights[0].shape[1]
    step = min(256, feed)
    rows = 2 * tokens
    block = pl.BlockSpec((rows, step), lambda f: (at, f))
    part = pl.BlockSpec((tokens, width), lambda f: (0, 0))
    full = pl.BlockSpec((rows, width), lambda f: (at, 0))
    n_in = 5 + len(saved)
    shapes = [jax.ShapeDtypeStruct((count * rows, width), BF16)]
    shapes += [jax.ShapeDtypeStruct((count * rows, feed), d) for d in dtypes]
    tail = [jax.ShapeDtypeStruct((tokens, width), d) for d in (F32, BF16)]
    flops = 6 * rows * width * feed
    return pl.pallas_call(
        kernel,
        grid=(feed // step,),
        in_specs=[part, part]
        + [pl.BlockSpec((width, step), lambda f: (0, f))] * 3
        + [block] * len(saved)
        + [pl.BlockSpec(memory_space=pl.ANY)] * len(held),
        out_specs=[full] + [block] * len(dtypes) + [part, part],
        out_shape=shapes + tail,
        scratch_shapes=[pltpu.VMEM((rows, width), F32)],
        input_output_aliases={n_in + k: k for k in range(len(held))},
        compiler_params=pltpu.CompilerParams(vmem_limit_bytes=32 * 1024 * 1024),
        cost_estimate=pl.CostEstimate(
            flops=flops, bytes_accessed=6 * width * feed, transcendentals=rows * feed
        ),
    )(*pair, *weights, *saved, *held)


def body(
    inputs,
    doc_lengths,
    w_query,
    w_key,
    w_value,
    w_out,
    gain_query,
    gain_key,
    gain_attn,
    w_gate,
    w_up,
    w_down,
    gain_ffn,
    cotangent,
):
    _, tok_count, model_width = inputs.shape
    n_x, n_core, n_z, n_y = (lax.axis_size(a) for a in ALL)
    n_seq, n_dp, n_all = n_z * n_y, n_x * n_core, n_x * n_core * n_z * n_y
    seq_at = lax.axis_index(SEQ)
    length = tok_count * n_seq
    score_scale = 1.0 / math.sqrt(HEAD_DIM)
    own_rows = w_query.shape[0]
    own_width = model_width // n_seq
    own_heads = own_width // HEAD_DIM
    feed_width = w_gate.shape[1]
    n_feed = n_core * n_z
    own_feed = feed_width // n_feed
    x_at, core_at, z_at, y_at = (lax.axis_index(a) for a in ALL)
    order = ring_order(n_z)
    ring = [(order[i], order[(i + 1) % n_z]) for i in range(n_z)]
    behind = jnp.array(
        [[order[(order.index(z) - s) % n_z] for z in range(n_z)] for s in range(n_z)], jnp.int32
    )
    tokens = inputs[0]

    def ring_send(part):
        return lax.ppermute(part, "z", ring)

    def seq_gather(own):
        chunks, held = [], own
        for step in range(n_z):
            chunks += [held, lax.ppermute(held, "y", SWAP)]
            if step < n_z - 1:
                held = ring_send(held)
        return jnp.concatenate(chunks, axis=0)

    def row_gather(own, gates):
        chunks, held = [], own
        for step in range(n_z):
            chunks.append((held, lax.ppermute(held, "y", SWAP)))
            if step < n_z - 1:
                held = ring_send(tie(held, *gates(step, held)))
        whole = jnp.zeros((n_seq * tok_count, own.shape[1]), own.dtype)
        for step, (mine, other) in enumerate(chunks):
            first = behind[step, z_at] * n_y * tok_count
            whole = lax.dynamic_update_slice(whole, mine, (first + y_at * tok_count, 0))
            whole = lax.dynamic_update_slice(whole, other, (first + (1 - y_at) * tok_count, 0))
        return whole, held

    def seq_order(array_in):
        chunks = []
        for step in range(n_z):
            for at_y in (y_at, 1 - y_at):
                first = (behind[step, z_at] * n_y + at_y) * tok_count
                chunks.append(lax.dynamic_slice_in_dim(array_in, first, tok_count))
        return jnp.concatenate(chunks, axis=0)

    def seq_sum(part_of):
        total = None
        for step in list(range(1, n_z)) + [0]:
            part = part_of(behind[step, z_at]).reshape(n_y, tok_count, model_width)
            away = lax.ppermute(pick(part, 1 - y_at).astype(BF16), "y", SWAP)
            mine = pick(part, y_at) + away.astype(F32)
            if total is not None:
                mine = mine + ring_send(total.astype(BF16)).astype(F32)
            total = mine
        return total

    def feed_weights(mats, earlier):
        blocks = jnp.stack(mats).reshape(len(mats), own_rows, n_feed, own_feed)
        mine = exchange(tie(blocks.transpose(2, 0, 1, 3), *earlier), FEED)
        return [mine[:, at].reshape(n_feed * own_rows, own_feed) for at in range(len(mats))]

    def rest_gather(mine, late, later):
        over_x, over_y = lax.ppermute(mine, "x", SWAP), lax.ppermute(mine, "y", SWAP)
        half = mine.shape[0] // 2
        corner_x = lax.ppermute(tie(over_x[:half], late), "y", SWAP)
        corner_y = lax.ppermute(tie(over_y[half:], late), "x", SWAP)
        mine = tie(mine, later)
        whole = jnp.zeros((n_x, n_y) + mine.shape, BF16)
        for at_x, at_y, first, part in (
            (x_at, y_at, 0, mine),
            (1 - x_at, y_at, 0, over_x),
            (x_at, 1 - y_at, 0, over_y),
            (1 - x_at, 1 - y_at, 0, corner_x),
            (1 - x_at, 1 - y_at, half, corner_y),
        ):
            whole = lax.dynamic_update_slice(whole, part[None, None], (at_x, at_y, first, 0))
        return whole.reshape(model_width, own_feed)

    def seq_total(term):
        term = term + lax.ppermute(term, "y", SWAP)
        hop = 1
        while hop < n_z:
            term = term + lax.ppermute(term, "z", [(z, z ^ hop) for z in range(n_z)])
            hop *= 2
        return term

    def to_feed_order(array_in):
        lead = array_in.shape[:-1]
        parts = array_in.reshape((-1, n_x, n_core, n_z, n_y, own_rows))
        return parts.transpose(0, 1, 4, 3, 2, 5).reshape(lead + (model_width,))

    def from_feed_order(array_in):
        lead = array_in.shape[:-1]
        parts = array_in.reshape((-1, n_x, n_y, n_z, n_core, own_rows))
        return parts.transpose(0, 1, 4, 3, 2, 5).reshape(lead + (model_width,))

    w_heads = jnp.stack([w_query, w_key, w_value])
    w_heads = w_heads.reshape(3, own_rows, n_seq, own_width).transpose(2, 1, 0, 3)
    w_heads = exchange(w_heads.reshape(n_seq, own_rows, 3 * own_width), SEQ)
    w_mine = w_heads.reshape(n_seq * own_rows, 3 * own_width)

    w_over = lax.ppermute(w_mine, "x", SWAP)
    w_heads = jnp.zeros((n_x, n_core) + w_mine.shape, BF16)
    for at_x, part in ((x_at, w_mine), (1 - x_at, w_over)):
        w_heads = lax.dynamic_update_slice(w_heads, part[None, None], (at_x, core_at, 0, 0))
        w_heads = lax.dynamic_update_slice(
            w_heads, core_swap(part)[None, None], (at_x, 1 - core_at, 0, 0)
        )
    w_heads = w_heads.reshape(model_width, 3 * own_width)
    def gates(step, held):
        return (w_mine,) if step == 1 else ()

    x_row, x_last = row_gather(tokens, gates)
    full_o = lax.all_gather(to_feed_order(w_out), ALL, axis=0, tiled=True)
    moved = feed_weights([w_gate, w_up, w_down.T], (x_last,))

    gains = spread(tie(jnp.stack([gain_query, gain_key, gain_attn, gain_ffn]), *moved), ALL)
    gains = gains.transpose(1, 0, 2).reshape(4, model_width).astype(F32)
    my_gq = lax.dynamic_slice_in_dim(gains[0:1], seq_at * own_width, own_width, 1)
    my_gk = lax.dynamic_slice_in_dim(gains[1:2], seq_at * own_width, own_width, 1)
    gain_a, gain_f = to_feed_order(gains[2]), to_feed_order(gains[3])

    qkv = matmul(x_row, w_heads)
    q_lin, k_lin = qkv[:, :own_width], qkv[:, own_width : 2 * own_width]
    squares = jnp.stack([jnp.sum(q_lin * q_lin, axis=1), jnp.sum(k_lin * k_lin, axis=1)])
    squares = seq_total(squares) / model_width
    factors = lax.rsqrt(squares + NORM_EPS).T
    q_factor, k_factor = factors[:, 0:1], factors[:, 1:2]
    tables = turn_tables(length)
    doc_ends = jnp.cumsum(doc_lengths[0])
    position = jnp.arange(length)
    doc_ids = jnp.sum((position[:, None] >= doc_ends[None, :]).astype(jnp.int32), axis=1)
    docs = (doc_ids[:, None], doc_ids[None, :])
    *saved, attended = attend(qkv, factors, my_gq, my_gk, tables, docs, own_heads)

    att_tok = exchange(attended.reshape(n_seq, tok_count, own_width), SEQ)
    att_tok = att_tok.transpose(1, 0, 2).reshape(tok_count, model_width)
    branch = matmul(att_tok, full_o)
    w_g = rest_gather(moved[0], attended, branch)
    w_u = lax.all_gather(moved[1], REST, axis=0, tiled=True)
    w_d = rest_gather(tie(moved[2], qkv), attended, branch)
    branch_norm, branch_factor = norm_apply(branch, gain_a)
    hidden = to_feed_order(tokens).astype(F32) + branch_norm
    hidden_low = hidden.astype(BF16)

    def feed_pass(own, saved, kernel, dtypes):
        held, total, rows = [], None, own
        for at in range(n_z):
            pair = (rows, core_swap(rows))
            if at < n_z - 1:
                rows = ring_send(rows)
            if at > 1:
                pair = tie(pair, total)
            *held, mine, away = feed_step(
                at, n_z, pair, (w_g, w_u, w_d), saved, held, kernel, dtypes
            )
            if at == 0:
                first = (mine, away)
            else:
                total = add_up(mine, away, total)
        return held, add_up(*first, total)

    def add_up(mine, away, total):
        mine = mine + core_swap(away).astype(F32)
        if total is not None:
            mine = mine + ring_send(total.astype(BF16)).astype(F32)
        return mine

    (hid, gate, upward, active), result = feed_pass(
        hidden_low, (), feed_kernel, (F32, F32, BF16)
    )
    result_norm, result_factor = norm_apply(result, gain_f)
    output = from_feed_order((hidden + result_norm).astype(BF16))

    grad_top = to_feed_order(cotangent[0]).astype(F32)
    grad_result, ffn_gain_term = norm_back(result, result_factor, gain_f, grad_top)
    def token_sum(left, right):
        return dot_left_t(left, right).astype(BF16)

    def rest_sum(term):
        return lax.psum_scatter(term, REST, scatter_dimension=0, tiled=True)

    def feed_home(term):
        return exchange(term.reshape(n_feed, own_rows, own_feed), FEED)

    def feed_rows(term):
        return term.transpose(1, 0, 2).reshape(own_rows, feed_width).astype(F32)

    def dp_sum(term):
        rows = term.shape[0] // n_dp

        def of(array_in, at):
            return lax.dynamic_slice_in_dim(array_in, at * rows, rows)

        def cores(at):
            return jnp.concatenate([of(term, x * n_core + at) for x in range(n_x)])

        away = core_swap(cores(1 - core_at))
        term = (cores(core_at).astype(F32) + away.astype(F32)).astype(BF16)
        away = lax.ppermute(of(term, 1 - x_at), "x", SWAP)
        return (of(term, x_at).astype(F32) + away.astype(F32)).astype(BF16)

    (g_res, g_gate, g_up), grad_ffn = feed_pass(
        grad_result.astype(BF16), (gate, upward), feed_back_kernel, (BF16, BF16)
    )
    grad_hidden = grad_top + grad_ffn
    term_d = token_sum(g_res, active)
    sum_d = rest_sum(term_d)
    term_g, term_u = token_sum(hid, g_gate), token_sum(hid, g_up)

    grad_branch, attn_gain_term = norm_back(branch, branch_factor, gain_a, grad_hidden)
    grad_branch = grad_branch.astype(BF16)
    grad_attended = dot_right_t(grad_branch, full_o).astype(BF16)
    g_att = grad_attended.reshape(tok_count, n_seq, own_width).transpose(1, 0, 2)
    g_att = exchange(g_att, SEQ).reshape(length, own_width)
    g_att = tie(g_att, term_g, term_u)
    sum_g, sum_u = rest_sum(term_g), rest_sum(term_u)

    grad_q, grad_k, grad_v, dot_q, dot_k = attend_back(
        saved, g_att, qkv, my_gq, my_gk, tables, docs, own_heads
    )
    dots = jnp.stack([jnp.sum(dot_q, axis=(0, 2)), jnp.sum(dot_k, axis=(0, 2))])
    dots = seq_total(dots) / model_width
    home_d = feed_home(tie(sum_d, dots))

    branch_row = seq_gather(tie(grad_branch, dots))
    grad_w_out = dot_left_t(seq_order(attended), branch_row).astype(BF16)
    grad_w_out = dp_sum(grad_w_out)
    home = [(d * n_seq + s, s * n_dp + d) for d in range(n_dp) for s in range(n_seq)]
    grad_w_out = lax.ppermute(grad_w_out, ALL, home)
    grad_w_out = from_feed_order(grad_w_out).astype(F32)


    def lin_back(grad_in, lin, factor, gain_vec, mean_dot):
        gain_term = jnp.sum(grad_in * lin * factor, axis=0)
        grad_out = factor * (grad_in * gain_vec) - lin * (factor * factor * factor) * mean_dot
        return grad_out.astype(BF16), gain_term

    grad_q_lin, query_gain_term = lin_back(grad_q, q_lin, q_factor, my_gq, dots[0][:, None])
    grad_k_lin, key_gain_term = lin_back(grad_k, k_lin, k_factor, my_gk, dots[1][:, None])
    grad_lin = jnp.concatenate([grad_q_lin, grad_k_lin, grad_v], axis=1)

    def row_part(z_of):
        rows = lax.dynamic_slice_in_dim(grad_lin, z_of * n_y * tok_count, n_y * tok_count)
        return dot_right_t(rows, w_heads)

    grad_input = from_feed_order(grad_hidden) + seq_sum(row_part)

    grad_heads = dot_left_t(x_row, grad_lin).astype(BF16)
    grad_heads = dp_sum(grad_heads)
    home_g = feed_home(tie(sum_g, home_d))
    home_u = feed_home(tie(sum_u, home_g))
    grad_w_gate, grad_w_up = feed_rows(home_g), feed_rows(home_u)
    grad_w_down = feed_rows(home_d).T
    grad_heads = exchange(grad_heads.reshape(n_seq, own_rows, 3 * own_width), SEQ)
    grad_heads = grad_heads.reshape(n_seq, own_rows, 3, own_width).transpose(2, 1, 0, 3)
    grad_heads = grad_heads.reshape(3, own_rows, model_width).astype(F32)

    def place(term):
        return lax.dynamic_update_slice(
            jnp.zeros((model_width,), F32), term, (seq_at * own_width,)
        )

    gain_terms = jnp.stack(
        [
            place(query_gain_term),
            place(key_gain_term),
            from_feed_order(attn_gain_term),
            from_feed_order(ffn_gain_term),
        ]
    )
    gain_terms = gain_terms.reshape(4, n_all, own_rows).transpose(1, 0, 2)
    gain_grads = jnp.sum(exchange(gain_terms, ALL), axis=0)

    return (
        output[None],
        grad_input[None],
        grad_heads[0],
        grad_heads[1],
        grad_heads[2],
        grad_w_out,
        gain_grads[0],
        gain_grads[1],
        gain_grads[2],
        grad_w_gate,
        grad_w_up,
        grad_w_down,
        gain_grads[3],
    )


def plain_rotation(first_pos, tok_count):
    half_dim = HEAD_DIM // 2
    position = (first_pos + jnp.arange(tok_count)).astype(jnp.float32)
    inverse = jnp.exp(-(jnp.arange(half_dim).astype(jnp.float32) / half_dim) * math.log(ROPE_BASE))
    angles = position[:, None] * inverse[None, :]
    return (jnp.cos(angles)[None, :, None, :], jnp.sin(angles)[None, :, None, :])


def plain_rotate(array_in, cosine, sine_t, turn_sign):
    half_dim = array_in.shape[-1] // 2
    first_half = array_in[..., :half_dim]
    second_half = array_in[..., half_dim:]
    return jnp.concatenate(
        [
            first_half * cosine - turn_sign * second_half * sine_t,
            second_half * cosine + turn_sign * first_half * sine_t,
        ],
        axis=-1,
    )


def plain_body(
    inputs,
    doc_lengths,
    w_query,
    w_key,
    w_value,
    w_out,
    gain_query,
    gain_key,
    gain_attn,
    w_gate,
    w_up,
    w_down,
    gain_ffn,
    cotangent,
):
    row_count, tok_count, model_width = inputs.shape
    length = tok_count * lax.axis_size("seq")
    first_pos = lax.axis_index("seq") * tok_count
    score_scale = 1.0 / math.sqrt(HEAD_DIM)
    tokens = inputs.reshape(row_count * tok_count, model_width)

    def heads_first(array_in):
        return array_in.reshape(row_count, tok_count, HEADS, HEAD_DIM).transpose(2, 0, 1, 3)

    def heads_last(array_in):
        return array_in.transpose(1, 2, 0, 3).reshape(row_count * tok_count, HEADS * HEAD_DIM)

    full_q, full_k, full_v, full_o, full_gq, full_gk, full_ga = (
        lax.all_gather(w_query, ("dp", "seq"), axis=0, tiled=True),
        lax.all_gather(w_key, ("dp", "seq"), axis=0, tiled=True),
        lax.all_gather(w_value, ("dp", "seq"), axis=0, tiled=True),
        lax.all_gather(w_out, ("dp", "seq"), axis=0, tiled=True),
        lax.all_gather(gain_query, ("dp", "seq"), axis=0, tiled=True),
        lax.all_gather(gain_key, ("dp", "seq"), axis=0, tiled=True),
        lax.all_gather(gain_attn, ("dp", "seq"), axis=0, tiled=True),
    )
    cosine, sine_t = plain_rotation(first_pos, tok_count)
    q_lin = matmul(tokens, full_q)
    k_lin = matmul(tokens, full_k)
    v_lin = matmul(tokens, full_v)
    q_norm, q_factor = norm_apply(q_lin, full_gq.astype(jnp.float32))
    k_norm, k_factor = norm_apply(k_lin, full_gk.astype(jnp.float32))
    queries = (
        plain_rotate(q_norm.reshape(row_count, tok_count, HEADS, HEAD_DIM), cosine, sine_t, 1.0)
        .astype(jnp.bfloat16)
        .transpose(2, 0, 1, 3)
    )
    keys_mine = (
        plain_rotate(k_norm.reshape(row_count, tok_count, HEADS, HEAD_DIM), cosine, sine_t, 1.0)
        .astype(jnp.bfloat16)
        .transpose(2, 0, 1, 3)
    )
    values_mine = heads_first(v_lin.astype(jnp.bfloat16))
    keys_all, values_all = (
        lax.all_gather(keys_mine, "seq", axis=2, tiled=True),
        lax.all_gather(values_mine, "seq", axis=2, tiled=True),
    )
    doc_ends = jnp.cumsum(doc_lengths, axis=1)
    position = jnp.arange(length)
    doc_ids = jnp.sum((position[None, :, None] >= doc_ends[:, None, :]).astype(jnp.int32), axis=2)
    my_pos = first_pos + jnp.arange(tok_count)
    docs_mine = lax.dynamic_slice_in_dim(doc_ids, first_pos, tok_count, 1)
    allowed = (position[None, None, :] <= my_pos[None, :, None]) & (
        doc_ids[:, None, :] == docs_mine[:, :, None]
    )

    def scores_of(q_head, k_head):
        raw_scores = (
            jnp.einsum("rtd,rkd->rtk", q_head, k_head, preferred_element_type=jnp.float32)
            * score_scale
        )
        return jnp.where(allowed, raw_scores, MASK_FILL)

    def attend(head_item):
        q_head, k_head, v_head = head_item
        scores = scores_of(q_head, k_head)
        row_max = jnp.max(scores, axis=-1, keepdims=True)
        row_total = row_max + jnp.log(jnp.sum(jnp.exp(scores - row_max), axis=-1, keepdims=True))
        attn_probs = jnp.exp(scores - row_total).astype(jnp.bfloat16)
        head_out = jnp.einsum(
            "rtk,rkd->rtd", attn_probs, v_head, preferred_element_type=jnp.float32
        )
        return (head_out, row_total[..., 0])

    attn_mixed, totals = lax.map(attend, (queries, keys_all, values_all))
    attended = heads_last(attn_mixed.astype(jnp.bfloat16))
    branch = matmul(attended, full_o)
    branch_norm, branch_factor = norm_apply(branch, full_ga.astype(jnp.float32))
    hidden = tokens.astype(jnp.float32) + branch_norm
    hidden_low = hidden.astype(jnp.bfloat16)
    gate_full, up_full, down_full, ffn_gain_full = (
        lax.all_gather(w_gate, ("dp", "seq"), axis=0, tiled=True),
        lax.all_gather(w_up, ("dp", "seq"), axis=0, tiled=True),
        lax.all_gather(w_down, ("dp", "seq"), axis=1, tiled=True),
        lax.all_gather(gain_ffn, ("dp", "seq"), axis=0, tiled=True),
    )
    gate_act = matmul(hidden_low, gate_full)
    upward = matmul(hidden_low, up_full)
    gate_sig = jax.nn.sigmoid(gate_act)
    active = (gate_act * gate_sig * upward).astype(jnp.bfloat16)
    result = matmul(active, down_full)
    result_norm, result_factor = norm_apply(result, ffn_gain_full.astype(jnp.float32))
    output = (hidden + result_norm).astype(jnp.bfloat16).reshape(row_count, tok_count, model_width)
    grad_top = cotangent.reshape(row_count * tok_count, model_width).astype(jnp.float32)
    grad_result, ffn_gain_term = norm_back(
        result, result_factor, ffn_gain_full.astype(jnp.float32), grad_top
    )
    grad_result = grad_result.astype(jnp.bfloat16)
    grad_active = dot_right_t(grad_result, down_full)
    grad_gate = (grad_active * upward * gate_sig * (1.0 + gate_act * (1.0 - gate_sig))).astype(
        jnp.bfloat16
    )
    grad_up = (grad_active * gate_act * gate_sig).astype(jnp.bfloat16)
    grad_hidden = grad_top + dot_right_t(grad_gate, gate_full) + dot_right_t(grad_up, up_full)
    feedforward_grads = lax.psum_scatter(
        jnp.concatenate(
            [
                dot_left_t(hidden_low, grad_gate),
                dot_left_t(hidden_low, grad_up),
                dot_left_t(grad_result, active),
            ],
            axis=1,
        ),
        ("dp", "seq"),
        scatter_dimension=0,
        tiled=True,
    )
    grad_branch, attn_gain_term = norm_back(
        branch, branch_factor, full_ga.astype(jnp.float32), grad_hidden
    )
    grad_branch = grad_branch.astype(jnp.bfloat16)
    back_q, back_k, back_v, back_o, back_gq, back_gk = (
        lax.all_gather(w_query, ("dp", "seq"), axis=0, tiled=True),
        lax.all_gather(w_key, ("dp", "seq"), axis=0, tiled=True),
        lax.all_gather(w_value, ("dp", "seq"), axis=0, tiled=True),
        lax.all_gather(w_out, ("dp", "seq"), axis=0, tiled=True),
        lax.all_gather(gain_query, ("dp", "seq"), axis=0, tiled=True),
        lax.all_gather(gain_key, ("dp", "seq"), axis=0, tiled=True),
    )
    grad_attended = dot_right_t(grad_branch, back_o).astype(jnp.bfloat16)
    grad_w_out_term = dot_left_t(attended, grad_branch)
    grad_mixed = heads_first(grad_attended)

    def head_back(head_item):
        q_head, k_head, v_head, g_head, t_head = head_item
        prob_full = jnp.exp(scores_of(q_head, k_head) - t_head[..., None])
        grad_probs = jnp.einsum("rtd,rkd->rtk", g_head, v_head, preferred_element_type=jnp.float32)
        offsets = jnp.sum(prob_full * grad_probs, axis=-1, keepdims=True)
        grad_scores = (prob_full * (grad_probs - offsets)).astype(jnp.bfloat16)
        grad_q = (
            jnp.einsum("rtk,rkd->rtd", grad_scores, k_head, preferred_element_type=jnp.float32)
            * score_scale
        )
        grad_k = (
            jnp.einsum("rtk,rtd->rkd", grad_scores, q_head, preferred_element_type=jnp.float32)
            * score_scale
        )
        grad_v = jnp.einsum(
            "rtk,rtd->rkd",
            prob_full.astype(jnp.bfloat16),
            g_head,
            preferred_element_type=jnp.float32,
        )
        return (grad_q, grad_k, grad_v)

    grad_queries, key_terms, value_terms = lax.map(
        head_back, (queries, keys_all, values_all, grad_mixed, totals)
    )
    grad_keys, grad_values = (
        lax.psum_scatter(
            key_terms.astype(jnp.bfloat16), "seq", scatter_dimension=2, tiled=True
        ).astype(jnp.float32),
        lax.psum_scatter(
            value_terms.astype(jnp.bfloat16), "seq", scatter_dimension=2, tiled=True
        ).astype(jnp.float32),
    )
    grad_q_norm = plain_rotate(grad_queries.transpose(1, 2, 0, 3), cosine, sine_t, -1.0).reshape(
        row_count * tok_count, model_width
    )
    grad_k_norm = plain_rotate(grad_keys.transpose(1, 2, 0, 3), cosine, sine_t, -1.0).reshape(
        row_count * tok_count, model_width
    )
    grad_q_lin, query_gain_term = norm_back(
        q_lin, q_factor, back_gq.astype(jnp.float32), grad_q_norm
    )
    grad_k_lin, key_gain_term = norm_back(k_lin, k_factor, back_gk.astype(jnp.float32), grad_k_norm)
    grad_q_lin = grad_q_lin.astype(jnp.bfloat16)
    grad_k_lin = grad_k_lin.astype(jnp.bfloat16)
    grad_v_lin = heads_last(grad_values).astype(jnp.bfloat16)
    grad_input = (
        grad_hidden
        + dot_right_t(grad_q_lin, back_q)
        + dot_right_t(grad_k_lin, back_k)
        + dot_right_t(grad_v_lin, back_v)
    )
    attention_grads = (
        lax.psum_scatter(
            dot_left_t(tokens, grad_q_lin), ("dp", "seq"), scatter_dimension=0, tiled=True
        ),
        lax.psum_scatter(
            dot_left_t(tokens, grad_k_lin), ("dp", "seq"), scatter_dimension=0, tiled=True
        ),
        lax.psum_scatter(
            dot_left_t(tokens, grad_v_lin), ("dp", "seq"), scatter_dimension=0, tiled=True
        ),
        lax.psum_scatter(grad_w_out_term, ("dp", "seq"), scatter_dimension=0, tiled=True),
        lax.psum_scatter(query_gain_term, ("dp", "seq"), scatter_dimension=0, tiled=True),
        lax.psum_scatter(key_gain_term, ("dp", "seq"), scatter_dimension=0, tiled=True),
        lax.psum_scatter(attn_gain_term, ("dp", "seq"), scatter_dimension=0, tiled=True),
        lax.psum_scatter(ffn_gain_term, ("dp", "seq"), scatter_dimension=0, tiled=True),
    )
    feed_width = w_gate.shape[1]
    grad_w_gate = feedforward_grads[:, :feed_width]
    grad_w_up = feedforward_grads[:, feed_width : 2 * feed_width]
    grad_w_down = feedforward_grads[:, 2 * feed_width :].T
    return (
        output,
        grad_input.reshape(row_count, tok_count, model_width),
        attention_grads[0],
        attention_grads[1],
        attention_grads[2],
        attention_grads[3],
        attention_grads[4],
        attention_grads[5],
        attention_grads[6],
        grad_w_gate,
        grad_w_up,
        grad_w_down,
        attention_grads[7],
    )


def solution(mesh):
    n_dp, n_seq = mesh.shape["dp"], mesh.shape["seq"]
    if n_dp == 4 and n_seq % 2 == 0 and HEADS % n_seq == 0:
        grid = Mesh(mesh.devices.reshape(n_dp // 2, 2, n_seq // 2, 2), ALL)
        layer, dp, seq = body, DP, SEQ
    else:
        grid, layer, dp, seq = mesh, plain_body, ("dp",), ("seq",)
    rows = P(dp, seq, None)
    split = P(dp + seq, None)
    vector = P(dp + seq)
    down = P(None, dp + seq)
    return jax.shard_map(
        layer,
        mesh=grid,
        in_specs=(rows, P(dp, None))
        + (split,) * 4
        + (vector,) * 3
        + (split, split, down, vector, rows),
        out_specs=(rows, rows) + (split,) * 4 + (vector,) * 3 + (split, split, down, vector),
        check_vma=False,
    )
```

```python
import math

import jax
import jax.numpy as jnp
from jax import lax
from jax.experimental import pallas as pl
from jax.experimental.pallas import tpu as pltpu
from jax.sharding import Mesh
from jax.sharding import PartitionSpec as P

HEADS = 16
HEAD_DIM = 128


NORM_EPS = 1e-06
ROPE_BASE = 500000.0
MASK_FILL = -1e30

SEQ = ("z", "y")
DP = ("x", "core")
FEED = ("z", "core")
REST = ("x", "y")
ALL = ("x", "core", "z", "y")
SWAP = [(0, 1), (1, 0)]
F32 = jnp.float32
BF16 = jnp.bfloat16


def matmul(left_mat, right_mat):
    return jnp.dot(left_mat, right_mat, preferred_element_type=F32)


def dot_right_t(left_mat, right_mat):
    return lax.dot_general(
        left_mat, right_mat, (((1,), (1,)), ((), ())), preferred_element_type=F32
    )


def dot_left_t(left_mat, right_mat):
    return lax.dot_general(
        left_mat, right_mat, (((0,), (0,)), ((), ())), preferred_element_type=F32
    )


def norm_apply(array_in, gain_vec):
    factor = lax.rsqrt(jnp.mean(array_in * array_in, axis=-1, keepdims=True) + NORM_EPS)
    return (array_in * factor * gain_vec, factor)


def norm_back(array_in, factor, gain_vec, grad_in):
    gain_term = jnp.sum(grad_in * array_in * factor, axis=0)
    scaled = grad_in * gain_vec
    grad_out = factor * scaled - array_in * (factor * factor * factor) * jnp.mean(
        scaled * array_in, axis=-1, keepdims=True
    )
    return (grad_out, gain_term)


def turn_tables(tok_count):
    half_dim = HEAD_DIM // 2
    position = jnp.arange(tok_count).astype(F32)
    inverse = jnp.exp(-(jnp.arange(half_dim).astype(F32) / half_dim) * math.log(ROPE_BASE))
    angles = position[:, None] * inverse[None, :]
    cosine, sine_t = jnp.cos(angles), jnp.sin(angles)
    return (
        jnp.concatenate([cosine, cosine], axis=1),
        jnp.concatenate([-sine_t, sine_t], axis=1),
    )


def rotate(array_in, cosine, sine_t):
    return array_in * cosine + pltpu.roll(array_in, HEAD_DIM // 2, 1) * sine_t


def rotate_back(array_in, cosine, sine_t):
    return array_in * cosine - pltpu.roll(array_in, HEAD_DIM // 2, 1) * sine_t


def exchange(array_in, axes):
    return lax.all_to_all(array_in, axes, split_axis=0, concat_axis=0, tiled=True)


def spread(array_in, axes):
    count = lax.axis_size(axes)
    return exchange(jnp.broadcast_to(array_in[None], (count,) + array_in.shape), axes)


def tie(value, *earlier):
    return lax.optimization_barrier((value,) + earlier)[0]


def ring_order(count):
    return [0] + list(range(1, count, 2)) + [v for v in range(count - 1, 0, -1) if v % 2 == 0]


def core_swap(array_in):
    return lax.ppermute(array_in, "core", SWAP)


def pick(array_in, at, axis=0):
    return lax.dynamic_index_in_dim(array_in, at, axis, keepdims=False)


def visible(doc_col, doc_row, first, rows, width):
    at = first + lax.broadcasted_iota(jnp.int32, (rows, width), 0)
    of = lax.broadcasted_iota(jnp.int32, (rows, width), 1)
    return (of <= at) & (doc_col == doc_row)


def attend_kernel(
    step,
    q_lin,
    k_lin,
    v_lin,
    factors,
    gain_q,
    gain_k,
    cosine,
    sine_t,
    doc_col,
    doc_row,
    queries,
    keys,
    values,
    totals,
    attended,
):
    cos, sin = cosine[...], sine_t[...]
    queries[...] = rotate(q_lin[...] * factors[:, 0:1] * gain_q[...], cos, sin).astype(BF16)
    keys[...] = rotate(k_lin[...] * factors[:, 1:2] * gain_k[...], cos, sin).astype(BF16)
    values[...] = v_lin[...].astype(BF16)
    scale = 1.0 / math.sqrt(HEAD_DIM)
    for first in range(0, queries.shape[0], step):
        width = first + step
        mine = pl.ds(first, step)
        scores = dot_right_t(queries[mine, :], keys[0:width, :]) * scale
        seen = visible(doc_col[mine, :], doc_row[:, 0:width], first, step, width)
        scores = jnp.where(seen, scores, MASK_FILL)
        row_max = jnp.max(scores, axis=1, keepdims=True)
        row_sum = jnp.sum(jnp.exp(scores - row_max), axis=1, keepdims=True)
        total = row_max + jnp.log(row_sum)
        probs = jnp.exp(scores - total).astype(BF16)
        totals[0, mine, :] = total
        attended[mine, :] = matmul(probs, values[0:width, :]).astype(BF16)


def attend_back_kernel(
    step,
    queries,
    keys,
    values,
    totals,
    g_att,
    q_lin,
    k_lin,
    gain_q,
    gain_k,
    cosine,
    sine_t,
    doc_col,
    doc_row,
    grad_q,
    grad_k,
    grad_v,
    dot_q,
    dot_k,
    k_sum,
    v_sum,
):
    scale = 1.0 / math.sqrt(HEAD_DIM)
    k_sum[...] = jnp.zeros_like(k_sum)
    v_sum[...] = jnp.zeros_like(v_sum)
    for first in range(0, queries.shape[0], step):
        width = first + step
        mine, upto = pl.ds(first, step), pl.ds(0, width)
        scores = dot_right_t(queries[mine, :], keys[upto, :]) * scale
        seen = visible(doc_col[mine, :], doc_row[:, 0:width], first, step, width)
        scores = jnp.where(seen, scores, MASK_FILL)
        prob_full = jnp.exp(scores - totals[0, mine, :])
        grad_probs = dot_right_t(g_att[mine, :], values[upto, :])
        offsets = jnp.sum(prob_full * grad_probs, axis=1, keepdims=True)
        grad_scores = (prob_full * (grad_probs - offsets)).astype(BF16)
        back = matmul(grad_scores, keys[upto, :]) * scale
        back = rotate_back(back, cosine[mine, :], sine_t[mine, :])
        grad_q[mine, :] = back
        dot_q[0, mine, :] = jnp.sum(back * gain_q[...] * q_lin[mine, :], axis=1, keepdims=True)
        k_sum[upto, :] += dot_left_t(grad_scores, queries[mine, :])
        v_sum[upto, :] += dot_left_t(prob_full.astype(BF16), g_att[mine, :])
    back = rotate_back(k_sum[...] * scale, cosine[...], sine_t[...])
    grad_k[...] = back
    dot_k[0] = jnp.sum(back * gain_k[...] * k_lin[...], axis=1, keepdims=True)
    grad_v[...] = v_sum[...].astype(BF16)


def head_specs(length, heads):
    def part(offset):
        return pl.BlockSpec((length, HEAD_DIM), lambda h: (0, h + offset))

    def gain():
        return pl.BlockSpec((1, HEAD_DIM), lambda h: (0, h))

    def whole(shape):
        return pl.BlockSpec(shape, lambda h: (0, 0))

    each = pl.BlockSpec((1, length, 1), lambda h: (h, 0, 0))
    table = whole((length, HEAD_DIM))
    docs = [whole((length, 1)), whole((1, length))]
    return part, gain, whole, each, table, docs


def attend(qkv, factors, gain_q, gain_k, tables, docs, heads):
    length = qkv.shape[0]
    part, gain, whole, each, table, doc_specs = head_specs(length, heads)
    low = jax.ShapeDtypeStruct((length, heads * HEAD_DIM), BF16)
    step = min(256, length)
    pairs = heads * length * length * HEAD_DIM
    return pl.pallas_call(
        lambda *refs: attend_kernel(step, *refs),
        grid=(heads,),
        in_specs=[part(0), part(heads), part(2 * heads), whole((length, 2)), gain(), gain()]
        + [table, table]
        + doc_specs,
        out_specs=[part(0), part(0), part(0), each, part(0)],
        out_shape=[low, low, low, jax.ShapeDtypeStruct((heads, length, 1), F32), low],
        compiler_params=pltpu.CompilerParams(vmem_limit_bytes=24 * 1024 * 1024),
        cost_estimate=pl.CostEstimate(
            flops=3 * pairs, bytes_accessed=qkv.size * 6, transcendentals=heads * length * length
        ),
    )(qkv, qkv, qkv, factors, gain_q, gain_k, *tables, *docs)


def attend_back(saved, g_att, qkv, gain_q, gain_k, tables, docs, heads):
    queries, keys, values, totals = saved
    length = qkv.shape[0]
    part, gain, whole, each, table, doc_specs = head_specs(length, heads)
    flat = jax.ShapeDtypeStruct((length, heads * HEAD_DIM), F32)
    low = jax.ShapeDtypeStruct((length, heads * HEAD_DIM), BF16)
    line = jax.ShapeDtypeStruct((heads, length, 1), F32)
    step = min(256, length)
    pairs = heads * length * length * HEAD_DIM
    return pl.pallas_call(
        lambda *refs: attend_back_kernel(step, *refs),
        grid=(heads,),
        in_specs=[part(0), part(0), part(0), each, part(0), part(0), part(heads), gain(), gain()]
        + [table, table]
        + doc_specs,
        out_specs=[part(0), part(0), part(0), each, each],
        out_shape=[flat, flat, low, line, line],
        scratch_shapes=[pltpu.VMEM((length, HEAD_DIM), F32)] * 2,
        compiler_params=pltpu.CompilerParams(vmem_limit_bytes=24 * 1024 * 1024),
        cost_estimate=pl.CostEstimate(
            flops=7 * pairs, bytes_accessed=qkv.size * 8, transcendentals=heads * length * length
        ),
    )(queries, keys, values, totals, g_att, qkv, qkv, gain_q, gain_k, *tables, *docs)


def feed_kernel(part, other, w_g, w_u, w_d, *refs):
    hid, gate, upward, active, mine, away, total = refs[-7:]
    block, tokens = pl.program_id(0), part.shape[0]

    @pl.when(block == 0)
    def _():
        hid[:tokens, :] = part[...]
        hid[tokens:, :] = other[...]

    g = matmul(hid[...], w_g[...])
    u = matmul(hid[...], w_u[...])
    a = (g * (1.0 / (1.0 + jnp.exp(-g))) * u).astype(BF16)
    gate[...], upward[...], active[...] = g, u, a
    term = dot_right_t(a, w_d[...])

    @pl.when(block == 0)
    def _():
        total[...] = term

    @pl.when(block > 0)
    def _():
        total[...] += term

    @pl.when(block == pl.num_programs(0) - 1)
    def _():
        mine[...] = total[:tokens, :]
        away[...] = total[tokens:, :].astype(BF16)


def feed_back_kernel(part, other, w_g, w_u, w_d, gate, upward, *refs):
    g_res, g_gate, g_up, mine, away, total = refs[-6:]
    block, tokens = pl.program_id(0), part.shape[0]

    @pl.when(block == 0)
    def _():
        g_res[:tokens, :] = part[...]
        g_res[tokens:, :] = other[...]

    a = matmul(g_res[...], w_d[...])
    g, u = gate[...], upward[...]
    s = 1.0 / (1.0 + jnp.exp(-g))
    gg = (a * u * s * (1.0 + g * (1.0 - s))).astype(BF16)
    gu = (a * g * s).astype(BF16)
    g_gate[...], g_up[...] = gg, gu
    term = dot_right_t(gg, w_g[...]) + dot_right_t(gu, w_u[...])

    @pl.when(block == 0)
    def _():
        total[...] = term

    @pl.when(block > 0)
    def _():
        total[...] += term

    @pl.when(block == pl.num_programs(0) - 1)
    def _():
        mine[...] = total[:tokens, :]
        away[...] = total[tokens:, :].astype(BF16)


def feed_step(at, count, pair, weights, saved, held, kernel, dtypes):
    tokens, width = pair[0].shape
    feed = weights[0].shape[1]
    step = min(256, feed)
    rows = 2 * tokens
    block = pl.BlockSpec((rows, step), lambda f: (at, f))
    part = pl.BlockSpec((tokens, width), lambda f: (0, 0))
    full = pl.BlockSpec((rows, width), lambda f: (at, 0))
    n_in = 5 + len(saved)
    shapes = [jax.ShapeDtypeStruct((count * rows, width), BF16)]
    shapes += [jax.ShapeDtypeStruct((count * rows, feed), d) for d in dtypes]
    tail = [jax.ShapeDtypeStruct((tokens, width), d) for d in (F32, BF16)]
    flops = 6 * rows * width * feed
    return pl.pallas_call(
        kernel,
        grid=(feed // step,),
        in_specs=[part, part]
        + [pl.BlockSpec((width, step), lambda f: (0, f))] * 3
        + [block] * len(saved)
        + [pl.BlockSpec(memory_space=pl.ANY)] * len(held),
        out_specs=[full] + [block] * len(dtypes) + [part, part],
        out_shape=shapes + tail,
        scratch_shapes=[pltpu.VMEM((rows, width), F32)],
        input_output_aliases={n_in + k: k for k in range(len(held))},
        compiler_params=pltpu.CompilerParams(vmem_limit_bytes=32 * 1024 * 1024),
        cost_estimate=pl.CostEstimate(
            flops=flops, bytes_accessed=6 * width * feed, transcendentals=rows * feed
        ),
    )(*pair, *weights, *saved, *held)


def body(
    inputs,
    doc_lengths,
    w_query,
    w_key,
    w_value,
    w_out,
    gain_query,
    gain_key,
    gain_attn,
    w_gate,
    w_up,
    w_down,
    gain_ffn,
    cotangent,
):
    _, tok_count, model_width = inputs.shape
    n_x, n_core, n_z, n_y = (lax.axis_size(a) for a in ALL)
    n_seq, n_dp, n_all = n_z * n_y, n_x * n_core, n_x * n_core * n_z * n_y
    seq_at = lax.axis_index(SEQ)
    length = tok_count * n_seq
    score_scale = 1.0 / math.sqrt(HEAD_DIM)
    own_rows = w_query.shape[0]
    own_width = model_width // n_seq
    own_heads = own_width // HEAD_DIM
    feed_width = w_gate.shape[1]
    n_feed = n_core * n_z
    own_feed = feed_width // n_feed
    x_at, core_at, z_at, y_at = (lax.axis_index(a) for a in ALL)
    order = ring_order(n_z)
    ring = [(order[i], order[(i + 1) % n_z]) for i in range(n_z)]
    behind = jnp.array(
        [[order[(order.index(z) - s) % n_z] for z in range(n_z)] for s in range(n_z)], jnp.int32
    )
    tokens = inputs[0]

    def ring_send(part):
        return lax.ppermute(part, "z", ring)

    def seq_gather(own):
        chunks, held = [], own
        for step in range(n_z):
            chunks += [held, lax.ppermute(held, "y", SWAP)]
            if step < n_z - 1:
                held = ring_send(held)
        return jnp.concatenate(chunks, axis=0)

    def row_gather(own, gates):
        chunks, held = [], own
        for step in range(n_z):
            chunks.append((held, lax.ppermute(held, "y", SWAP)))
            if step < n_z - 1:
                held = ring_send(tie(held, *gates(step, held)))

        def whole(first, count):
            out = jnp.zeros((n_seq * count, own.shape[1]), own.dtype)
            for step, pair in enumerate(chunks):
                for at_y, part in zip((y_at, 1 - y_at), pair):
                    at = (behind[step, z_at] * n_y + at_y) * count
                    part = part[first : first + count]
                    out = lax.dynamic_update_slice(out, part, (at, 0))
            return out

        return whole(0, tok_count), whole(tok_count, own.shape[0] - tok_count), held

    def dp_gather(mine):
        out = jnp.zeros((n_x, n_core) + mine.shape, mine.dtype)
        for at_x, part in ((x_at, mine), (1 - x_at, lax.ppermute(mine, "x", SWAP))):
            for at_core, block in ((core_at, part), (1 - core_at, core_swap(part))):
                block = block[None, None]
                out = lax.dynamic_update_slice(out, block, (at_x, at_core, 0, 0))
        return out.reshape((n_dp * mine.shape[0], mine.shape[1]))

    def seq_order(array_in):
        chunks = []
        for step in range(n_z):
            for at_y in (y_at, 1 - y_at):
                first = (behind[step, z_at] * n_y + at_y) * tok_count
                chunks.append(lax.dynamic_slice_in_dim(array_in, first, tok_count))
        return jnp.concatenate(chunks, axis=0)

    def seq_sum(part_of):
        total = None
        for step in list(range(1, n_z)) + [0]:
            part = part_of(behind[step, z_at]).reshape(n_y, tok_count, model_width)
            away = lax.ppermute(pick(part, 1 - y_at).astype(BF16), "y", SWAP)
            mine = pick(part, y_at) + away.astype(F32)
            if total is not None:
                mine = mine + ring_send(total.astype(BF16)).astype(F32)
            total = mine
        return total

    def feed_weights(mats, earlier):
        blocks = jnp.stack(mats).reshape(len(mats), own_rows, n_feed, own_feed)
        mine = exchange(tie(blocks.transpose(2, 0, 1, 3), *earlier), FEED)
        return [mine[:, at].reshape(n_feed * own_rows, own_feed) for at in range(len(mats))]

    def rest_send(mine):
        return mine, lax.ppermute(mine, "y", SWAP), lax.ppermute(mine, "x", SWAP)

    def rest_gather(sent, corner, later):
        mine, over_y, over_x = sent
        mine = tie(mine, later)
        whole = jnp.zeros((n_x, n_y) + mine.shape, BF16)
        for at_x, at_y, part in (
            (x_at, y_at, mine),
            (1 - x_at, y_at, over_x),
            (x_at, 1 - y_at, over_y),
            (1 - x_at, 1 - y_at, corner),
        ):
            whole = lax.dynamic_update_slice(whole, part[None, None], (at_x, at_y, 0, 0))
        return whole.reshape(model_width, own_feed)

    def seq_total(term):
        return jnp.sum(spread(term, SEQ), axis=0)

    def to_feed_order(array_in):
        lead = array_in.shape[:-1]
        parts = array_in.reshape((-1, n_x, n_core, n_z, n_y, own_rows))
        return parts.transpose(0, 1, 4, 3, 2, 5).reshape(lead + (model_width,))

    def from_feed_order(array_in):
        lead = array_in.shape[:-1]
        parts = array_in.reshape((-1, n_x, n_y, n_z, n_core, own_rows))
        return parts.transpose(0, 1, 4, 3, 2, 5).reshape(lead + (model_width,))

    gains = spread(jnp.stack([gain_query, gain_key, gain_attn, gain_ffn]), ALL)
    gains = gains.transpose(1, 0, 2).reshape(4, model_width).astype(F32)
    my_gq = lax.dynamic_slice_in_dim(gains[0:1], seq_at * own_width, own_width, 1)
    my_gk = lax.dynamic_slice_in_dim(gains[1:2], seq_at * own_width, own_width, 1)
    gain_a, gain_f = to_feed_order(gains[2]), to_feed_order(gains[3])

    w_heads = jnp.stack([w_query, w_key, w_value])
    w_heads = w_heads.reshape(3, own_rows, n_seq, own_width).transpose(2, 1, 0, 3)
    w_heads = w_heads.reshape(n_seq, own_rows, 3 * own_width)
    w_heads = exchange(tie(w_heads, gains), SEQ)
    w_mine = w_heads.reshape(n_seq * own_rows, 3 * own_width)

    w_heads = dp_gather(w_mine)
    def gates(step, held):
        return (w_mine,) if step == 1 else ()

    own = jnp.concatenate([tokens, to_feed_order(w_out)])
    x_row, w_out_mine, x_last = row_gather(own, gates)
    moved = feed_weights([w_gate, w_up], (x_last,))

    qkv = matmul(x_row, w_heads)
    q_lin, k_lin = qkv[:, :own_width], qkv[:, own_width : 2 * own_width]
    squares = jnp.stack([jnp.sum(q_lin * q_lin, axis=1), jnp.sum(k_lin * k_lin, axis=1)])
    squares = seq_total(squares) / model_width
    factors = lax.rsqrt(squares + NORM_EPS).T
    q_factor, k_factor = factors[:, 0:1], factors[:, 1:2]
    tables = turn_tables(length)
    doc_ends = jnp.cumsum(doc_lengths[0])
    position = jnp.arange(length)
    doc_ids = jnp.sum((position[:, None] >= doc_ends[None, :]).astype(jnp.int32), axis=1)
    docs = (doc_ids[:, None], doc_ids[None, :])
    w_u = lax.all_gather(moved[1], REST, axis=0, tiled=True)
    sent_g = rest_send(tie(moved[0], squares))
    moved += feed_weights([w_down.T], (squares,))
    sent_d = rest_send(moved[2])
    *saved, attended = attend(qkv, factors, my_gq, my_gk, tables, docs, own_heads)

    corner_g = lax.ppermute(sent_g[1], "x", SWAP)
    att_tok = tie(attended.reshape(n_seq, tok_count, own_width), *sent_g)
    att_tok = exchange(att_tok, SEQ)
    corner_d = lax.ppermute(sent_d[1], "x", SWAP)
    att_tok = att_tok.transpose(1, 0, 2).reshape(tok_count, model_width)
    full_o = dp_gather(w_out_mine)
    branch = tie(matmul(att_tok, full_o), *sent_d)
    w_g = rest_gather(sent_g, corner_g, branch)
    w_d = rest_gather(sent_d, corner_d, branch)
    branch_norm, branch_factor = norm_apply(branch, gain_a)
    hidden = to_feed_order(tokens).astype(F32) + branch_norm
    hidden_low = hidden.astype(BF16)

    def feed_pass(own, saved, kernel, dtypes):
        held, total, rows = [], None, own
        for at in range(n_z):
            pair = (rows, core_swap(rows))
            if at < n_z - 1:
                rows = ring_send(rows)
            if at > 1:
                pair = tie(pair, total)
            *held, mine, away = feed_step(
                at, n_z, pair, (w_g, w_u, w_d), saved, held, kernel, dtypes
            )
            if at == 0:
                first = (mine, away)
            else:
                total = add_up(mine, away, total)
        return held, add_up(*first, total)

    def add_up(mine, away, total):
        mine = mine + core_swap(away).astype(F32)
        if total is not None:
            mine = mine + ring_send(total.astype(BF16)).astype(F32)
        return mine

    (hid, gate, upward, active), result = feed_pass(
        hidden_low, (), feed_kernel, (F32, F32, BF16)
    )
    result_norm, result_factor = norm_apply(result, gain_f)
    output = from_feed_order((hidden + result_norm).astype(BF16))

    grad_top = to_feed_order(cotangent[0]).astype(F32)
    grad_result, ffn_gain_term = norm_back(result, result_factor, gain_f, grad_top)
    def token_sum(left, right):
        return dot_left_t(left, right).astype(BF16)

    def rest_sum(term):
        return lax.psum_scatter(term, REST, scatter_dimension=0, tiled=True)

    def feed_home(term):
        return exchange(term.reshape(n_feed, own_rows, own_feed), FEED)

    def feed_rows(term):
        return term.transpose(1, 0, 2).reshape(own_rows, feed_width).astype(F32)

    def dp_sum(term):
        rows = term.shape[0] // n_dp

        def of(array_in, at):
            return lax.dynamic_slice_in_dim(array_in, at * rows, rows)

        def cores(at):
            return jnp.concatenate([of(term, x * n_core + at) for x in range(n_x)])

        away = core_swap(cores(1 - core_at))
        term = (cores(core_at).astype(F32) + away.astype(F32)).astype(BF16)
        away = lax.ppermute(of(term, 1 - x_at), "x", SWAP)
        return (of(term, x_at).astype(F32) + away.astype(F32)).astype(BF16)

    (g_res, g_gate, g_up), grad_ffn = feed_pass(
        grad_result.astype(BF16), (gate, upward), feed_back_kernel, (BF16, BF16)
    )
    grad_hidden = grad_top + grad_ffn
    term_d = token_sum(g_res, active)
    sum_d = rest_sum(term_d)
    term_g, term_u = token_sum(hid, g_gate), token_sum(hid, g_up)

    grad_branch, attn_gain_term = norm_back(branch, branch_factor, gain_a, grad_hidden)
    grad_branch = grad_branch.astype(BF16)
    grad_attended = dot_right_t(grad_branch, full_o).astype(BF16)
    g_att = grad_attended.reshape(tok_count, n_seq, own_width).transpose(1, 0, 2)
    g_att = exchange(g_att, SEQ).reshape(length, own_width)
    g_att = tie(g_att, term_g, term_u)
    sum_g, sum_u = rest_sum(term_g), rest_sum(term_u)

    grad_q, grad_k, grad_v, dot_q, dot_k = attend_back(
        saved, g_att, qkv, my_gq, my_gk, tables, docs, own_heads
    )
    dots = jnp.stack([jnp.sum(dot_q, axis=(0, 2)), jnp.sum(dot_k, axis=(0, 2))])
    branch_row = seq_gather(grad_branch)
    dots = seq_total(tie(dots, branch_row)) / model_width
    home_d = feed_home(tie(sum_d, dots))

    grad_w_out = dot_left_t(seq_order(attended), branch_row).astype(BF16)
    grad_w_out = dp_sum(grad_w_out)
    home = [(d * n_seq + s, s * n_dp + d) for d in range(n_dp) for s in range(n_seq)]
    grad_w_out = lax.ppermute(grad_w_out, ALL, home)
    grad_w_out = from_feed_order(grad_w_out).astype(F32)


    def lin_back(grad_in, lin, factor, gain_vec, mean_dot):
        gain_term = jnp.sum(grad_in * lin * factor, axis=0)
        grad_out = factor * (grad_in * gain_vec) - lin * (factor * factor * factor) * mean_dot
        return grad_out.astype(BF16), gain_term

    grad_q_lin, query_gain_term = lin_back(grad_q, q_lin, q_factor, my_gq, dots[0][:, None])
    grad_k_lin, key_gain_term = lin_back(grad_k, k_lin, k_factor, my_gk, dots[1][:, None])
    grad_lin = jnp.concatenate([grad_q_lin, grad_k_lin, grad_v], axis=1)

    def row_part(z_of):
        rows = lax.dynamic_slice_in_dim(grad_lin, z_of * n_y * tok_count, n_y * tok_count)
        return dot_right_t(rows, w_heads)

    grad_input = from_feed_order(grad_hidden) + seq_sum(row_part)

    grad_heads = dot_left_t(x_row, grad_lin).astype(BF16)
    grad_heads = dp_sum(grad_heads)
    home_g = feed_home(tie(sum_g, home_d))
    home_u = feed_home(tie(sum_u, home_g))
    grad_w_gate, grad_w_up = feed_rows(home_g), feed_rows(home_u)
    grad_w_down = feed_rows(home_d).T
    grad_heads = exchange(grad_heads.reshape(n_seq, own_rows, 3 * own_width), SEQ)
    grad_heads = grad_heads.reshape(n_seq, own_rows, 3, own_width).transpose(2, 1, 0, 3)
    grad_heads = grad_heads.reshape(3, own_rows, model_width).astype(F32)

    def place(term):
        return lax.dynamic_update_slice(
            jnp.zeros((model_width,), F32), term, (seq_at * own_width,)
        )

    gain_terms = jnp.stack(
        [
            place(query_gain_term),
            place(key_gain_term),
            from_feed_order(attn_gain_term),
            from_feed_order(ffn_gain_term),
        ]
    )
    gain_terms = gain_terms.reshape(4, n_all, own_rows).transpose(1, 0, 2)
    gain_grads = jnp.sum(exchange(gain_terms, ALL), axis=0)

    return (
        output[None],
        grad_input[None],
        grad_heads[0],
        grad_heads[1],
        grad_heads[2],
        grad_w_out,
        gain_grads[0],
        gain_grads[1],
        gain_grads[2],
        grad_w_gate,
        grad_w_up,
        grad_w_down,
        gain_grads[3],
    )


def plain_rotation(first_pos, tok_count):
    half_dim = HEAD_DIM // 2
    position = (first_pos + jnp.arange(tok_count)).astype(jnp.float32)
    inverse = jnp.exp(-(jnp.arange(half_dim).astype(jnp.float32) / half_dim) * math.log(ROPE_BASE))
    angles = position[:, None] * inverse[None, :]
    return (jnp.cos(angles)[None, :, None, :], jnp.sin(angles)[None, :, None, :])


def plain_rotate(array_in, cosine, sine_t, turn_sign):
    half_dim = array_in.shape[-1] // 2
    first_half = array_in[..., :half_dim]
    second_half = array_in[..., half_dim:]
    return jnp.concatenate(
        [
            first_half * cosine - turn_sign * second_half * sine_t,
            second_half * cosine + turn_sign * first_half * sine_t,
        ],
        axis=-1,
    )


def plain_body(
    inputs,
    doc_lengths,
    w_query,
    w_key,
    w_value,
    w_out,
    gain_query,
    gain_key,
    gain_attn,
    w_gate,
    w_up,
    w_down,
    gain_ffn,
    cotangent,
):
    row_count, tok_count, model_width = inputs.shape
    length = tok_count * lax.axis_size("seq")
    first_pos = lax.axis_index("seq") * tok_count
    score_scale = 1.0 / math.sqrt(HEAD_DIM)
    tokens = inputs.reshape(row_count * tok_count, model_width)

    def heads_first(array_in):
        return array_in.reshape(row_count, tok_count, HEADS, HEAD_DIM).transpose(2, 0, 1, 3)

    def heads_last(array_in):
        return array_in.transpose(1, 2, 0, 3).reshape(row_count * tok_count, HEADS * HEAD_DIM)

    full_q, full_k, full_v, full_o, full_gq, full_gk, full_ga = (
        lax.all_gather(w_query, ("dp", "seq"), axis=0, tiled=True),
        lax.all_gather(w_key, ("dp", "seq"), axis=0, tiled=True),
        lax.all_gather(w_value, ("dp", "seq"), axis=0, tiled=True),
        lax.all_gather(w_out, ("dp", "seq"), axis=0, tiled=True),
        lax.all_gather(gain_query, ("dp", "seq"), axis=0, tiled=True),
        lax.all_gather(gain_key, ("dp", "seq"), axis=0, tiled=True),
        lax.all_gather(gain_attn, ("dp", "seq"), axis=0, tiled=True),
    )
    cosine, sine_t = plain_rotation(first_pos, tok_count)
    q_lin = matmul(tokens, full_q)
    k_lin = matmul(tokens, full_k)
    v_lin = matmul(tokens, full_v)
    q_norm, q_factor = norm_apply(q_lin, full_gq.astype(jnp.float32))
    k_norm, k_factor = norm_apply(k_lin, full_gk.astype(jnp.float32))
    queries = (
        plain_rotate(q_norm.reshape(row_count, tok_count, HEADS, HEAD_DIM), cosine, sine_t, 1.0)
        .astype(jnp.bfloat16)
        .transpose(2, 0, 1, 3)
    )
    keys_mine = (
        plain_rotate(k_norm.reshape(row_count, tok_count, HEADS, HEAD_DIM), cosine, sine_t, 1.0)
        .astype(jnp.bfloat16)
        .transpose(2, 0, 1, 3)
    )
    values_mine = heads_first(v_lin.astype(jnp.bfloat16))
    keys_all, values_all = (
        lax.all_gather(keys_mine, "seq", axis=2, tiled=True),
        lax.all_gather(values_mine, "seq", axis=2, tiled=True),
    )
    doc_ends = jnp.cumsum(doc_lengths, axis=1)
    position = jnp.arange(length)
    doc_ids = jnp.sum((position[None, :, None] >= doc_ends[:, None, :]).astype(jnp.int32), axis=2)
    my_pos = first_pos + jnp.arange(tok_count)
    docs_mine = lax.dynamic_slice_in_dim(doc_ids, first_pos, tok_count, 1)
    allowed = (position[None, None, :] <= my_pos[None, :, None]) & (
        doc_ids[:, None, :] == docs_mine[:, :, None]
    )

    def scores_of(q_head, k_head):
        raw_scores = (
            jnp.einsum("rtd,rkd->rtk", q_head, k_head, preferred_element_type=jnp.float32)
            * score_scale
        )
        return jnp.where(allowed, raw_scores, MASK_FILL)

    def attend(head_item):
        q_head, k_head, v_head = head_item
        scores = scores_of(q_head, k_head)
        row_max = jnp.max(scores, axis=-1, keepdims=True)
        row_total = row_max + jnp.log(jnp.sum(jnp.exp(scores - row_max), axis=-1, keepdims=True))
        attn_probs = jnp.exp(scores - row_total).astype(jnp.bfloat16)
        head_out = jnp.einsum(
            "rtk,rkd->rtd", attn_probs, v_head, preferred_element_type=jnp.float32
        )
        return (head_out, row_total[..., 0])

    attn_mixed, totals = lax.map(attend, (queries, keys_all, values_all))
    attended = heads_last(attn_mixed.astype(jnp.bfloat16))
    branch = matmul(attended, full_o)
    branch_norm, branch_factor = norm_apply(branch, full_ga.astype(jnp.float32))
    hidden = tokens.astype(jnp.float32) + branch_norm
    hidden_low = hidden.astype(jnp.bfloat16)
    gate_full, up_full, down_full, ffn_gain_full = (
        lax.all_gather(w_gate, ("dp", "seq"), axis=0, tiled=True),
        lax.all_gather(w_up, ("dp", "seq"), axis=0, tiled=True),
        lax.all_gather(w_down, ("dp", "seq"), axis=1, tiled=True),
        lax.all_gather(gain_ffn, ("dp", "seq"), axis=0, tiled=True),
    )
    gate_act = matmul(hidden_low, gate_full)
    upward = matmul(hidden_low, up_full)
    gate_sig = jax.nn.sigmoid(gate_act)
    active = (gate_act * gate_sig * upward).astype(jnp.bfloat16)
    result = matmul(active, down_full)
    result_norm, result_factor = norm_apply(result, ffn_gain_full.astype(jnp.float32))
    output = (hidden + result_norm).astype(jnp.bfloat16).reshape(row_count, tok_count, model_width)
    grad_top = cotangent.reshape(row_count * tok_count, model_width).astype(jnp.float32)
    grad_result, ffn_gain_term = norm_back(
        result, result_factor, ffn_gain_full.astype(jnp.float32), grad_top
    )
    grad_result = grad_result.astype(jnp.bfloat16)
    grad_active = dot_right_t(grad_result, down_full)
    grad_gate = (grad_active * upward * gate_sig * (1.0 + gate_act * (1.0 - gate_sig))).astype(
        jnp.bfloat16
    )
    grad_up = (grad_active * gate_act * gate_sig).astype(jnp.bfloat16)
    grad_hidden = grad_top + dot_right_t(grad_gate, gate_full) + dot_right_t(grad_up, up_full)
    feedforward_grads = lax.psum_scatter(
        jnp.concatenate(
            [
                dot_left_t(hidden_low, grad_gate),
                dot_left_t(hidden_low, grad_up),
                dot_left_t(grad_result, active),
            ],
            axis=1,
        ),
        ("dp", "seq"),
        scatter_dimension=0,
        tiled=True,
    )
    grad_branch, attn_gain_term = norm_back(
        branch, branch_factor, full_ga.astype(jnp.float32), grad_hidden
    )
    grad_branch = grad_branch.astype(jnp.bfloat16)
    back_q, back_k, back_v, back_o, back_gq, back_gk = (
        lax.all_gather(w_query, ("dp", "seq"), axis=0, tiled=True),
        lax.all_gather(w_key, ("dp", "seq"), axis=0, tiled=True),
        lax.all_gather(w_value, ("dp", "seq"), axis=0, tiled=True),
        lax.all_gather(w_out, ("dp", "seq"), axis=0, tiled=True),
        lax.all_gather(gain_query, ("dp", "seq"), axis=0, tiled=True),
        lax.all_gather(gain_key, ("dp", "seq"), axis=0, tiled=True),
    )
    grad_attended = dot_right_t(grad_branch, back_o).astype(jnp.bfloat16)
    grad_w_out_term = dot_left_t(attended, grad_branch)
    grad_mixed = heads_first(grad_attended)

    def head_back(head_item):
        q_head, k_head, v_head, g_head, t_head = head_item
        prob_full = jnp.exp(scores_of(q_head, k_head) - t_head[..., None])
        grad_probs = jnp.einsum("rtd,rkd->rtk", g_head, v_head, preferred_element_type=jnp.float32)
        offsets = jnp.sum(prob_full * grad_probs, axis=-1, keepdims=True)
        grad_scores = (prob_full * (grad_probs - offsets)).astype(jnp.bfloat16)
        grad_q = (
            jnp.einsum("rtk,rkd->rtd", grad_scores, k_head, preferred_element_type=jnp.float32)
            * score_scale
        )
        grad_k = (
            jnp.einsum("rtk,rtd->rkd", grad_scores, q_head, preferred_element_type=jnp.float32)
            * score_scale
        )
        grad_v = jnp.einsum(
            "rtk,rtd->rkd",
            prob_full.astype(jnp.bfloat16),
            g_head,
            preferred_element_type=jnp.float32,
        )
        return (grad_q, grad_k, grad_v)

    grad_queries, key_terms, value_terms = lax.map(
        head_back, (queries, keys_all, values_all, grad_mixed, totals)
    )
    grad_keys, grad_values = (
        lax.psum_scatter(
            key_terms.astype(jnp.bfloat16), "seq", scatter_dimension=2, tiled=True
        ).astype(jnp.float32),
        lax.psum_scatter(
            value_terms.astype(jnp.bfloat16), "seq", scatter_dimension=2, tiled=True
        ).astype(jnp.float32),
    )
    grad_q_norm = plain_rotate(grad_queries.transpose(1, 2, 0, 3), cosine, sine_t, -1.0).reshape(
        row_count * tok_count, model_width
    )
    grad_k_norm = plain_rotate(grad_keys.transpose(1, 2, 0, 3), cosine, sine_t, -1.0).reshape(
        row_count * tok_count, model_width
    )
    grad_q_lin, query_gain_term = norm_back(
        q_lin, q_factor, back_gq.astype(jnp.float32), grad_q_norm
    )
    grad_k_lin, key_gain_term = norm_back(k_lin, k_factor, back_gk.astype(jnp.float32), grad_k_norm)
    grad_q_lin = grad_q_lin.astype(jnp.bfloat16)
    grad_k_lin = grad_k_lin.astype(jnp.bfloat16)
    grad_v_lin = heads_last(grad_values).astype(jnp.bfloat16)
    grad_input = (
        grad_hidden
        + dot_right_t(grad_q_lin, back_q)
        + dot_right_t(grad_k_lin, back_k)
        + dot_right_t(grad_v_lin, back_v)
    )
    attention_grads = (
        lax.psum_scatter(
            dot_left_t(tokens, grad_q_lin), ("dp", "seq"), scatter_dimension=0, tiled=True
        ),
        lax.psum_scatter(
            dot_left_t(tokens, grad_k_lin), ("dp", "seq"), scatter_dimension=0, tiled=True
        ),
        lax.psum_scatter(
            dot_left_t(tokens, grad_v_lin), ("dp", "seq"), scatter_dimension=0, tiled=True
        ),
        lax.psum_scatter(grad_w_out_term, ("dp", "seq"), scatter_dimension=0, tiled=True),
        lax.psum_scatter(query_gain_term, ("dp", "seq"), scatter_dimension=0, tiled=True),
        lax.psum_scatter(key_gain_term, ("dp", "seq"), scatter_dimension=0, tiled=True),
        lax.psum_scatter(attn_gain_term, ("dp", "seq"), scatter_dimension=0, tiled=True),
        lax.psum_scatter(ffn_gain_term, ("dp", "seq"), scatter_dimension=0, tiled=True),
    )
    feed_width = w_gate.shape[1]
    grad_w_gate = feedforward_grads[:, :feed_width]
    grad_w_up = feedforward_grads[:, feed_width : 2 * feed_width]
    grad_w_down = feedforward_grads[:, 2 * feed_width :].T
    return (
        output,
        grad_input.reshape(row_count, tok_count, model_width),
        attention_grads[0],
        attention_grads[1],
        attention_grads[2],
        attention_grads[3],
        attention_grads[4],
        attention_grads[5],
        attention_grads[6],
        grad_w_gate,
        grad_w_up,
        grad_w_down,
        attention_grads[7],
    )


def solution(mesh):
    n_dp, n_seq = mesh.shape["dp"], mesh.shape["seq"]
    if n_dp == 4 and n_seq % 2 == 0 and HEADS % n_seq == 0:
        grid = Mesh(mesh.devices.reshape(n_dp // 2, 2, n_seq // 2, 2), ALL)
        layer, dp, seq = body, DP, SEQ
    else:
        grid, layer, dp, seq = mesh, plain_body, ("dp",), ("seq",)
    rows = P(dp, seq, None)
    split = P(dp + seq, None)
    vector = P(dp + seq)
    down = P(None, dp + seq)
    return jax.shard_map(
        layer,
        mesh=grid,
        in_specs=(rows, P(dp, None))
        + (split,) * 4
        + (vector,) * 3
        + (split, split, down, vector, rows),
        out_specs=(rows, rows) + (split,) * 4 + (vector,) * 3 + (split, split, down, vector),
        check_vma=False,
    )
```

```python
import math

import jax
import jax.numpy as jnp
from jax import lax
from jax.experimental import pallas as pl
from jax.experimental.pallas import tpu as pltpu
from jax.sharding import Mesh
from jax.sharding import PartitionSpec as P

HEADS = 16
HEAD_DIM = 128


NORM_EPS = 1e-06
ROPE_BASE = 500000.0
MASK_FILL = -1e30

SEQ = ("z", "y")
DP = ("x", "core")
FEED = ("z", "core")
REST = ("x", "y")
ALL = ("x", "core", "z", "y")
SWAP = [(0, 1), (1, 0)]
F32 = jnp.float32
BF16 = jnp.bfloat16


def matmul(left_mat, right_mat):
    return jnp.dot(left_mat, right_mat, preferred_element_type=F32)


def dot_right_t(left_mat, right_mat):
    return lax.dot_general(
        left_mat, right_mat, (((1,), (1,)), ((), ())), preferred_element_type=F32
    )


def dot_left_t(left_mat, right_mat):
    return lax.dot_general(
        left_mat, right_mat, (((0,), (0,)), ((), ())), preferred_element_type=F32
    )


def norm_apply(array_in, gain_vec):
    factor = lax.rsqrt(jnp.mean(array_in * array_in, axis=-1, keepdims=True) + NORM_EPS)
    return (array_in * factor * gain_vec, factor)


def norm_back(array_in, factor, gain_vec, grad_in):
    gain_term = jnp.sum(grad_in * array_in * factor, axis=0)
    scaled = grad_in * gain_vec
    grad_out = factor * scaled - array_in * (factor * factor * factor) * jnp.mean(
        scaled * array_in, axis=-1, keepdims=True
    )
    return (grad_out, gain_term)


def turn_tables(tok_count):
    half_dim = HEAD_DIM // 2
    position = jnp.arange(tok_count).astype(F32)
    inverse = jnp.exp(-(jnp.arange(half_dim).astype(F32) / half_dim) * math.log(ROPE_BASE))
    angles = position[:, None] * inverse[None, :]
    cosine, sine_t = jnp.cos(angles), jnp.sin(angles)
    return (
        jnp.concatenate([cosine, cosine], axis=1),
        jnp.concatenate([-sine_t, sine_t], axis=1),
    )


def rotate(array_in, cosine, sine_t):
    return array_in * cosine + pltpu.roll(array_in, HEAD_DIM // 2, 1) * sine_t


def rotate_back(array_in, cosine, sine_t):
    return array_in * cosine - pltpu.roll(array_in, HEAD_DIM // 2, 1) * sine_t


def exchange(array_in, axes):
    return lax.all_to_all(array_in, axes, split_axis=0, concat_axis=0, tiled=True)


def spread(array_in, axes):
    count = lax.axis_size(axes)
    return exchange(jnp.broadcast_to(array_in[None], (count,) + array_in.shape), axes)


def tie(value, *earlier):
    return lax.optimization_barrier((value,) + earlier)[0]


def ring_order(count):
    return [0] + list(range(1, count, 2)) + [v for v in range(count - 1, 0, -1) if v % 2 == 0]


def core_swap(array_in):
    return lax.ppermute(array_in, "core", SWAP)


def pick(array_in, at, axis=0):
    return lax.dynamic_index_in_dim(array_in, at, axis, keepdims=False)


def visible(doc_col, doc_row, first, rows, width):
    at = first + lax.broadcasted_iota(jnp.int32, (rows, width), 0)
    of = lax.broadcasted_iota(jnp.int32, (rows, width), 1)
    return (of <= at) & (doc_col == doc_row)


def attend_kernel(
    step,
    q_lin,
    k_lin,
    v_lin,
    factors,
    gain_q,
    gain_k,
    cosine,
    sine_t,
    doc_col,
    doc_row,
    queries,
    keys,
    values,
    totals,
    attended,
):
    cos, sin = cosine[...], sine_t[...]
    queries[...] = rotate(q_lin[...] * factors[:, 0:1] * gain_q[...], cos, sin).astype(BF16)
    keys[...] = rotate(k_lin[...] * factors[:, 1:2] * gain_k[...], cos, sin).astype(BF16)
    values[...] = v_lin[...].astype(BF16)
    scale = 1.0 / math.sqrt(HEAD_DIM)
    for first in range(0, queries.shape[0], step):
        width = first + step
        mine = pl.ds(first, step)
        scores = dot_right_t(queries[mine, :], keys[0:width, :]) * scale
        seen = visible(doc_col[mine, :], doc_row[:, 0:width], first, step, width)
        scores = jnp.where(seen, scores, MASK_FILL)
        row_max = jnp.max(scores, axis=1, keepdims=True)
        row_sum = jnp.sum(jnp.exp(scores - row_max), axis=1, keepdims=True)
        total = row_max + jnp.log(row_sum)
        probs = jnp.exp(scores - total).astype(BF16)
        totals[0, mine, :] = total
        attended[mine, :] = matmul(probs, values[0:width, :]).astype(BF16)


def attend_back_kernel(
    step,
    queries,
    keys,
    values,
    totals,
    g_att,
    q_lin,
    k_lin,
    gain_q,
    gain_k,
    cosine,
    sine_t,
    doc_col,
    doc_row,
    grad_q,
    grad_k,
    grad_v,
    dot_q,
    dot_k,
    k_sum,
    v_sum,
):
    scale = 1.0 / math.sqrt(HEAD_DIM)
    k_sum[...] = jnp.zeros_like(k_sum)
    v_sum[...] = jnp.zeros_like(v_sum)
    for first in range(0, queries.shape[0], step):
        width = first + step
        mine, upto = pl.ds(first, step), pl.ds(0, width)
        scores = dot_right_t(queries[mine, :], keys[upto, :]) * scale
        seen = visible(doc_col[mine, :], doc_row[:, 0:width], first, step, width)
        scores = jnp.where(seen, scores, MASK_FILL)
        prob_full = jnp.exp(scores - totals[0, mine, :])
        grad_probs = dot_right_t(g_att[mine, :], values[upto, :])
        offsets = jnp.sum(prob_full * grad_probs, axis=1, keepdims=True)
        grad_scores = (prob_full * (grad_probs - offsets)).astype(BF16)
        back = matmul(grad_scores, keys[upto, :]) * scale
        back = rotate_back(back, cosine[mine, :], sine_t[mine, :])
        grad_q[mine, :] = back
        dot_q[0, mine, :] = jnp.sum(back * gain_q[...] * q_lin[mine, :], axis=1, keepdims=True)
        k_sum[upto, :] += dot_left_t(grad_scores, queries[mine, :])
        v_sum[upto, :] += dot_left_t(prob_full.astype(BF16), g_att[mine, :])
    back = rotate_back(k_sum[...] * scale, cosine[...], sine_t[...])
    grad_k[...] = back
    dot_k[0] = jnp.sum(back * gain_k[...] * k_lin[...], axis=1, keepdims=True)
    grad_v[...] = v_sum[...].astype(BF16)


def head_specs(length, heads):
    def part(offset):
        return pl.BlockSpec((length, HEAD_DIM), lambda h: (0, h + offset))

    def gain():
        return pl.BlockSpec((1, HEAD_DIM), lambda h: (0, h))

    def whole(shape):
        return pl.BlockSpec(shape, lambda h: (0, 0))

    each = pl.BlockSpec((1, length, 1), lambda h: (h, 0, 0))
    table = whole((length, HEAD_DIM))
    docs = [whole((length, 1)), whole((1, length))]
    return part, gain, whole, each, table, docs


def attend(qkv, factors, gain_q, gain_k, tables, docs, heads):
    length = qkv.shape[0]
    part, gain, whole, each, table, doc_specs = head_specs(length, heads)
    low = jax.ShapeDtypeStruct((length, heads * HEAD_DIM), BF16)
    step = min(256, length)
    pairs = heads * length * length * HEAD_DIM
    return pl.pallas_call(
        lambda *refs: attend_kernel(step, *refs),
        grid=(heads,),
        in_specs=[part(0), part(heads), part(2 * heads), whole((length, 2)), gain(), gain()]
        + [table, table]
        + doc_specs,
        out_specs=[part(0), part(0), part(0), each, part(0)],
        out_shape=[low, low, low, jax.ShapeDtypeStruct((heads, length, 1), F32), low],
        compiler_params=pltpu.CompilerParams(vmem_limit_bytes=24 * 1024 * 1024),
        cost_estimate=pl.CostEstimate(
            flops=3 * pairs, bytes_accessed=qkv.size * 6, transcendentals=heads * length * length
        ),
    )(qkv, qkv, qkv, factors, gain_q, gain_k, *tables, *docs)


def attend_back(saved, g_att, qkv, gain_q, gain_k, tables, docs, heads):
    queries, keys, values, totals = saved
    length = qkv.shape[0]
    part, gain, whole, each, table, doc_specs = head_specs(length, heads)
    flat = jax.ShapeDtypeStruct((length, heads * HEAD_DIM), F32)
    low = jax.ShapeDtypeStruct((length, heads * HEAD_DIM), BF16)
    line = jax.ShapeDtypeStruct((heads, length, 1), F32)
    step = min(256, length)
    pairs = heads * length * length * HEAD_DIM
    return pl.pallas_call(
        lambda *refs: attend_back_kernel(step, *refs),
        grid=(heads,),
        in_specs=[part(0), part(0), part(0), each, part(0), part(0), part(heads), gain(), gain()]
        + [table, table]
        + doc_specs,
        out_specs=[part(0), part(0), part(0), each, each],
        out_shape=[flat, flat, low, line, line],
        scratch_shapes=[pltpu.VMEM((length, HEAD_DIM), F32)] * 2,
        compiler_params=pltpu.CompilerParams(vmem_limit_bytes=24 * 1024 * 1024),
        cost_estimate=pl.CostEstimate(
            flops=7 * pairs, bytes_accessed=qkv.size * 8, transcendentals=heads * length * length
        ),
    )(queries, keys, values, totals, g_att, qkv, qkv, gain_q, gain_k, *tables, *docs)


def feed_kernel(part, other, w_g, w_u, w_d, *refs):
    hid, gate, upward, active, mine, away, total = refs[-7:]
    block, tokens = pl.program_id(0), part.shape[0]

    @pl.when(block == 0)
    def _():
        hid[:tokens, :] = part[...]
        hid[tokens:, :] = other[...]

    g = matmul(hid[...], w_g[...])
    u = matmul(hid[...], w_u[...])
    a = (g * (1.0 / (1.0 + jnp.exp(-g))) * u).astype(BF16)
    gate[...], upward[...], active[...] = g, u, a
    term = dot_right_t(a, w_d[...])

    @pl.when(block == 0)
    def _():
        total[...] = term

    @pl.when(block > 0)
    def _():
        total[...] += term

    @pl.when(block == pl.num_programs(0) - 1)
    def _():
        mine[...] = total[:tokens, :]
        away[...] = total[tokens:, :].astype(BF16)


def feed_back_kernel(part, other, w_g, w_u, w_d, gate, upward, *refs):
    g_res, g_gate, g_up, mine, away, total = refs[-6:]
    block, tokens = pl.program_id(0), part.shape[0]

    @pl.when(block == 0)
    def _():
        g_res[:tokens, :] = part[...]
        g_res[tokens:, :] = other[...]

    a = matmul(g_res[...], w_d[...])
    g, u = gate[...], upward[...]
    s = 1.0 / (1.0 + jnp.exp(-g))
    gg = (a * u * s * (1.0 + g * (1.0 - s))).astype(BF16)
    gu = (a * g * s).astype(BF16)
    g_gate[...], g_up[...] = gg, gu
    term = dot_right_t(gg, w_g[...]) + dot_right_t(gu, w_u[...])

    @pl.when(block == 0)
    def _():
        total[...] = term

    @pl.when(block > 0)
    def _():
        total[...] += term

    @pl.when(block == pl.num_programs(0) - 1)
    def _():
        mine[...] = total[:tokens, :]
        away[...] = total[tokens:, :].astype(BF16)


def feed_step(at, count, pair, weights, saved, held, kernel, dtypes):
    tokens, width = pair[0].shape
    feed = weights[0].shape[1]
    step = min(512, feed)
    rows = 2 * tokens
    block = pl.BlockSpec((rows, step), lambda f: (at, f))
    part = pl.BlockSpec((tokens, width), lambda f: (0, 0))
    full = pl.BlockSpec((rows, width), lambda f: (at, 0))
    n_in = 5 + len(saved)
    shapes = [jax.ShapeDtypeStruct((count * rows, width), BF16)]
    shapes += [jax.ShapeDtypeStruct((count * rows, feed), d) for d in dtypes]
    tail = [jax.ShapeDtypeStruct((tokens, width), d) for d in (F32, BF16)]
    flops = 6 * rows * width * feed
    return pl.pallas_call(
        kernel,
        grid=(feed // step,),
        in_specs=[part, part]
        + [pl.BlockSpec((width, step), lambda f: (0, f))] * 3
        + [block] * len(saved)
        + [pl.BlockSpec(memory_space=pl.ANY)] * len(held),
        out_specs=[full] + [block] * len(dtypes) + [part, part],
        out_shape=shapes + tail,
        scratch_shapes=[pltpu.VMEM((rows, width), F32)],
        input_output_aliases={n_in + k: k for k in range(len(held))},
        compiler_params=pltpu.CompilerParams(vmem_limit_bytes=32 * 1024 * 1024),
        cost_estimate=pl.CostEstimate(
            flops=flops, bytes_accessed=6 * width * feed, transcendentals=rows * feed
        ),
    )(*pair, *weights, *saved, *held)


def body(
    inputs,
    doc_lengths,
    w_query,
    w_key,
    w_value,
    w_out,
    gain_query,
    gain_key,
    gain_attn,
    w_gate,
    w_up,
    w_down,
    gain_ffn,
    cotangent,
):
    _, tok_count, model_width = inputs.shape
    n_x, n_core, n_z, n_y = (lax.axis_size(a) for a in ALL)
    n_seq, n_dp, n_all = n_z * n_y, n_x * n_core, n_x * n_core * n_z * n_y
    seq_at = lax.axis_index(SEQ)
    length = tok_count * n_seq
    score_scale = 1.0 / math.sqrt(HEAD_DIM)
    own_rows = w_query.shape[0]
    own_width = model_width // n_seq
    own_heads = own_width // HEAD_DIM
    feed_width = w_gate.shape[1]
    n_feed = n_core * n_z
    own_feed = feed_width // n_feed
    x_at, core_at, z_at, y_at = (lax.axis_index(a) for a in ALL)
    order = ring_order(n_z)
    ring = [(order[i], order[(i + 1) % n_z]) for i in range(n_z)]
    behind = jnp.array(
        [[order[(order.index(z) - s) % n_z] for z in range(n_z)] for s in range(n_z)], jnp.int32
    )
    tokens = inputs[0]

    def ring_send(part):
        return lax.ppermute(part, "z", ring)

    def seq_gather(own):
        chunks, held = [], own
        for step in range(n_z):
            chunks += [held, lax.ppermute(held, "y", SWAP)]
            if step < n_z - 1:
                held = ring_send(held)
        return jnp.concatenate(chunks, axis=0)

    def row_gather(own, gates):
        chunks, held = [], own
        for step in range(n_z):
            chunks.append((held, lax.ppermute(held, "y", SWAP)))
            if step < n_z - 1:
                held = ring_send(tie(held, *gates(step, held)))

        def whole(first, count):
            out = jnp.zeros((n_seq * count, own.shape[1]), own.dtype)
            for step, pair in enumerate(chunks):
                for at_y, part in zip((y_at, 1 - y_at), pair):
                    at = (behind[step, z_at] * n_y + at_y) * count
                    part = part[first : first + count]
                    out = lax.dynamic_update_slice(out, part, (at, 0))
            return out

        return whole(0, tok_count), whole(tok_count, own.shape[0] - tok_count), held

    def dp_gather(mine):
        out = jnp.zeros((n_x, n_core) + mine.shape, mine.dtype)
        for at_x, part in ((x_at, mine), (1 - x_at, lax.ppermute(mine, "x", SWAP))):
            for at_core, block in ((core_at, part), (1 - core_at, core_swap(part))):
                block = block[None, None]
                out = lax.dynamic_update_slice(out, block, (at_x, at_core, 0, 0))
        return out.reshape((n_dp * mine.shape[0], mine.shape[1]))

    def seq_order(array_in):
        chunks = []
        for step in range(n_z):
            for at_y in (y_at, 1 - y_at):
                first = (behind[step, z_at] * n_y + at_y) * tok_count
                chunks.append(lax.dynamic_slice_in_dim(array_in, first, tok_count))
        return jnp.concatenate(chunks, axis=0)

    def seq_sum(part_of, *last):
        total = None
        for step in list(range(1, n_z)) + [0]:
            part = part_of(behind[step, z_at], *(() if step else last))
            part = part.reshape(n_y, tok_count, model_width)
            away = lax.ppermute(pick(part, 1 - y_at).astype(BF16), "y", SWAP)
            mine = pick(part, y_at) + away.astype(F32)
            if total is not None:
                mine = mine + ring_send(total.astype(BF16)).astype(F32)
            total = mine
        return total

    def feed_weights(mats, earlier):
        blocks = jnp.stack(mats).reshape(len(mats), own_rows, n_feed, own_feed)
        mine = exchange(tie(blocks.transpose(2, 0, 1, 3), *earlier), FEED)
        return [mine[:, at].reshape(n_feed * own_rows, own_feed) for at in range(len(mats))]

    def rest_send(mine):
        return mine, lax.ppermute(mine, "y", SWAP), lax.ppermute(mine, "x", SWAP)

    def rest_gather(sent, corner, later):
        mine, over_y, over_x = sent
        mine = tie(mine, later)
        whole = jnp.zeros((n_x, n_y) + mine.shape, BF16)
        for at_x, at_y, part in (
            (x_at, y_at, mine),
            (1 - x_at, y_at, over_x),
            (x_at, 1 - y_at, over_y),
            (1 - x_at, 1 - y_at, corner),
        ):
            whole = lax.dynamic_update_slice(whole, part[None, None], (at_x, at_y, 0, 0))
        return whole.reshape(model_width, own_feed)

    def seq_total(term):
        return jnp.sum(spread(term, SEQ), axis=0)

    def to_feed_order(array_in):
        lead = array_in.shape[:-1]
        parts = array_in.reshape((-1, n_x, n_core, n_z, n_y, own_rows))
        return parts.transpose(0, 1, 4, 3, 2, 5).reshape(lead + (model_width,))

    def from_feed_order(array_in):
        lead = array_in.shape[:-1]
        parts = array_in.reshape((-1, n_x, n_y, n_z, n_core, own_rows))
        return parts.transpose(0, 1, 4, 3, 2, 5).reshape(lead + (model_width,))

    gains = spread(jnp.stack([gain_query, gain_key, gain_attn, gain_ffn]), ALL)
    gains = gains.transpose(1, 0, 2).reshape(4, model_width).astype(F32)
    my_gq = lax.dynamic_slice_in_dim(gains[0:1], seq_at * own_width, own_width, 1)
    my_gk = lax.dynamic_slice_in_dim(gains[1:2], seq_at * own_width, own_width, 1)
    gain_a, gain_f = to_feed_order(gains[2]), to_feed_order(gains[3])

    w_heads = jnp.stack([w_query, w_key, w_value])
    w_heads = w_heads.reshape(3, own_rows, n_seq, own_width).transpose(2, 1, 0, 3)
    w_heads = w_heads.reshape(n_seq, own_rows, 3 * own_width)
    w_heads = exchange(tie(w_heads, gains), SEQ)
    w_mine = w_heads.reshape(n_seq * own_rows, 3 * own_width)

    w_heads = dp_gather(w_mine)
    def gates(step, held):
        return (w_mine,) if step == 1 else ()

    own = jnp.concatenate([tokens, to_feed_order(w_out)])
    x_row, w_out_mine, x_last = row_gather(own, gates)
    moved = feed_weights([w_gate, w_up], (x_last,))

    qkv = matmul(x_row, w_heads)
    q_lin, k_lin = qkv[:, :own_width], qkv[:, own_width : 2 * own_width]
    squares = jnp.stack([jnp.sum(q_lin * q_lin, axis=1), jnp.sum(k_lin * k_lin, axis=1)])
    squares = seq_total(squares) / model_width
    factors = lax.rsqrt(squares + NORM_EPS).T
    q_factor, k_factor = factors[:, 0:1], factors[:, 1:2]
    tables = turn_tables(length)
    doc_ends = jnp.cumsum(doc_lengths[0])
    position = jnp.arange(length)
    doc_ids = jnp.sum((position[:, None] >= doc_ends[None, :]).astype(jnp.int32), axis=1)
    docs = (doc_ids[:, None], doc_ids[None, :])
    w_u = lax.all_gather(moved[1], REST, axis=0, tiled=True)
    sent_g = rest_send(tie(moved[0], squares))
    moved += feed_weights([w_down.T], (squares,))
    sent_d = rest_send(moved[2])
    *saved, attended = attend(qkv, factors, my_gq, my_gk, tables, docs, own_heads)

    corner_g = lax.ppermute(sent_g[1], "x", SWAP)
    att_tok = tie(attended.reshape(n_seq, tok_count, own_width), *sent_g)
    att_tok = exchange(att_tok, SEQ)
    corner_d = lax.ppermute(sent_d[2], "y", SWAP)
    att_tok = att_tok.transpose(1, 0, 2).reshape(tok_count, model_width)
    full_o = dp_gather(w_out_mine)
    branch = matmul(att_tok, full_o)
    w_g = rest_gather(sent_g, corner_g, branch)
    w_d = rest_gather(sent_d, corner_d, branch)
    branch_norm, branch_factor = norm_apply(branch, gain_a)
    hidden = to_feed_order(tokens).astype(F32) + branch_norm
    hidden_low = hidden.astype(BF16)

    def feed_pass(own, saved, kernel, dtypes, gate=()):
        held, total, rows = [], None, own
        for at in range(n_z):
            pair = (rows, core_swap(rows))
            if at < n_z - 1:
                rows = ring_send(tie(rows, *gate) if gate and at == 1 else rows)
            if at > 1:
                pair = tie(pair, total)
            *held, mine, away = feed_step(
                at, n_z, pair, (w_g, w_u, w_d), saved, held, kernel, dtypes
            )
            if at == 0:
                first = (mine, away)
            else:
                total = add_up(mine, away, total)
        return held, add_up(*first, total)

    def add_up(mine, away, total):
        mine = mine + core_swap(away).astype(F32)
        if total is not None:
            mine = mine + ring_send(total.astype(BF16)).astype(F32)
        return mine

    (hid, gate, upward, active), result = feed_pass(
        hidden_low, (), feed_kernel, (F32, F32, BF16), sent_d
    )
    result_norm, result_factor = norm_apply(result, gain_f)
    output = from_feed_order((hidden + result_norm).astype(BF16))

    grad_top = to_feed_order(cotangent[0]).astype(F32)
    grad_result, ffn_gain_term = norm_back(result, result_factor, gain_f, grad_top)
    def token_sum(left, right):
        return dot_left_t(left, right).astype(BF16)

    def rest_sum(term):
        return lax.psum_scatter(term, REST, scatter_dimension=0, tiled=True)

    def feed_home(term):
        return exchange(term.reshape(n_feed, own_rows, own_feed), FEED)

    def feed_rows(term):
        return term.transpose(1, 0, 2).reshape(own_rows, feed_width).astype(F32)

    def dp_sum(term):
        rows = term.shape[0] // n_dp

        def of(array_in, at):
            return lax.dynamic_slice_in_dim(array_in, at * rows, rows)

        def cores(at):
            return jnp.concatenate([of(term, x * n_core + at) for x in range(n_x)])

        away = core_swap(cores(1 - core_at))
        term = (cores(core_at).astype(F32) + away.astype(F32)).astype(BF16)
        away = lax.ppermute(of(term, 1 - x_at), "x", SWAP)
        return (of(term, x_at).astype(F32) + away.astype(F32)).astype(BF16)

    (g_res, g_gate, g_up), grad_ffn = feed_pass(
        grad_result.astype(BF16), (gate, upward), feed_back_kernel, (BF16, BF16)
    )
    grad_hidden = grad_top + grad_ffn
    term_d = token_sum(g_res, active)
    sum_d = rest_sum(term_d)
    term_g, term_u = token_sum(hid, g_gate), token_sum(hid, g_up)

    grad_branch, attn_gain_term = norm_back(branch, branch_factor, gain_a, grad_hidden)
    grad_branch = grad_branch.astype(BF16)
    grad_attended = dot_right_t(grad_branch, full_o).astype(BF16)
    g_att = grad_attended.reshape(tok_count, n_seq, own_width).transpose(1, 0, 2)
    g_att = exchange(g_att, SEQ).reshape(length, own_width)
    g_att = tie(g_att, term_g, term_u)
    sum_g, sum_u = rest_sum(term_g), rest_sum(term_u)

    grad_q, grad_k, grad_v, dot_q, dot_k = attend_back(
        saved, g_att, qkv, my_gq, my_gk, tables, docs, own_heads
    )
    dots = jnp.stack([jnp.sum(dot_q, axis=(0, 2)), jnp.sum(dot_k, axis=(0, 2))])
    branch_row = seq_gather(from_feed_order(tie(grad_branch, grad_attended)))
    hidden_back, ffn_gain_term, attn_gain_term = [
        from_feed_order(tie(a, grad_attended))
        for a in (grad_hidden, ffn_gain_term, attn_gain_term)
    ]
    early = (branch_row, hidden_back, ffn_gain_term, attn_gain_term)
    dots = seq_total(tie(dots, *early)) / model_width
    home_d = feed_home(tie(sum_d, dots))
    grad_w_down = feed_rows(home_d).T

    grad_w_out = dot_left_t(seq_order(attended), branch_row).astype(BF16)
    grad_w_out = dp_sum(grad_w_out)
    home = [(d * n_seq + s, s * n_dp + d) for d in range(n_dp) for s in range(n_seq)]
    grad_w_out = lax.ppermute(grad_w_out, ALL, home)
    grad_w_out = grad_w_out.astype(F32)


    def lin_back(grad_in, lin, factor, gain_vec, mean_dot):
        gain_term = jnp.sum(grad_in * lin * factor, axis=0)
        grad_out = factor * (grad_in * gain_vec) - lin * (factor * factor * factor) * mean_dot
        return grad_out.astype(BF16), gain_term

    grad_q_lin, query_gain_term = lin_back(grad_q, q_lin, q_factor, my_gq, dots[0][:, None])
    grad_k_lin, key_gain_term = lin_back(grad_k, k_lin, k_factor, my_gk, dots[1][:, None])
    grad_lin = jnp.concatenate([grad_q_lin, grad_k_lin, grad_v], axis=1)

    def place(term):
        mine = jnp.arange(n_seq)[:, None] == seq_at
        return jnp.where(mine, term[None, :], 0.0).reshape(model_width)

    gain_terms = jnp.stack(
        [
            place(query_gain_term),
            place(key_gain_term),
            attn_gain_term,
            ffn_gain_term,
        ]
    )
    gain_terms = gain_terms.reshape(4, n_all, own_rows).transpose(1, 0, 2)
    gain_grads = jnp.sum(exchange(gain_terms, ALL), axis=0)

    def row_part(z_of, *earlier):
        rows = lax.dynamic_slice_in_dim(grad_lin, z_of * n_y * tok_count, n_y * tok_count)
        if earlier:
            rows = tie(rows, *earlier)
        return dot_right_t(rows, w_heads)

    grad_input = hidden_back + seq_sum(row_part, grad_w_down, grad_w_out)

    grad_heads = dot_left_t(x_row, grad_lin).astype(BF16)
    grad_heads = dp_sum(grad_heads)
    home_g = feed_home(tie(sum_g, home_d))
    home_u = feed_home(tie(sum_u, home_g, gain_grads, grad_w_out))
    grad_w_gate, grad_w_up = feed_rows(home_g), feed_rows(home_u)
    grad_heads = exchange(grad_heads.reshape(n_seq, own_rows, 3 * own_width), SEQ)
    grad_heads = grad_heads.reshape(n_seq, own_rows, 3, own_width).transpose(2, 1, 0, 3)
    grad_heads = grad_heads.reshape(3, own_rows, model_width).astype(F32)

    return (
        output[None],
        grad_input[None],
        grad_heads[0],
        grad_heads[1],
        grad_heads[2],
        grad_w_out,
        gain_grads[0],
        gain_grads[1],
        gain_grads[2],
        grad_w_gate,
        grad_w_up,
        grad_w_down,
        gain_grads[3],
    )


def plain_rotation(first_pos, tok_count):
    half_dim = HEAD_DIM // 2
    position = (first_pos + jnp.arange(tok_count)).astype(jnp.float32)
    inverse = jnp.exp(-(jnp.arange(half_dim).astype(jnp.float32) / half_dim) * math.log(ROPE_BASE))
    angles = position[:, None] * inverse[None, :]
    return (jnp.cos(angles)[None, :, None, :], jnp.sin(angles)[None, :, None, :])


def plain_rotate(array_in, cosine, sine_t, turn_sign):
    half_dim = array_in.shape[-1] // 2
    first_half = array_in[..., :half_dim]
    second_half = array_in[..., half_dim:]
    return jnp.concatenate(
        [
            first_half * cosine - turn_sign * second_half * sine_t,
            second_half * cosine + turn_sign * first_half * sine_t,
        ],
        axis=-1,
    )


def plain_body(
    inputs,
    doc_lengths,
    w_query,
    w_key,
    w_value,
    w_out,
    gain_query,
    gain_key,
    gain_attn,
    w_gate,
    w_up,
    w_down,
    gain_ffn,
    cotangent,
):
    row_count, tok_count, model_width = inputs.shape
    length = tok_count * lax.axis_size("seq")
    first_pos = lax.axis_index("seq") * tok_count
    score_scale = 1.0 / math.sqrt(HEAD_DIM)
    tokens = inputs.reshape(row_count * tok_count, model_width)

    def heads_first(array_in):
        return array_in.reshape(row_count, tok_count, HEADS, HEAD_DIM).transpose(2, 0, 1, 3)

    def heads_last(array_in):
        return array_in.transpose(1, 2, 0, 3).reshape(row_count * tok_count, HEADS * HEAD_DIM)

    full_q, full_k, full_v, full_o, full_gq, full_gk, full_ga = (
        lax.all_gather(w_query, ("dp", "seq"), axis=0, tiled=True),
        lax.all_gather(w_key, ("dp", "seq"), axis=0, tiled=True),
        lax.all_gather(w_value, ("dp", "seq"), axis=0, tiled=True),
        lax.all_gather(w_out, ("dp", "seq"), axis=0, tiled=True),
        lax.all_gather(gain_query, ("dp", "seq"), axis=0, tiled=True),
        lax.all_gather(gain_key, ("dp", "seq"), axis=0, tiled=True),
        lax.all_gather(gain_attn, ("dp", "seq"), axis=0, tiled=True),
    )
    cosine, sine_t = plain_rotation(first_pos, tok_count)
    q_lin = matmul(tokens, full_q)
    k_lin = matmul(tokens, full_k)
    v_lin = matmul(tokens, full_v)
    q_norm, q_factor = norm_apply(q_lin, full_gq.astype(jnp.float32))
    k_norm, k_factor = norm_apply(k_lin, full_gk.astype(jnp.float32))
    queries = (
        plain_rotate(q_norm.reshape(row_count, tok_count, HEADS, HEAD_DIM), cosine, sine_t, 1.0)
        .astype(jnp.bfloat16)
        .transpose(2, 0, 1, 3)
    )
    keys_mine = (
        plain_rotate(k_norm.reshape(row_count, tok_count, HEADS, HEAD_DIM), cosine, sine_t, 1.0)
        .astype(jnp.bfloat16)
        .transpose(2, 0, 1, 3)
    )
    values_mine = heads_first(v_lin.astype(jnp.bfloat16))
    keys_all, values_all = (
        lax.all_gather(keys_mine, "seq", axis=2, tiled=True),
        lax.all_gather(values_mine, "seq", axis=2, tiled=True),
    )
    doc_ends = jnp.cumsum(doc_lengths, axis=1)
    position = jnp.arange(length)
    doc_ids = jnp.sum((position[None, :, None] >= doc_ends[:, None, :]).astype(jnp.int32), axis=2)
    my_pos = first_pos + jnp.arange(tok_count)
    docs_mine = lax.dynamic_slice_in_dim(doc_ids, first_pos, tok_count, 1)
    allowed = (position[None, None, :] <= my_pos[None, :, None]) & (
        doc_ids[:, None, :] == docs_mine[:, :, None]
    )

    def scores_of(q_head, k_head):
        raw_scores = (
            jnp.einsum("rtd,rkd->rtk", q_head, k_head, preferred_element_type=jnp.float32)
            * score_scale
        )
        return jnp.where(allowed, raw_scores, MASK_FILL)

    def attend(head_item):
        q_head, k_head, v_head = head_item
        scores = scores_of(q_head, k_head)
        row_max = jnp.max(scores, axis=-1, keepdims=True)
        row_total = row_max + jnp.log(jnp.sum(jnp.exp(scores - row_max), axis=-1, keepdims=True))
        attn_probs = jnp.exp(scores - row_total).astype(jnp.bfloat16)
        head_out = jnp.einsum(
            "rtk,rkd->rtd", attn_probs, v_head, preferred_element_type=jnp.float32
        )
        return (head_out, row_total[..., 0])

    attn_mixed, totals = lax.map(attend, (queries, keys_all, values_all))
    attended = heads_last(attn_mixed.astype(jnp.bfloat16))
    branch = matmul(attended, full_o)
    branch_norm, branch_factor = norm_apply(branch, full_ga.astype(jnp.float32))
    hidden = tokens.astype(jnp.float32) + branch_norm
    hidden_low = hidden.astype(jnp.bfloat16)
    gate_full, up_full, down_full, ffn_gain_full = (
        lax.all_gather(w_gate, ("dp", "seq"), axis=0, tiled=True),
        lax.all_gather(w_up, ("dp", "seq"), axis=0, tiled=True),
        lax.all_gather(w_down, ("dp", "seq"), axis=1, tiled=True),
        lax.all_gather(gain_ffn, ("dp", "seq"), axis=0, tiled=True),
    )
    gate_act = matmul(hidden_low, gate_full)
    upward = matmul(hidden_low, up_full)
    gate_sig = jax.nn.sigmoid(gate_act)
    active = (gate_act * gate_sig * upward).astype(jnp.bfloat16)
    result = matmul(active, down_full)
    result_norm, result_factor = norm_apply(result, ffn_gain_full.astype(jnp.float32))
    output = (hidden + result_norm).astype(jnp.bfloat16).reshape(row_count, tok_count, model_width)
    grad_top = cotangent.reshape(row_count * tok_count, model_width).astype(jnp.float32)
    grad_result, ffn_gain_term = norm_back(
        result, result_factor, ffn_gain_full.astype(jnp.float32), grad_top
    )
    grad_result = grad_result.astype(jnp.bfloat16)
    grad_active = dot_right_t(grad_result, down_full)
    grad_gate = (grad_active * upward * gate_sig * (1.0 + gate_act * (1.0 - gate_sig))).astype(
        jnp.bfloat16
    )
    grad_up = (grad_active * gate_act * gate_sig).astype(jnp.bfloat16)
    grad_hidden = grad_top + dot_right_t(grad_gate, gate_full) + dot_right_t(grad_up, up_full)
    feedforward_grads = lax.psum_scatter(
        jnp.concatenate(
            [
                dot_left_t(hidden_low, grad_gate),
                dot_left_t(hidden_low, grad_up),
                dot_left_t(grad_result, active),
            ],
            axis=1,
        ),
        ("dp", "seq"),
        scatter_dimension=0,
        tiled=True,
    )
    grad_branch, attn_gain_term = norm_back(
        branch, branch_factor, full_ga.astype(jnp.float32), grad_hidden
    )
    grad_branch = grad_branch.astype(jnp.bfloat16)
    back_q, back_k, back_v, back_o, back_gq, back_gk = (
        lax.all_gather(w_query, ("dp", "seq"), axis=0, tiled=True),
        lax.all_gather(w_key, ("dp", "seq"), axis=0, tiled=True),
        lax.all_gather(w_value, ("dp", "seq"), axis=0, tiled=True),
        lax.all_gather(w_out, ("dp", "seq"), axis=0, tiled=True),
        lax.all_gather(gain_query, ("dp", "seq"), axis=0, tiled=True),
        lax.all_gather(gain_key, ("dp", "seq"), axis=0, tiled=True),
    )
    grad_attended = dot_right_t(grad_branch, back_o).astype(jnp.bfloat16)
    grad_w_out_term = dot_left_t(attended, grad_branch)
    grad_mixed = heads_first(grad_attended)

    def head_back(head_item):
        q_head, k_head, v_head, g_head, t_head = head_item
        prob_full = jnp.exp(scores_of(q_head, k_head) - t_head[..., None])
        grad_probs = jnp.einsum("rtd,rkd->rtk", g_head, v_head, preferred_element_type=jnp.float32)
        offsets = jnp.sum(prob_full * grad_probs, axis=-1, keepdims=True)
        grad_scores = (prob_full * (grad_probs - offsets)).astype(jnp.bfloat16)
        grad_q = (
            jnp.einsum("rtk,rkd->rtd", grad_scores, k_head, preferred_element_type=jnp.float32)
            * score_scale
        )
        grad_k = (
            jnp.einsum("rtk,rtd->rkd", grad_scores, q_head, preferred_element_type=jnp.float32)
            * score_scale
        )
        grad_v = jnp.einsum(
            "rtk,rtd->rkd",
            prob_full.astype(jnp.bfloat16),
            g_head,
            preferred_element_type=jnp.float32,
        )
        return (grad_q, grad_k, grad_v)

    grad_queries, key_terms, value_terms = lax.map(
        head_back, (queries, keys_all, values_all, grad_mixed, totals)
    )
    grad_keys, grad_values = (
        lax.psum_scatter(
            key_terms.astype(jnp.bfloat16), "seq", scatter_dimension=2, tiled=True
        ).astype(jnp.float32),
        lax.psum_scatter(
            value_terms.astype(jnp.bfloat16), "seq", scatter_dimension=2, tiled=True
        ).astype(jnp.float32),
    )
    grad_q_norm = plain_rotate(grad_queries.transpose(1, 2, 0, 3), cosine, sine_t, -1.0).reshape(
        row_count * tok_count, model_width
    )
    grad_k_norm = plain_rotate(grad_keys.transpose(1, 2, 0, 3), cosine, sine_t, -1.0).reshape(
        row_count * tok_count, model_width
    )
    grad_q_lin, query_gain_term = norm_back(
        q_lin, q_factor, back_gq.astype(jnp.float32), grad_q_norm
    )
    grad_k_lin, key_gain_term = norm_back(k_lin, k_factor, back_gk.astype(jnp.float32), grad_k_norm)
    grad_q_lin = grad_q_lin.astype(jnp.bfloat16)
    grad_k_lin = grad_k_lin.astype(jnp.bfloat16)
    grad_v_lin = heads_last(grad_values).astype(jnp.bfloat16)
    grad_input = (
        grad_hidden
        + dot_right_t(grad_q_lin, back_q)
        + dot_right_t(grad_k_lin, back_k)
        + dot_right_t(grad_v_lin, back_v)
    )
    attention_grads = (
        lax.psum_scatter(
            dot_left_t(tokens, grad_q_lin), ("dp", "seq"), scatter_dimension=0, tiled=True
        ),
        lax.psum_scatter(
            dot_left_t(tokens, grad_k_lin), ("dp", "seq"), scatter_dimension=0, tiled=True
        ),
        lax.psum_scatter(
            dot_left_t(tokens, grad_v_lin), ("dp", "seq"), scatter_dimension=0, tiled=True
        ),
        lax.psum_scatter(grad_w_out_term, ("dp", "seq"), scatter_dimension=0, tiled=True),
        lax.psum_scatter(query_gain_term, ("dp", "seq"), scatter_dimension=0, tiled=True),
        lax.psum_scatter(key_gain_term, ("dp", "seq"), scatter_dimension=0, tiled=True),
        lax.psum_scatter(attn_gain_term, ("dp", "seq"), scatter_dimension=0, tiled=True),
        lax.psum_scatter(ffn_gain_term, ("dp", "seq"), scatter_dimension=0, tiled=True),
    )
    feed_width = w_gate.shape[1]
    grad_w_gate = feedforward_grads[:, :feed_width]
    grad_w_up = feedforward_grads[:, feed_width : 2 * feed_width]
    grad_w_down = feedforward_grads[:, 2 * feed_width :].T
    return (
        output,
        grad_input.reshape(row_count, tok_count, model_width),
        attention_grads[0],
        attention_grads[1],
        attention_grads[2],
        attention_grads[3],
        attention_grads[4],
        attention_grads[5],
        attention_grads[6],
        grad_w_gate,
        grad_w_up,
        grad_w_down,
        attention_grads[7],
    )


def solution(mesh):
    n_dp, n_seq = mesh.shape["dp"], mesh.shape["seq"]
    if n_dp == 4 and n_seq % 2 == 0 and HEADS % n_seq == 0:
        grid = Mesh(mesh.devices.reshape(n_dp // 2, 2, n_seq // 2, 2), ALL)
        layer, dp, seq = body, DP, SEQ
    else:
        grid, layer, dp, seq = mesh, plain_body, ("dp",), ("seq",)
    rows = P(dp, seq, None)
    split = P(dp + seq, None)
    vector = P(dp + seq)
    down = P(None, dp + seq)
    return jax.shard_map(
        layer,
        mesh=grid,
        in_specs=(rows, P(dp, None))
        + (split,) * 4
        + (vector,) * 3
        + (split, split, down, vector, rows),
        out_specs=(rows, rows) + (split,) * 4 + (vector,) * 3 + (split, split, down, vector),
        check_vma=False,
    )
```

```python
import math

import jax
import jax.numpy as jnp
from jax import lax
from jax.experimental import pallas as pl
from jax.experimental.pallas import tpu as pltpu
from jax.sharding import Mesh
from jax.sharding import PartitionSpec as P

HEADS = 16
HEAD_DIM = 128


NORM_EPS = 1e-06
ROPE_BASE = 500000.0
MASK_FILL = -1e30

SEQ = ("z", "y")
DP = ("x", "core")
FEED = ("z", "core")
REST = ("x", "y")
ALL = ("x", "core", "z", "y")
SWAP = [(0, 1), (1, 0)]
F32 = jnp.float32
BF16 = jnp.bfloat16


def matmul(left_mat, right_mat):
    return jnp.dot(left_mat, right_mat, preferred_element_type=F32)


def dot_right_t(left_mat, right_mat):
    return lax.dot_general(
        left_mat, right_mat, (((1,), (1,)), ((), ())), preferred_element_type=F32
    )


def dot_left_t(left_mat, right_mat):
    return lax.dot_general(
        left_mat, right_mat, (((0,), (0,)), ((), ())), preferred_element_type=F32
    )


def norm_apply(array_in, gain_vec):
    factor = lax.rsqrt(jnp.mean(array_in * array_in, axis=-1, keepdims=True) + NORM_EPS)
    return (array_in * factor * gain_vec, factor)


def norm_back(array_in, factor, gain_vec, grad_in):
    gain_term = jnp.sum(grad_in * array_in * factor, axis=0)
    scaled = grad_in * gain_vec
    grad_out = factor * scaled - array_in * (factor * factor * factor) * jnp.mean(
        scaled * array_in, axis=-1, keepdims=True
    )
    return (grad_out, gain_term)


def turn_tables(tok_count):
    half_dim = HEAD_DIM // 2
    position = jnp.arange(tok_count).astype(F32)
    inverse = jnp.exp(-(jnp.arange(half_dim).astype(F32) / half_dim) * math.log(ROPE_BASE))
    angles = position[:, None] * inverse[None, :]
    cosine, sine_t = jnp.cos(angles), jnp.sin(angles)
    return (
        jnp.concatenate([cosine, cosine], axis=1),
        jnp.concatenate([-sine_t, sine_t], axis=1),
    )


def rotate(array_in, cosine, sine_t):
    return array_in * cosine + pltpu.roll(array_in, HEAD_DIM // 2, 1) * sine_t


def rotate_back(array_in, cosine, sine_t):
    return array_in * cosine - pltpu.roll(array_in, HEAD_DIM // 2, 1) * sine_t


def exchange(array_in, axes):
    return lax.all_to_all(array_in, axes, split_axis=0, concat_axis=0, tiled=True)


def spread(array_in, axes):
    count = lax.axis_size(axes)
    return exchange(jnp.broadcast_to(array_in[None], (count,) + array_in.shape), axes)


def tie(value, *earlier):
    return lax.optimization_barrier((value,) + earlier)[0]


def ring_order(count):
    return [0] + list(range(1, count, 2)) + [v for v in range(count - 1, 0, -1) if v % 2 == 0]


def core_swap(array_in):
    return lax.ppermute(array_in, "core", SWAP)


def pick(array_in, at, axis=0):
    return lax.dynamic_index_in_dim(array_in, at, axis, keepdims=False)


def visible(doc_col, doc_row, first, rows, width):
    at = first + lax.broadcasted_iota(jnp.int32, (rows, width), 0)
    of = lax.broadcasted_iota(jnp.int32, (rows, width), 1)
    return (of <= at) & (doc_col == doc_row)


def attend_kernel(
    step,
    q_lin,
    k_lin,
    v_lin,
    factors,
    gain_q,
    gain_k,
    cosine,
    sine_t,
    doc_col,
    doc_row,
    queries,
    keys,
    values,
    totals,
    attended,
):
    cos, sin = cosine[...], sine_t[...]
    queries[...] = rotate(q_lin[...] * factors[:, 0:1] * gain_q[...], cos, sin).astype(BF16)
    keys[...] = rotate(k_lin[...] * factors[:, 1:2] * gain_k[...], cos, sin).astype(BF16)
    values[...] = v_lin[...].astype(BF16)
    scale = 1.0 / math.sqrt(HEAD_DIM)
    for first in range(0, queries.shape[0], step):
        width = first + step
        mine = pl.ds(first, step)
        scores = dot_right_t(queries[mine, :], keys[0:width, :]) * scale
        seen = visible(doc_col[mine, :], doc_row[:, 0:width], first, step, width)
        scores = jnp.where(seen, scores, MASK_FILL)
        row_max = jnp.max(scores, axis=1, keepdims=True)
        row_sum = jnp.sum(jnp.exp(scores - row_max), axis=1, keepdims=True)
        total = row_max + jnp.log(row_sum)
        probs = jnp.exp(scores - total).astype(BF16)
        totals[0, mine, :] = total
        attended[mine, :] = matmul(probs, values[0:width, :]).astype(BF16)


def attend_back_kernel(
    step,
    queries,
    keys,
    values,
    totals,
    g_att,
    q_lin,
    k_lin,
    gain_q,
    gain_k,
    cosine,
    sine_t,
    doc_col,
    doc_row,
    grad_q,
    grad_k,
    grad_v,
    dot_q,
    dot_k,
    k_sum,
    v_sum,
):
    scale = 1.0 / math.sqrt(HEAD_DIM)
    k_sum[...] = jnp.zeros_like(k_sum)
    v_sum[...] = jnp.zeros_like(v_sum)
    for first in range(0, queries.shape[0], step):
        width = first + step
        mine, upto = pl.ds(first, step), pl.ds(0, width)
        scores = dot_right_t(queries[mine, :], keys[upto, :]) * scale
        seen = visible(doc_col[mine, :], doc_row[:, 0:width], first, step, width)
        scores = jnp.where(seen, scores, MASK_FILL)
        prob_full = jnp.exp(scores - totals[0, mine, :])
        grad_probs = dot_right_t(g_att[mine, :], values[upto, :])
        offsets = jnp.sum(prob_full * grad_probs, axis=1, keepdims=True)
        grad_scores = (prob_full * (grad_probs - offsets)).astype(BF16)
        back = matmul(grad_scores, keys[upto, :]) * scale
        back = rotate_back(back, cosine[mine, :], sine_t[mine, :])
        grad_q[mine, :] = back
        dot_q[0, mine, :] = jnp.sum(back * gain_q[...] * q_lin[mine, :], axis=1, keepdims=True)
        k_sum[upto, :] += dot_left_t(grad_scores, queries[mine, :])
        v_sum[upto, :] += dot_left_t(prob_full.astype(BF16), g_att[mine, :])
    back = rotate_back(k_sum[...] * scale, cosine[...], sine_t[...])
    grad_k[...] = back
    dot_k[0] = jnp.sum(back * gain_k[...] * k_lin[...], axis=1, keepdims=True)
    grad_v[...] = v_sum[...].astype(BF16)


def head_specs(length, heads):
    def part(offset):
        return pl.BlockSpec((length, HEAD_DIM), lambda h: (0, h + offset))

    def gain():
        return pl.BlockSpec((1, HEAD_DIM), lambda h: (0, h))

    def whole(shape):
        return pl.BlockSpec(shape, lambda h: (0, 0))

    each = pl.BlockSpec((1, length, 1), lambda h: (h, 0, 0))
    table = whole((length, HEAD_DIM))
    docs = [whole((length, 1)), whole((1, length))]
    return part, gain, whole, each, table, docs


def attend(qkv, factors, gain_q, gain_k, tables, docs, heads):
    length = qkv.shape[0]
    part, gain, whole, each, table, doc_specs = head_specs(length, heads)
    low = jax.ShapeDtypeStruct((length, heads * HEAD_DIM), BF16)
    step = min(256, length)
    pairs = heads * length * length * HEAD_DIM
    return pl.pallas_call(
        lambda *refs: attend_kernel(step, *refs),
        grid=(heads,),
        in_specs=[part(0), part(heads), part(2 * heads), whole((length, 2)), gain(), gain()]
        + [table, table]
        + doc_specs,
        out_specs=[part(0), part(0), part(0), each, part(0)],
        out_shape=[low, low, low, jax.ShapeDtypeStruct((heads, length, 1), F32), low],
        compiler_params=pltpu.CompilerParams(vmem_limit_bytes=58 * 1024 * 1024),
        cost_estimate=pl.CostEstimate(
            flops=3 * pairs, bytes_accessed=qkv.size * 6, transcendentals=heads * length * length
        ),
    )(qkv, qkv, qkv, factors, gain_q, gain_k, *tables, *docs)


def attend_back(saved, g_att, qkv, gain_q, gain_k, tables, docs, heads):
    queries, keys, values, totals = saved
    length = qkv.shape[0]
    part, gain, whole, each, table, doc_specs = head_specs(length, heads)
    flat = jax.ShapeDtypeStruct((length, heads * HEAD_DIM), F32)
    low = jax.ShapeDtypeStruct((length, heads * HEAD_DIM), BF16)
    line = jax.ShapeDtypeStruct((heads, length, 1), F32)
    step = min(256, length)
    pairs = heads * length * length * HEAD_DIM
    return pl.pallas_call(
        lambda *refs: attend_back_kernel(step, *refs),
        grid=(heads,),
        in_specs=[part(0), part(0), part(0), each, part(0), part(0), part(heads), gain(), gain()]
        + [table, table]
        + doc_specs,
        out_specs=[part(0), part(0), part(0), each, each],
        out_shape=[flat, flat, low, line, line],
        scratch_shapes=[pltpu.VMEM((length, HEAD_DIM), F32)] * 2,
        compiler_params=pltpu.CompilerParams(vmem_limit_bytes=58 * 1024 * 1024),
        cost_estimate=pl.CostEstimate(
            flops=7 * pairs, bytes_accessed=qkv.size * 8, transcendentals=heads * length * length
        ),
    )(queries, keys, values, totals, g_att, qkv, qkv, gain_q, gain_k, *tables, *docs)


def feed_kernel(part, other, w_g, w_u, w_d, *refs):
    hid, gate, upward, active, mine, away, total = refs[-7:]
    block, tokens = pl.program_id(0), part.shape[0]

    @pl.when(block == 0)
    def _():
        hid[:tokens, :] = part[...]
        hid[tokens:, :] = other[...]

    g = matmul(hid[...], w_g[...])
    u = matmul(hid[...], w_u[...])
    a = (g * (1.0 / (1.0 + jnp.exp(-g))) * u).astype(BF16)
    gate[...], upward[...], active[...] = g, u, a
    term = dot_right_t(a, w_d[...])

    @pl.when(block == 0)
    def _():
        total[...] = term

    @pl.when(block > 0)
    def _():
        total[...] += term

    @pl.when(block == pl.num_programs(0) - 1)
    def _():
        mine[...] = total[:tokens, :]
        away[...] = total[tokens:, :].astype(BF16)


def feed_back_kernel(part, other, w_g, w_u, w_d, gate, upward, *refs):
    g_res, g_gate, g_up, mine, away, total = refs[-6:]
    block, tokens = pl.program_id(0), part.shape[0]

    @pl.when(block == 0)
    def _():
        g_res[:tokens, :] = part[...]
        g_res[tokens:, :] = other[...]

    a = matmul(g_res[...], w_d[...])
    g, u = gate[...], upward[...]
    s = 1.0 / (1.0 + jnp.exp(-g))
    gg = (a * u * s * (1.0 + g * (1.0 - s))).astype(BF16)
    gu = (a * g * s).astype(BF16)
    g_gate[...], g_up[...] = gg, gu
    term = dot_right_t(gg, w_g[...]) + dot_right_t(gu, w_u[...])

    @pl.when(block == 0)
    def _():
        total[...] = term

    @pl.when(block > 0)
    def _():
        total[...] += term

    @pl.when(block == pl.num_programs(0) - 1)
    def _():
        mine[...] = total[:tokens, :]
        away[...] = total[tokens:, :].astype(BF16)


def feed_step(at, count, pair, weights, saved, held, kernel, dtypes):
    tokens, width = pair[0].shape
    feed = weights[0].shape[1]
    step = min(512, feed)
    rows = 2 * tokens
    block = pl.BlockSpec((rows, step), lambda f: (at, f))
    part = pl.BlockSpec((tokens, width), lambda f: (0, 0))
    full = pl.BlockSpec((rows, width), lambda f: (at, 0))
    n_in = 5 + len(saved)
    shapes = [jax.ShapeDtypeStruct((count * rows, width), BF16)]
    shapes += [jax.ShapeDtypeStruct((count * rows, feed), d) for d in dtypes]
    tail = [jax.ShapeDtypeStruct((tokens, width), d) for d in (F32, BF16)]
    flops = 6 * rows * width * feed
    return pl.pallas_call(
        kernel,
        grid=(feed // step,),
        in_specs=[part, part]
        + [pl.BlockSpec((width, step), lambda f: (0, f))] * 3
        + [block] * len(saved)
        + [pl.BlockSpec(memory_space=pl.ANY)] * len(held),
        out_specs=[full] + [block] * len(dtypes) + [part, part],
        out_shape=shapes + tail,
        scratch_shapes=[pltpu.VMEM((rows, width), F32)],
        input_output_aliases={n_in + k: k for k in range(len(held))},
        compiler_params=pltpu.CompilerParams(vmem_limit_bytes=32 * 1024 * 1024),
        cost_estimate=pl.CostEstimate(
            flops=flops, bytes_accessed=6 * width * feed, transcendentals=rows * feed
        ),
    )(*pair, *weights, *saved, *held)


def body(
    inputs,
    doc_lengths,
    w_query,
    w_key,
    w_value,
    w_out,
    gain_query,
    gain_key,
    gain_attn,
    w_gate,
    w_up,
    w_down,
    gain_ffn,
    cotangent,
):
    _, tok_count, model_width = inputs.shape
    n_x, n_core, n_z, n_y = (lax.axis_size(a) for a in ALL)
    n_seq, n_dp, n_all = n_z * n_y, n_x * n_core, n_x * n_core * n_z * n_y
    seq_at = lax.axis_index(SEQ)
    length = tok_count * n_seq
    score_scale = 1.0 / math.sqrt(HEAD_DIM)
    own_rows = w_query.shape[0]
    own_width = model_width // n_seq
    own_heads = own_width // HEAD_DIM
    feed_width = w_gate.shape[1]
    n_feed = n_core * n_z
    own_feed = feed_width // n_feed
    x_at, core_at, z_at, y_at = (lax.axis_index(a) for a in ALL)
    order = ring_order(n_z)
    ring = [(order[i], order[(i + 1) % n_z]) for i in range(n_z)]
    behind = jnp.array(
        [[order[(order.index(z) - s) % n_z] for z in range(n_z)] for s in range(n_z)], jnp.int32
    )
    tokens = inputs[0]

    def ring_send(part):
        return lax.ppermute(part, "z", ring)

    def seq_gather(own):
        chunks, held = [], own
        for step in range(n_z):
            chunks += [held, lax.ppermute(held, "y", SWAP)]
            if step < n_z - 1:
                held = ring_send(held)
        return jnp.concatenate(chunks, axis=0)

    def row_gather(own, gates):
        chunks, held = [], own
        for step in range(n_z):
            chunks.append((held, lax.ppermute(held, "y", SWAP)))
            if step < n_z - 1:
                held = ring_send(tie(held, *gates(step, held)))

        def whole(first, count):
            out = jnp.zeros((n_seq * count, own.shape[1]), own.dtype)
            for step, pair in enumerate(chunks):
                for at_y, part in zip((y_at, 1 - y_at), pair):
                    at = (behind[step, z_at] * n_y + at_y) * count
                    part = part[first : first + count]
                    out = lax.dynamic_update_slice(out, part, (at, 0))
            return out

        return whole(0, tok_count), whole(tok_count, own.shape[0] - tok_count), held

    def dp_gather(mine):
        out = jnp.zeros((n_x, n_core) + mine.shape, mine.dtype)
        for at_x, part in ((x_at, mine), (1 - x_at, lax.ppermute(mine, "x", SWAP))):
            for at_core, block in ((core_at, part), (1 - core_at, core_swap(part))):
                block = block[None, None]
                out = lax.dynamic_update_slice(out, block, (at_x, at_core, 0, 0))
        return out.reshape((n_dp * mine.shape[0], mine.shape[1]))

    def seq_order(array_in):
        chunks = []
        for step in range(n_z):
            for at_y in (y_at, 1 - y_at):
                first = (behind[step, z_at] * n_y + at_y) * tok_count
                chunks.append(lax.dynamic_slice_in_dim(array_in, first, tok_count))
        return jnp.concatenate(chunks, axis=0)

    def seq_sum(part_of, *last):
        total = None
        for step in list(range(1, n_z)) + [0]:
            part = part_of(behind[step, z_at], *(() if step else last))
            part = part.reshape(n_y, tok_count, model_width)
            away = lax.ppermute(pick(part, 1 - y_at).astype(BF16), "y", SWAP)
            mine = pick(part, y_at) + away.astype(F32)
            if total is not None:
                mine = mine + ring_send(total.astype(BF16)).astype(F32)
            total = mine
        return total

    def feed_weights(mats, earlier):
        blocks = jnp.stack(mats).reshape(len(mats), own_rows, n_feed, own_feed)
        mine = exchange(tie(blocks.transpose(2, 0, 1, 3), *earlier), FEED)
        return [mine[:, at].reshape(n_feed * own_rows, own_feed) for at in range(len(mats))]

    def rest_send(mine):
        return mine, lax.ppermute(mine, "y", SWAP), lax.ppermute(mine, "x", SWAP)

    def rest_gather(sent, corner, later):
        mine, over_y, over_x = sent
        mine = tie(mine, later)
        whole = jnp.zeros((n_x, n_y) + mine.shape, BF16)
        for at_x, at_y, part in (
            (x_at, y_at, mine),
            (1 - x_at, y_at, over_x),
            (x_at, 1 - y_at, over_y),
            (1 - x_at, 1 - y_at, corner),
        ):
            whole = lax.dynamic_update_slice(whole, part[None, None], (at_x, at_y, 0, 0))
        return whole.reshape(model_width, own_feed)

    def seq_total(term):
        return jnp.sum(spread(term, SEQ), axis=0)

    def to_feed_order(array_in):
        lead = array_in.shape[:-1]
        parts = array_in.reshape((-1, n_x, n_core, n_z, n_y, own_rows))
        return parts.transpose(0, 1, 4, 3, 2, 5).reshape(lead + (model_width,))

    def from_feed_order(array_in):
        lead = array_in.shape[:-1]
        parts = array_in.reshape((-1, n_x, n_y, n_z, n_core, own_rows))
        return parts.transpose(0, 1, 4, 3, 2, 5).reshape(lead + (model_width,))

    gains = spread(jnp.stack([gain_query, gain_key, gain_attn, gain_ffn]), ALL)
    gains = gains.transpose(1, 0, 2).reshape(4, model_width).astype(F32)
    my_gq = lax.dynamic_slice_in_dim(gains[0:1], seq_at * own_width, own_width, 1)
    my_gk = lax.dynamic_slice_in_dim(gains[1:2], seq_at * own_width, own_width, 1)
    gain_a, gain_f = to_feed_order(gains[2]), to_feed_order(gains[3])

    w_heads = jnp.stack([w_query, w_key, w_value])
    w_heads = w_heads.reshape(3, own_rows, n_seq, own_width).transpose(2, 1, 0, 3)
    w_heads = w_heads.reshape(n_seq, own_rows, 3 * own_width)
    w_heads = exchange(tie(w_heads, gains), SEQ)
    w_mine = w_heads.reshape(n_seq * own_rows, 3 * own_width)

    w_heads = dp_gather(w_mine)
    def gates(step, held):
        return (w_mine,) if step == 1 else ()

    own = jnp.concatenate([tokens, to_feed_order(w_out)])
    x_row, w_out_mine, x_last = row_gather(own, gates)
    moved = feed_weights([w_gate, w_up], (x_last,))

    qkv = matmul(x_row, w_heads)
    q_lin, k_lin = qkv[:, :own_width], qkv[:, own_width : 2 * own_width]
    squares = jnp.stack([jnp.sum(q_lin * q_lin, axis=1), jnp.sum(k_lin * k_lin, axis=1)])
    squares = seq_total(squares) / model_width
    factors = lax.rsqrt(squares + NORM_EPS).T
    q_factor, k_factor = factors[:, 0:1], factors[:, 1:2]
    tables = turn_tables(length)
    doc_ends = jnp.cumsum(doc_lengths[0])
    position = jnp.arange(length)
    doc_ids = jnp.sum((position[:, None] >= doc_ends[None, :]).astype(jnp.int32), axis=1)
    docs = (doc_ids[:, None], doc_ids[None, :])
    w_u = lax.all_gather(moved[1], REST, axis=0, tiled=True)
    sent_g = rest_send(tie(moved[0], squares))
    moved += feed_weights([w_down.T], (squares,))
    sent_d = rest_send(moved[2])
    *saved, attended = attend(qkv, factors, my_gq, my_gk, tables, docs, own_heads)

    corner_g = lax.ppermute(sent_g[1], "x", SWAP)
    att_tok = tie(attended.reshape(n_seq, tok_count, own_width), *sent_g)
    att_tok = exchange(att_tok, SEQ)
    corner_d = lax.ppermute(sent_d[2], "y", SWAP)
    att_tok = att_tok.transpose(1, 0, 2).reshape(tok_count, model_width)
    full_o = dp_gather(w_out_mine)
    branch = matmul(att_tok, full_o)
    w_g = rest_gather(sent_g, corner_g, branch)
    w_d = rest_gather(sent_d, corner_d, branch)
    branch_norm, branch_factor = norm_apply(branch, gain_a)
    hidden = to_feed_order(tokens).astype(F32) + branch_norm
    hidden_low = hidden.astype(BF16)

    def feed_pass(own, saved, kernel, dtypes, gate=()):
        held, total, rows = [], None, own
        for at in range(n_z):
            pair = (rows, core_swap(rows))
            if at < n_z - 1:
                rows = ring_send(tie(rows, *gate) if gate and at == 1 else rows)
            if at > 1:
                pair = tie(pair, total)
            *held, mine, away = feed_step(
                at, n_z, pair, (w_g, w_u, w_d), saved, held, kernel, dtypes
            )
            if at == 0:
                first = (mine, away)
            else:
                total = add_up(mine, away, total)
        return held, add_up(*first, total)

    def add_up(mine, away, total):
        mine = mine + core_swap(away).astype(F32)
        if total is not None:
            mine = mine + ring_send(total.astype(BF16)).astype(F32)
        return mine

    (hid, gate, upward, active), result = feed_pass(
        hidden_low, (), feed_kernel, (F32, F32, BF16), sent_d
    )
    result_norm, result_factor = norm_apply(result, gain_f)
    output = from_feed_order((hidden + result_norm).astype(BF16))

    grad_top = to_feed_order(cotangent[0]).astype(F32)
    grad_result, ffn_gain_term = norm_back(result, result_factor, gain_f, grad_top)
    def token_sum(left, right):
        return dot_left_t(left, right).astype(BF16)

    def rest_sum(term):
        return lax.psum_scatter(term, REST, scatter_dimension=0, tiled=True)

    def feed_home(term):
        return exchange(term.reshape(n_feed, own_rows, own_feed), FEED)

    def feed_rows(term):
        return term.transpose(1, 0, 2).reshape(own_rows, feed_width).astype(F32)

    def dp_sum(term):
        rows = term.shape[0] // n_dp

        def of(array_in, at):
            return lax.dynamic_slice_in_dim(array_in, at * rows, rows)

        def cores(at):
            return jnp.concatenate([of(term, x * n_core + at) for x in range(n_x)])

        away = core_swap(cores(1 - core_at))
        term = (cores(core_at).astype(F32) + away.astype(F32)).astype(BF16)
        away = lax.ppermute(of(term, 1 - x_at), "x", SWAP)
        return (of(term, x_at).astype(F32) + away.astype(F32)).astype(BF16)

    (g_res, g_gate, g_up), grad_ffn = feed_pass(
        grad_result.astype(BF16), (gate, upward), feed_back_kernel, (BF16, BF16), (output,)
    )
    grad_hidden = grad_top + grad_ffn
    term_d = token_sum(g_res, active)
    sum_d = rest_sum(term_d)
    term_g, term_u = token_sum(hid, g_gate), token_sum(hid, g_up)

    grad_branch, attn_gain_term = norm_back(branch, branch_factor, gain_a, grad_hidden)
    grad_branch = grad_branch.astype(BF16)
    grad_attended = dot_right_t(grad_branch, full_o).astype(BF16)
    g_att = grad_attended.reshape(tok_count, n_seq, own_width).transpose(1, 0, 2)
    g_att = exchange(g_att, SEQ).reshape(length, own_width)
    g_att = tie(g_att, term_g, term_u)
    sum_g, sum_u = rest_sum(term_g), rest_sum(term_u)

    grad_q, grad_k, grad_v, dot_q, dot_k = attend_back(
        saved, g_att, qkv, my_gq, my_gk, tables, docs, own_heads
    )
    dots = jnp.stack([jnp.sum(dot_q, axis=(0, 2)), jnp.sum(dot_k, axis=(0, 2))])
    branch_row = seq_gather(from_feed_order(tie(grad_branch, grad_attended)))
    hidden_back, ffn_gain_term, attn_gain_term = [
        from_feed_order(tie(a, grad_attended))
        for a in (grad_hidden, ffn_gain_term, attn_gain_term)
    ]
    early = (branch_row, hidden_back, ffn_gain_term, attn_gain_term)
    dots = seq_total(tie(dots, *early)) / model_width
    home_d = feed_home(tie(sum_d, dots))
    grad_w_down = feed_rows(home_d).T

    grad_w_out = dot_left_t(seq_order(attended), branch_row).astype(BF16)
    grad_w_out = dp_sum(grad_w_out)
    home = [(d * n_seq + s, s * n_dp + d) for d in range(n_dp) for s in range(n_seq)]
    grad_w_out = lax.ppermute(grad_w_out, ALL, home)
    grad_w_out = grad_w_out.astype(F32)


    def lin_back(grad_in, lin, factor, gain_vec, mean_dot):
        gain_term = jnp.sum(grad_in * lin * factor, axis=0)
        grad_out = factor * (grad_in * gain_vec) - lin * (factor * factor * factor) * mean_dot
        return grad_out.astype(BF16), gain_term

    grad_q_lin, query_gain_term = lin_back(grad_q, q_lin, q_factor, my_gq, dots[0][:, None])
    grad_k_lin, key_gain_term = lin_back(grad_k, k_lin, k_factor, my_gk, dots[1][:, None])
    grad_lin = jnp.concatenate([grad_q_lin, grad_k_lin, grad_v], axis=1)

    def place(term):
        mine = jnp.arange(n_seq)[:, None] == seq_at
        return jnp.where(mine, term[None, :], 0.0).reshape(model_width)

    gain_terms = jnp.stack(
        [
            place(query_gain_term),
            place(key_gain_term),
            attn_gain_term,
            ffn_gain_term,
        ]
    )
    gain_terms = gain_terms.reshape(4, n_all, own_rows).transpose(1, 0, 2)
    gain_grads = jnp.sum(exchange(gain_terms, ALL), axis=0)

    def row_part(z_of, *earlier):
        rows = lax.dynamic_slice_in_dim(grad_lin, z_of * n_y * tok_count, n_y * tok_count)
        if earlier:
            rows = tie(rows, *earlier)
        return dot_right_t(rows, w_heads)

    grad_input = hidden_back + seq_sum(row_part, grad_w_down, grad_w_out)

    grad_heads = dot_left_t(x_row, grad_lin).astype(BF16)
    grad_heads = dp_sum(grad_heads)
    home_g = feed_home(tie(sum_g, home_d))
    home_u = feed_home(tie(sum_u, home_g, gain_grads, grad_w_out))
    grad_w_gate, grad_w_up = feed_rows(home_g), feed_rows(home_u)
    grad_heads = exchange(grad_heads.reshape(n_seq, own_rows, 3 * own_width), SEQ)
    grad_heads = grad_heads.reshape(n_seq, own_rows, 3, own_width).transpose(2, 1, 0, 3)
    grad_heads = grad_heads.reshape(3, own_rows, model_width).astype(F32)

    return (
        output[None],
        grad_input[None],
        grad_heads[0],
        grad_heads[1],
        grad_heads[2],
        grad_w_out,
        gain_grads[0],
        gain_grads[1],
        gain_grads[2],
        grad_w_gate,
        grad_w_up,
        grad_w_down,
        gain_grads[3],
    )


def plain_rotation(first_pos, tok_count):
    half_dim = HEAD_DIM // 2
    position = (first_pos + jnp.arange(tok_count)).astype(jnp.float32)
    inverse = jnp.exp(-(jnp.arange(half_dim).astype(jnp.float32) / half_dim) * math.log(ROPE_BASE))
    angles = position[:, None] * inverse[None, :]
    return (jnp.cos(angles)[None, :, None, :], jnp.sin(angles)[None, :, None, :])


def plain_rotate(array_in, cosine, sine_t, turn_sign):
    half_dim = array_in.shape[-1] // 2
    first_half = array_in[..., :half_dim]
    second_half = array_in[..., half_dim:]
    return jnp.concatenate(
        [
            first_half * cosine - turn_sign * second_half * sine_t,
            second_half * cosine + turn_sign * first_half * sine_t,
        ],
        axis=-1,
    )


def plain_body(
    inputs,
    doc_lengths,
    w_query,
    w_key,
    w_value,
    w_out,
    gain_query,
    gain_key,
    gain_attn,
    w_gate,
    w_up,
    w_down,
    gain_ffn,
    cotangent,
):
    row_count, tok_count, model_width = inputs.shape
    length = tok_count * lax.axis_size("seq")
    first_pos = lax.axis_index("seq") * tok_count
    score_scale = 1.0 / math.sqrt(HEAD_DIM)
    tokens = inputs.reshape(row_count * tok_count, model_width)

    def heads_first(array_in):
        return array_in.reshape(row_count, tok_count, HEADS, HEAD_DIM).transpose(2, 0, 1, 3)

    def heads_last(array_in):
        return array_in.transpose(1, 2, 0, 3).reshape(row_count * tok_count, HEADS * HEAD_DIM)

    full_q, full_k, full_v, full_o, full_gq, full_gk, full_ga = (
        lax.all_gather(w_query, ("dp", "seq"), axis=0, tiled=True),
        lax.all_gather(w_key, ("dp", "seq"), axis=0, tiled=True),
        lax.all_gather(w_value, ("dp", "seq"), axis=0, tiled=True),
        lax.all_gather(w_out, ("dp", "seq"), axis=0, tiled=True),
        lax.all_gather(gain_query, ("dp", "seq"), axis=0, tiled=True),
        lax.all_gather(gain_key, ("dp", "seq"), axis=0, tiled=True),
        lax.all_gather(gain_attn, ("dp", "seq"), axis=0, tiled=True),
    )
    cosine, sine_t = plain_rotation(first_pos, tok_count)
    q_lin = matmul(tokens, full_q)
    k_lin = matmul(tokens, full_k)
    v_lin = matmul(tokens, full_v)
    q_norm, q_factor = norm_apply(q_lin, full_gq.astype(jnp.float32))
    k_norm, k_factor = norm_apply(k_lin, full_gk.astype(jnp.float32))
    queries = (
        plain_rotate(q_norm.reshape(row_count, tok_count, HEADS, HEAD_DIM), cosine, sine_t, 1.0)
        .astype(jnp.bfloat16)
        .transpose(2, 0, 1, 3)
    )
    keys_mine = (
        plain_rotate(k_norm.reshape(row_count, tok_count, HEADS, HEAD_DIM), cosine, sine_t, 1.0)
        .astype(jnp.bfloat16)
        .transpose(2, 0, 1, 3)
    )
    values_mine = heads_first(v_lin.astype(jnp.bfloat16))
    keys_all, values_all = (
        lax.all_gather(keys_mine, "seq", axis=2, tiled=True),
        lax.all_gather(values_mine, "seq", axis=2, tiled=True),
    )
    doc_ends = jnp.cumsum(doc_lengths, axis=1)
    position = jnp.arange(length)
    doc_ids = jnp.sum((position[None, :, None] >= doc_ends[:, None, :]).astype(jnp.int32), axis=2)
    my_pos = first_pos + jnp.arange(tok_count)
    docs_mine = lax.dynamic_slice_in_dim(doc_ids, first_pos, tok_count, 1)
    allowed = (position[None, None, :] <= my_pos[None, :, None]) & (
        doc_ids[:, None, :] == docs_mine[:, :, None]
    )

    def scores_of(q_head, k_head):
        raw_scores = (
            jnp.einsum("rtd,rkd->rtk", q_head, k_head, preferred_element_type=jnp.float32)
            * score_scale
        )
        return jnp.where(allowed, raw_scores, MASK_FILL)

    def attend(head_item):
        q_head, k_head, v_head = head_item
        scores = scores_of(q_head, k_head)
        row_max = jnp.max(scores, axis=-1, keepdims=True)
        row_total = row_max + jnp.log(jnp.sum(jnp.exp(scores - row_max), axis=-1, keepdims=True))
        attn_probs = jnp.exp(scores - row_total).astype(jnp.bfloat16)
        head_out = jnp.einsum(
            "rtk,rkd->rtd", attn_probs, v_head, preferred_element_type=jnp.float32
        )
        return (head_out, row_total[..., 0])

    attn_mixed, totals = lax.map(attend, (queries, keys_all, values_all))
    attended = heads_last(attn_mixed.astype(jnp.bfloat16))
    branch = matmul(attended, full_o)
    branch_norm, branch_factor = norm_apply(branch, full_ga.astype(jnp.float32))
    hidden = tokens.astype(jnp.float32) + branch_norm
    hidden_low = hidden.astype(jnp.bfloat16)
    gate_full, up_full, down_full, ffn_gain_full = (
        lax.all_gather(w_gate, ("dp", "seq"), axis=0, tiled=True),
        lax.all_gather(w_up, ("dp", "seq"), axis=0, tiled=True),
        lax.all_gather(w_down, ("dp", "seq"), axis=1, tiled=True),
        lax.all_gather(gain_ffn, ("dp", "seq"), axis=0, tiled=True),
    )
    gate_act = matmul(hidden_low, gate_full)
    upward = matmul(hidden_low, up_full)
    gate_sig = jax.nn.sigmoid(gate_act)
    active = (gate_act * gate_sig * upward).astype(jnp.bfloat16)
    result = matmul(active, down_full)
    result_norm, result_factor = norm_apply(result, ffn_gain_full.astype(jnp.float32))
    output = (hidden + result_norm).astype(jnp.bfloat16).reshape(row_count, tok_count, model_width)
    grad_top = cotangent.reshape(row_count * tok_count, model_width).astype(jnp.float32)
    grad_result, ffn_gain_term = norm_back(
        result, result_factor, ffn_gain_full.astype(jnp.float32), grad_top
    )
    grad_result = grad_result.astype(jnp.bfloat16)
    grad_active = dot_right_t(grad_result, down_full)
    grad_gate = (grad_active * upward * gate_sig * (1.0 + gate_act * (1.0 - gate_sig))).astype(
        jnp.bfloat16
    )
    grad_up = (grad_active * gate_act * gate_sig).astype(jnp.bfloat16)
    grad_hidden = grad_top + dot_right_t(grad_gate, gate_full) + dot_right_t(grad_up, up_full)
    feedforward_grads = lax.psum_scatter(
        jnp.concatenate(
            [
                dot_left_t(hidden_low, grad_gate),
                dot_left_t(hidden_low, grad_up),
                dot_left_t(grad_result, active),
            ],
            axis=1,
        ),
        ("dp", "seq"),
        scatter_dimension=0,
        tiled=True,
    )
    grad_branch, attn_gain_term = norm_back(
        branch, branch_factor, full_ga.astype(jnp.float32), grad_hidden
    )
    grad_branch = grad_branch.astype(jnp.bfloat16)
    back_q, back_k, back_v, back_o, back_gq, back_gk = (
        lax.all_gather(w_query, ("dp", "seq"), axis=0, tiled=True),
        lax.all_gather(w_key, ("dp", "seq"), axis=0, tiled=True),
        lax.all_gather(w_value, ("dp", "seq"), axis=0, tiled=True),
        lax.all_gather(w_out, ("dp", "seq"), axis=0, tiled=True),
        lax.all_gather(gain_query, ("dp", "seq"), axis=0, tiled=True),
        lax.all_gather(gain_key, ("dp", "seq"), axis=0, tiled=True),
    )
    grad_attended = dot_right_t(grad_branch, back_o).astype(jnp.bfloat16)
    grad_w_out_term = dot_left_t(attended, grad_branch)
    grad_mixed = heads_first(grad_attended)

    def head_back(head_item):
        q_head, k_head, v_head, g_head, t_head = head_item
        prob_full = jnp.exp(scores_of(q_head, k_head) - t_head[..., None])
        grad_probs = jnp.einsum("rtd,rkd->rtk", g_head, v_head, preferred_element_type=jnp.float32)
        offsets = jnp.sum(prob_full * grad_probs, axis=-1, keepdims=True)
        grad_scores = (prob_full * (grad_probs - offsets)).astype(jnp.bfloat16)
        grad_q = (
            jnp.einsum("rtk,rkd->rtd", grad_scores, k_head, preferred_element_type=jnp.float32)
            * score_scale
        )
        grad_k = (
            jnp.einsum("rtk,rtd->rkd", grad_scores, q_head, preferred_element_type=jnp.float32)
            * score_scale
        )
        grad_v = jnp.einsum(
            "rtk,rtd->rkd",
            prob_full.astype(jnp.bfloat16),
            g_head,
            preferred_element_type=jnp.float32,
        )
        return (grad_q, grad_k, grad_v)

    grad_queries, key_terms, value_terms = lax.map(
        head_back, (queries, keys_all, values_all, grad_mixed, totals)
    )
    grad_keys, grad_values = (
        lax.psum_scatter(
            key_terms.astype(jnp.bfloat16), "seq", scatter_dimension=2, tiled=True
        ).astype(jnp.float32),
        lax.psum_scatter(
            value_terms.astype(jnp.bfloat16), "seq", scatter_dimension=2, tiled=True
        ).astype(jnp.float32),
    )
    grad_q_norm = plain_rotate(grad_queries.transpose(1, 2, 0, 3), cosine, sine_t, -1.0).reshape(
        row_count * tok_count, model_width
    )
    grad_k_norm = plain_rotate(grad_keys.transpose(1, 2, 0, 3), cosine, sine_t, -1.0).reshape(
        row_count * tok_count, model_width
    )
    grad_q_lin, query_gain_term = norm_back(
        q_lin, q_factor, back_gq.astype(jnp.float32), grad_q_norm
    )
    grad_k_lin, key_gain_term = norm_back(k_lin, k_factor, back_gk.astype(jnp.float32), grad_k_norm)
    grad_q_lin = grad_q_lin.astype(jnp.bfloat16)
    grad_k_lin = grad_k_lin.astype(jnp.bfloat16)
    grad_v_lin = heads_last(grad_values).astype(jnp.bfloat16)
    grad_input = (
        grad_hidden
        + dot_right_t(grad_q_lin, back_q)
        + dot_right_t(grad_k_lin, back_k)
        + dot_right_t(grad_v_lin, back_v)
    )
    attention_grads = (
        lax.psum_scatter(
            dot_left_t(tokens, grad_q_lin), ("dp", "seq"), scatter_dimension=0, tiled=True
        ),
        lax.psum_scatter(
            dot_left_t(tokens, grad_k_lin), ("dp", "seq"), scatter_dimension=0, tiled=True
        ),
        lax.psum_scatter(
            dot_left_t(tokens, grad_v_lin), ("dp", "seq"), scatter_dimension=0, tiled=True
        ),
        lax.psum_scatter(grad_w_out_term, ("dp", "seq"), scatter_dimension=0, tiled=True),
        lax.psum_scatter(query_gain_term, ("dp", "seq"), scatter_dimension=0, tiled=True),
        lax.psum_scatter(key_gain_term, ("dp", "seq"), scatter_dimension=0, tiled=True),
        lax.psum_scatter(attn_gain_term, ("dp", "seq"), scatter_dimension=0, tiled=True),
        lax.psum_scatter(ffn_gain_term, ("dp", "seq"), scatter_dimension=0, tiled=True),
    )
    feed_width = w_gate.shape[1]
    grad_w_gate = feedforward_grads[:, :feed_width]
    grad_w_up = feedforward_grads[:, feed_width : 2 * feed_width]
    grad_w_down = feedforward_grads[:, 2 * feed_width :].T
    return (
        output,
        grad_input.reshape(row_count, tok_count, model_width),
        attention_grads[0],
        attention_grads[1],
        attention_grads[2],
        attention_grads[3],
        attention_grads[4],
        attention_grads[5],
        attention_grads[6],
        grad_w_gate,
        grad_w_up,
        grad_w_down,
        attention_grads[7],
    )


def solution(mesh):
    n_dp, n_seq = mesh.shape["dp"], mesh.shape["seq"]
    if n_dp == 4 and n_seq % 2 == 0 and HEADS % n_seq == 0:
        grid = Mesh(mesh.devices.reshape(n_dp // 2, 2, n_seq // 2, 2), ALL)
        layer, dp, seq = body, DP, SEQ
    else:
        grid, layer, dp, seq = mesh, plain_body, ("dp",), ("seq",)
    rows = P(dp, seq, None)
    split = P(dp + seq, None)
    vector = P(dp + seq)
    down = P(None, dp + seq)
    return jax.shard_map(
        layer,
        mesh=grid,
        in_specs=(rows, P(dp, None))
        + (split,) * 4
        + (vector,) * 3
        + (split, split, down, vector, rows),
        out_specs=(rows, rows) + (split,) * 4 + (vector,) * 3 + (split, split, down, vector),
        check_vma=False,
    )
```

```python
import math

import jax
import jax.numpy as jnp
from jax import lax
from jax.experimental import pallas as pl
from jax.experimental.pallas import tpu as pltpu
from jax.sharding import Mesh
from jax.sharding import PartitionSpec as P

HEADS = 16
HEAD_DIM = 128


NORM_EPS = 1e-06
ROPE_BASE = 500000.0
MASK_FILL = -1e30

SEQ = ("z", "y")
DP = ("x", "core")
FEED = ("z", "core")
REST = ("x", "y")
ALL = ("x", "core", "z", "y")
SWAP = [(0, 1), (1, 0)]
F32 = jnp.float32
BF16 = jnp.bfloat16


def matmul(left_mat, right_mat):
    return jnp.dot(left_mat, right_mat, preferred_element_type=F32)


def dot_right_t(left_mat, right_mat):
    return lax.dot_general(
        left_mat, right_mat, (((1,), (1,)), ((), ())), preferred_element_type=F32
    )


def dot_left_t(left_mat, right_mat):
    return lax.dot_general(
        left_mat, right_mat, (((0,), (0,)), ((), ())), preferred_element_type=F32
    )


def norm_apply(array_in, gain_vec):
    factor = lax.rsqrt(jnp.mean(array_in * array_in, axis=-1, keepdims=True) + NORM_EPS)
    return (array_in * factor * gain_vec, factor)


def norm_back(array_in, factor, gain_vec, grad_in):
    gain_term = jnp.sum(grad_in * array_in * factor, axis=0)
    scaled = grad_in * gain_vec
    grad_out = factor * scaled - array_in * (factor * factor * factor) * jnp.mean(
        scaled * array_in, axis=-1, keepdims=True
    )
    return (grad_out, gain_term)


def turn_tables(tok_count):
    half_dim = HEAD_DIM // 2
    position = jnp.arange(tok_count).astype(F32)
    inverse = jnp.exp(-(jnp.arange(half_dim).astype(F32) / half_dim) * math.log(ROPE_BASE))
    angles = position[:, None] * inverse[None, :]
    cosine, sine_t = jnp.cos(angles), jnp.sin(angles)
    return (
        jnp.concatenate([cosine, cosine], axis=1),
        jnp.concatenate([-sine_t, sine_t], axis=1),
    )


def rotate(array_in, cosine, sine_t):
    return array_in * cosine + pltpu.roll(array_in, HEAD_DIM // 2, 1) * sine_t


def rotate_back(array_in, cosine, sine_t):
    return array_in * cosine - pltpu.roll(array_in, HEAD_DIM // 2, 1) * sine_t


def exchange(array_in, axes):
    return lax.all_to_all(array_in, axes, split_axis=0, concat_axis=0, tiled=True)


def spread(array_in, axes):
    count = lax.axis_size(axes)
    return exchange(jnp.broadcast_to(array_in[None], (count,) + array_in.shape), axes)


def tie(value, *earlier):
    return lax.optimization_barrier((value,) + earlier)[0]


def ring_order(count):
    return [0] + list(range(1, count, 2)) + [v for v in range(count - 1, 0, -1) if v % 2 == 0]


def core_swap(array_in):
    return lax.ppermute(array_in, "core", SWAP)


def pick(array_in, at, axis=0):
    return lax.dynamic_index_in_dim(array_in, at, axis, keepdims=False)


def visible(doc_col, doc_row, first, rows, width):
    at = first + lax.broadcasted_iota(jnp.int32, (rows, width), 0)
    of = lax.broadcasted_iota(jnp.int32, (rows, width), 1)
    return (of <= at) & (doc_col == doc_row)


def attend_kernel(
    step,
    q_lin,
    k_lin,
    v_lin,
    factors,
    gain_q,
    gain_k,
    cosine,
    sine_t,
    doc_col,
    doc_row,
    queries,
    keys,
    values,
    totals,
    attended,
):
    cos, sin = cosine[...], sine_t[...]
    queries[...] = rotate(q_lin[...] * factors[:, 0:1] * gain_q[...], cos, sin).astype(BF16)
    keys[...] = rotate(k_lin[...] * factors[:, 1:2] * gain_k[...], cos, sin).astype(BF16)
    values[...] = v_lin[...].astype(BF16)
    scale = 1.0 / math.sqrt(HEAD_DIM)
    for first in range(0, queries.shape[0], step):
        width = first + step
        mine = pl.ds(first, step)
        scores = dot_right_t(queries[mine, :], keys[0:width, :]) * scale
        seen = visible(doc_col[mine, :], doc_row[:, 0:width], first, step, width)
        scores = jnp.where(seen, scores, MASK_FILL)
        row_max = jnp.max(scores, axis=1, keepdims=True)
        row_sum = jnp.sum(jnp.exp(scores - row_max), axis=1, keepdims=True)
        total = row_max + jnp.log(row_sum)
        probs = jnp.exp(scores - total).astype(BF16)
        totals[0, mine, :] = total
        attended[mine, :] = matmul(probs, values[0:width, :]).astype(BF16)


def attend_back_kernel(
    step,
    queries,
    keys,
    values,
    totals,
    g_att,
    q_lin,
    k_lin,
    gain_q,
    gain_k,
    cosine,
    sine_t,
    doc_col,
    doc_row,
    grad_q,
    grad_k,
    grad_v,
    dot_q,
    dot_k,
    k_sum,
    v_sum,
):
    scale = 1.0 / math.sqrt(HEAD_DIM)
    k_sum[...] = jnp.zeros_like(k_sum)
    v_sum[...] = jnp.zeros_like(v_sum)
    for first in range(0, queries.shape[0], step):
        width = first + step
        mine, upto = pl.ds(first, step), pl.ds(0, width)
        scores = dot_right_t(queries[mine, :], keys[upto, :]) * scale
        seen = visible(doc_col[mine, :], doc_row[:, 0:width], first, step, width)
        scores = jnp.where(seen, scores, MASK_FILL)
        prob_full = jnp.exp(scores - totals[0, mine, :])
        grad_probs = dot_right_t(g_att[mine, :], values[upto, :])
        offsets = jnp.sum(prob_full * grad_probs, axis=1, keepdims=True)
        grad_scores = (prob_full * (grad_probs - offsets)).astype(BF16)
        back = matmul(grad_scores, keys[upto, :]) * scale
        back = rotate_back(back, cosine[mine, :], sine_t[mine, :])
        grad_q[mine, :] = back
        dot_q[0, mine, :] = jnp.sum(back * gain_q[...] * q_lin[mine, :], axis=1, keepdims=True)
        k_sum[upto, :] += dot_left_t(grad_scores, queries[mine, :])
        v_sum[upto, :] += dot_left_t(prob_full.astype(BF16), g_att[mine, :])
    back = rotate_back(k_sum[...] * scale, cosine[...], sine_t[...])
    grad_k[...] = back
    dot_k[0] = jnp.sum(back * gain_k[...] * k_lin[...], axis=1, keepdims=True)
    grad_v[...] = v_sum[...].astype(BF16)


def head_specs(length, heads):
    def part(offset):
        return pl.BlockSpec((length, HEAD_DIM), lambda h: (0, h + offset))

    def gain():
        return pl.BlockSpec((1, HEAD_DIM), lambda h: (0, h))

    def whole(shape):
        return pl.BlockSpec(shape, lambda h: (0, 0))

    each = pl.BlockSpec((1, length, 1), lambda h: (h, 0, 0))
    table = whole((length, HEAD_DIM))
    docs = [whole((length, 1)), whole((1, length))]
    return part, gain, whole, each, table, docs


def attend(qkv, factors, gain_q, gain_k, tables, docs, heads):
    length = qkv.shape[0]
    part, gain, whole, each, table, doc_specs = head_specs(length, heads)
    low = jax.ShapeDtypeStruct((length, heads * HEAD_DIM), BF16)
    step = min(256, length)
    pairs = heads * length * length * HEAD_DIM
    return pl.pallas_call(
        lambda *refs: attend_kernel(step, *refs),
        grid=(heads,),
        in_specs=[part(0), part(heads), part(2 * heads), whole((length, 2)), gain(), gain()]
        + [table, table]
        + doc_specs,
        out_specs=[part(0), part(0), part(0), each, part(0)],
        out_shape=[low, low, low, jax.ShapeDtypeStruct((heads, length, 1), F32), low],
        compiler_params=pltpu.CompilerParams(vmem_limit_bytes=58 * 1024 * 1024),
        cost_estimate=pl.CostEstimate(
            flops=3 * pairs, bytes_accessed=qkv.size * 6, transcendentals=heads * length * length
        ),
    )(qkv, qkv, qkv, factors, gain_q, gain_k, *tables, *docs)


def attend_back(saved, g_att, qkv, gain_q, gain_k, tables, docs, heads):
    queries, keys, values, totals = saved
    length = qkv.shape[0]
    part, gain, whole, each, table, doc_specs = head_specs(length, heads)
    flat = jax.ShapeDtypeStruct((length, heads * HEAD_DIM), F32)
    low = jax.ShapeDtypeStruct((length, heads * HEAD_DIM), BF16)
    line = jax.ShapeDtypeStruct((heads, length, 1), F32)
    step = min(256, length)
    pairs = heads * length * length * HEAD_DIM
    return pl.pallas_call(
        lambda *refs: attend_back_kernel(step, *refs),
        grid=(heads,),
        in_specs=[part(0), part(0), part(0), each, part(0), part(0), part(heads), gain(), gain()]
        + [table, table]
        + doc_specs,
        out_specs=[part(0), part(0), part(0), each, each],
        out_shape=[flat, flat, low, line, line],
        scratch_shapes=[pltpu.VMEM((length, HEAD_DIM), F32)] * 2,
        compiler_params=pltpu.CompilerParams(vmem_limit_bytes=58 * 1024 * 1024),
        cost_estimate=pl.CostEstimate(
            flops=7 * pairs, bytes_accessed=qkv.size * 8, transcendentals=heads * length * length
        ),
    )(queries, keys, values, totals, g_att, qkv, qkv, gain_q, gain_k, *tables, *docs)


def feed_kernel(part, other, w_g, w_u, w_d, *refs):
    hid, gate, upward, active, mine, away, total = refs[-7:]
    block, tokens = pl.program_id(0), part.shape[0]

    @pl.when(block == 0)
    def _():
        hid[:tokens, :] = part[...]
        hid[tokens:, :] = other[...]

    g = matmul(hid[...], w_g[...])
    u = matmul(hid[...], w_u[...])
    a = (g * (1.0 / (1.0 + jnp.exp(-g))) * u).astype(BF16)
    gate[...], upward[...], active[...] = g, u, a
    term = dot_right_t(a, w_d[...])

    @pl.when(block == 0)
    def _():
        total[...] = term

    @pl.when(block > 0)
    def _():
        total[...] += term

    @pl.when(block == pl.num_programs(0) - 1)
    def _():
        mine[...] = total[:tokens, :]
        away[...] = total[tokens:, :].astype(BF16)


def feed_back_kernel(part, other, w_g, w_u, w_d, gate, upward, *refs):
    g_res, g_gate, g_up, mine, away, total = refs[-6:]
    block, tokens = pl.program_id(0), part.shape[0]

    @pl.when(block == 0)
    def _():
        g_res[:tokens, :] = part[...]
        g_res[tokens:, :] = other[...]

    a = matmul(g_res[...], w_d[...])
    g, u = gate[...], upward[...]
    s = 1.0 / (1.0 + jnp.exp(-g))
    gg = (a * u * s * (1.0 + g * (1.0 - s))).astype(BF16)
    gu = (a * g * s).astype(BF16)
    g_gate[...], g_up[...] = gg, gu
    term = dot_right_t(gg, w_g[...]) + dot_right_t(gu, w_u[...])

    @pl.when(block == 0)
    def _():
        total[...] = term

    @pl.when(block > 0)
    def _():
        total[...] += term

    @pl.when(block == pl.num_programs(0) - 1)
    def _():
        mine[...] = total[:tokens, :]
        away[...] = total[tokens:, :].astype(BF16)


def feed_step(at, count, pair, weights, saved, held, kernel, dtypes):
    tokens, width = pair[0].shape
    feed = weights[0].shape[1]
    step = min(512, feed)
    rows = 2 * tokens
    block = pl.BlockSpec((rows, step), lambda f: (at, f))
    part = pl.BlockSpec((tokens, width), lambda f: (0, 0))
    full = pl.BlockSpec((rows, width), lambda f: (at, 0))
    n_in = 5 + len(saved)
    shapes = [jax.ShapeDtypeStruct((count * rows, width), BF16)]
    shapes += [jax.ShapeDtypeStruct((count * rows, feed), d) for d in dtypes]
    tail = [jax.ShapeDtypeStruct((tokens, width), d) for d in (F32, BF16)]
    flops = 6 * rows * width * feed
    return pl.pallas_call(
        kernel,
        grid=(feed // step,),
        in_specs=[part, part]
        + [pl.BlockSpec((width, step), lambda f: (0, f))] * 3
        + [block] * len(saved)
        + [pl.BlockSpec(memory_space=pl.ANY)] * len(held),
        out_specs=[full] + [block] * len(dtypes) + [part, part],
        out_shape=shapes + tail,
        scratch_shapes=[pltpu.VMEM((rows, width), F32)],
        input_output_aliases={n_in + k: k for k in range(len(held))},
        compiler_params=pltpu.CompilerParams(vmem_limit_bytes=32 * 1024 * 1024),
        cost_estimate=pl.CostEstimate(
            flops=flops, bytes_accessed=6 * width * feed, transcendentals=rows * feed
        ),
    )(*pair, *weights, *saved, *held)


def body(
    inputs,
    doc_lengths,
    w_query,
    w_key,
    w_value,
    w_out,
    gain_query,
    gain_key,
    gain_attn,
    w_gate,
    w_up,
    w_down,
    gain_ffn,
    cotangent,
):
    _, tok_count, model_width = inputs.shape
    n_x, n_core, n_z, n_y = (lax.axis_size(a) for a in ALL)
    n_seq, n_dp, n_all = n_z * n_y, n_x * n_core, n_x * n_core * n_z * n_y
    seq_at = lax.axis_index(SEQ)
    length = tok_count * n_seq
    score_scale = 1.0 / math.sqrt(HEAD_DIM)
    own_rows = w_query.shape[0]
    own_width = model_width // n_seq
    own_heads = own_width // HEAD_DIM
    feed_width = w_gate.shape[1]
    n_feed = n_core * n_z
    own_feed = feed_width // n_feed
    x_at, core_at, z_at, y_at = (lax.axis_index(a) for a in ALL)
    order = ring_order(n_z)
    ring = [(order[i], order[(i + 1) % n_z]) for i in range(n_z)]
    behind = jnp.array(
        [[order[(order.index(z) - s) % n_z] for z in range(n_z)] for s in range(n_z)], jnp.int32
    )
    tokens = inputs[0]

    def ring_send(part):
        return lax.ppermute(part, "z", ring)

    def seq_gather(own):
        chunks, held = [], own
        for step in range(n_z):
            chunks += [held, lax.ppermute(held, "y", SWAP)]
            if step < n_z - 1:
                held = ring_send(held)
        return jnp.concatenate(chunks, axis=0)

    def row_gather(own, gates):
        chunks, held = [], own
        for step in range(n_z):
            chunks.append((held, lax.ppermute(held, "y", SWAP)))
            if step < n_z - 1:
                held = ring_send(tie(held, *gates(step, held)))

        def whole(first, count):
            out = jnp.zeros((n_seq * count, own.shape[1]), own.dtype)
            for step, pair in enumerate(chunks):
                for at_y, part in zip((y_at, 1 - y_at), pair):
                    at = (behind[step, z_at] * n_y + at_y) * count
                    part = part[first : first + count]
                    out = lax.dynamic_update_slice(out, part, (at, 0))
            return out

        return whole(0, tok_count), whole(tok_count, own.shape[0] - tok_count), held

    def dp_gather(mine):
        out = jnp.zeros((n_x, n_core) + mine.shape, mine.dtype)
        for at_x, part in ((x_at, mine), (1 - x_at, lax.ppermute(mine, "x", SWAP))):
            for at_core, block in ((core_at, part), (1 - core_at, core_swap(part))):
                block = block[None, None]
                out = lax.dynamic_update_slice(out, block, (at_x, at_core, 0, 0))
        return out.reshape((n_dp * mine.shape[0], mine.shape[1]))

    def seq_order(array_in):
        chunks = []
        for step in range(n_z):
            for at_y in (y_at, 1 - y_at):
                first = (behind[step, z_at] * n_y + at_y) * tok_count
                chunks.append(lax.dynamic_slice_in_dim(array_in, first, tok_count))
        return jnp.concatenate(chunks, axis=0)

    def seq_sum(part_of, *last):
        total = None
        for step in list(range(1, n_z)) + [0]:
            part = part_of(behind[step, z_at], *(() if step else last))
            part = part.reshape(n_y, tok_count, model_width)
            away = lax.ppermute(pick(part, 1 - y_at).astype(BF16), "y", SWAP)
            mine = pick(part, y_at) + away.astype(F32)
            if total is not None:
                mine = mine + ring_send(total.astype(BF16)).astype(F32)
            total = mine
        return total

    def feed_weights(mats, earlier):
        blocks = jnp.stack(mats).reshape(len(mats), own_rows, n_feed, own_feed)
        mine = exchange(tie(blocks.transpose(2, 0, 1, 3), *earlier), FEED)
        return [mine[:, at].reshape(n_feed * own_rows, own_feed) for at in range(len(mats))]

    def rest_send(mine):
        return mine, lax.ppermute(mine, "y", SWAP), lax.ppermute(mine, "x", SWAP)

    def rest_gather(sent, corner, later):
        mine, over_y, over_x = sent
        mine = tie(mine, later)
        whole = jnp.zeros((n_x, n_y) + mine.shape, BF16)
        for at_x, at_y, part in (
            (x_at, y_at, mine),
            (1 - x_at, y_at, over_x),
            (x_at, 1 - y_at, over_y),
            (1 - x_at, 1 - y_at, corner),
        ):
            whole = lax.dynamic_update_slice(whole, part[None, None], (at_x, at_y, 0, 0))
        return whole.reshape(model_width, own_feed)

    def seq_total(term):
        return jnp.sum(spread(term, SEQ), axis=0)

    def to_feed_order(array_in):
        lead = array_in.shape[:-1]
        parts = array_in.reshape((-1, n_x, n_core, n_z, n_y, own_rows))
        return parts.transpose(0, 1, 4, 3, 2, 5).reshape(lead + (model_width,))

    def from_feed_order(array_in):
        lead = array_in.shape[:-1]
        parts = array_in.reshape((-1, n_x, n_y, n_z, n_core, own_rows))
        return parts.transpose(0, 1, 4, 3, 2, 5).reshape(lead + (model_width,))

    gains = spread(jnp.stack([gain_query, gain_key, gain_attn, gain_ffn]), ALL)
    gains = gains.transpose(1, 0, 2).reshape(4, model_width).astype(F32)
    my_gq = lax.dynamic_slice_in_dim(gains[0:1], seq_at * own_width, own_width, 1)
    my_gk = lax.dynamic_slice_in_dim(gains[1:2], seq_at * own_width, own_width, 1)
    gain_a, gain_f = to_feed_order(gains[2]), to_feed_order(gains[3])

    w_heads = jnp.stack([w_query, w_key, w_value])
    w_heads = w_heads.reshape(3, own_rows, n_seq, own_width).transpose(2, 1, 0, 3)
    w_heads = w_heads.reshape(n_seq, own_rows, 3 * own_width)
    w_heads = exchange(tie(w_heads, gains), SEQ)
    w_mine = w_heads.reshape(n_seq * own_rows, 3 * own_width)

    w_heads = dp_gather(w_mine)
    def gates(step, held):
        return (w_mine,) if step == 1 else ()

    own = jnp.concatenate([tokens, to_feed_order(w_out)])
    x_row, w_out_mine, x_last = row_gather(own, gates)
    moved = feed_weights([w_gate, w_up], (x_last,))

    qkv = matmul(x_row, w_heads)
    q_lin, k_lin = qkv[:, :own_width], qkv[:, own_width : 2 * own_width]
    squares = jnp.stack([jnp.sum(q_lin * q_lin, axis=1), jnp.sum(k_lin * k_lin, axis=1)])
    squares = seq_total(squares) / model_width
    factors = lax.rsqrt(squares + NORM_EPS).T
    q_factor, k_factor = factors[:, 0:1], factors[:, 1:2]
    tables = turn_tables(length)
    doc_ends = jnp.cumsum(doc_lengths[0])
    position = jnp.arange(length)
    doc_ids = jnp.sum((position[:, None] >= doc_ends[None, :]).astype(jnp.int32), axis=1)
    docs = (doc_ids[:, None], doc_ids[None, :])
    w_u = lax.all_gather(moved[1], REST, axis=0, tiled=True)
    sent_g = rest_send(tie(moved[0], squares))
    moved += feed_weights([w_down.T], (squares,))
    sent_d = rest_send(moved[2])
    *saved, attended = attend(qkv, factors, my_gq, my_gk, tables, docs, own_heads)

    corner_g = lax.ppermute(sent_g[1], "x", SWAP)
    att_tok = tie(attended.reshape(n_seq, tok_count, own_width), *sent_g)
    att_tok = exchange(att_tok, SEQ)
    corner_d = lax.ppermute(sent_d[2], "y", SWAP)
    att_tok = att_tok.transpose(1, 0, 2).reshape(tok_count, model_width)
    full_o = dp_gather(w_out_mine)
    branch = matmul(att_tok, full_o)
    w_g = rest_gather(sent_g, corner_g, branch)
    w_d = rest_gather(sent_d, corner_d, branch)
    branch_norm, branch_factor = norm_apply(branch, gain_a)
    hidden = to_feed_order(tokens).astype(F32) + branch_norm
    hidden_low = hidden.astype(BF16)

    def feed_pass(own, saved, kernel, dtypes, gate=()):
        held, total, rows = [], None, own
        for at in range(n_z):
            pair = (rows, core_swap(rows))
            if at < n_z - 1:
                rows = ring_send(tie(rows, *gate) if gate and at == 1 else rows)
            if at > 2:
                pair = tie(pair, total)
            *held, mine, away = feed_step(
                at, n_z, pair, (w_g, w_u, w_d), saved, held, kernel, dtypes
            )
            if at == 0:
                first = (mine, away)
            else:
                total = add_up(mine, away, total)
        return held, add_up(*first, total)

    def add_up(mine, away, total):
        mine = mine + core_swap(away).astype(F32)
        if total is not None:
            mine = mine + ring_send(total.astype(BF16)).astype(F32)
        return mine

    (hid, gate, upward, active), result = feed_pass(
        hidden_low, (), feed_kernel, (F32, F32, BF16), sent_d
    )
    result_norm, result_factor = norm_apply(result, gain_f)
    output = from_feed_order((hidden + result_norm).astype(BF16))

    grad_top = to_feed_order(cotangent[0]).astype(F32)
    grad_result, ffn_gain_term = norm_back(result, result_factor, gain_f, grad_top)
    def token_sum(left, right):
        return dot_left_t(left, right).astype(BF16)

    def rest_sum(term):
        return lax.psum_scatter(term, REST, scatter_dimension=0, tiled=True)

    def feed_home(term):
        return exchange(term.reshape(n_feed, own_rows, own_feed), FEED)

    def feed_rows(term):
        return term.transpose(1, 0, 2).reshape(own_rows, feed_width).astype(F32)

    def dp_sum(term):
        rows = term.shape[0] // n_dp

        def of(array_in, at):
            return lax.dynamic_slice_in_dim(array_in, at * rows, rows)

        def cores(at):
            return jnp.concatenate([of(term, x * n_core + at) for x in range(n_x)])

        away = core_swap(cores(1 - core_at))
        term = (cores(core_at).astype(F32) + away.astype(F32)).astype(BF16)
        away = lax.ppermute(of(term, 1 - x_at), "x", SWAP)
        return (of(term, x_at).astype(F32) + away.astype(F32)).astype(BF16)

    (g_res, g_gate, g_up), grad_ffn = feed_pass(
        grad_result.astype(BF16), (gate, upward), feed_back_kernel, (BF16, BF16), (output,)
    )
    grad_hidden = grad_top + grad_ffn
    term_d = token_sum(g_res, active)
    sum_d = rest_sum(term_d)
    term_g, term_u = token_sum(hid, g_gate), token_sum(hid, g_up)

    grad_branch, attn_gain_term = norm_back(branch, branch_factor, gain_a, grad_hidden)
    grad_branch = grad_branch.astype(BF16)
    grad_attended = dot_right_t(grad_branch, full_o).astype(BF16)
    g_att = grad_attended.reshape(tok_count, n_seq, own_width).transpose(1, 0, 2)
    g_att = exchange(g_att, SEQ).reshape(length, own_width)
    g_att = tie(g_att, term_g, term_u)
    sum_g, sum_u = rest_sum(term_g), rest_sum(term_u)

    grad_q, grad_k, grad_v, dot_q, dot_k = attend_back(
        saved, g_att, qkv, my_gq, my_gk, tables, docs, own_heads
    )
    dots = jnp.stack([jnp.sum(dot_q, axis=(0, 2)), jnp.sum(dot_k, axis=(0, 2))])
    branch_row = seq_gather(from_feed_order(tie(grad_branch, grad_attended)))
    hidden_back, ffn_gain_term, attn_gain_term = [
        from_feed_order(tie(a, grad_attended))
        for a in (grad_hidden, ffn_gain_term, attn_gain_term)
    ]
    early = (branch_row, hidden_back, ffn_gain_term, attn_gain_term)
    dots = seq_total(tie(dots, *early)) / model_width
    home_d = feed_home(tie(sum_d, dots))
    grad_w_down = feed_rows(home_d).T

    grad_w_out = dot_left_t(seq_order(attended), branch_row).astype(BF16)
    grad_w_out = dp_sum(grad_w_out)
    home = [(d * n_seq + s, s * n_dp + d) for d in range(n_dp) for s in range(n_seq)]
    grad_w_out = lax.ppermute(grad_w_out, ALL, home)
    grad_w_out = grad_w_out.astype(F32)


    def lin_back(grad_in, lin, factor, gain_vec, mean_dot):
        gain_term = jnp.sum(grad_in * lin * factor, axis=0)
        grad_out = factor * (grad_in * gain_vec) - lin * (factor * factor * factor) * mean_dot
        return grad_out.astype(BF16), gain_term

    grad_q_lin, query_gain_term = lin_back(grad_q, q_lin, q_factor, my_gq, dots[0][:, None])
    grad_k_lin, key_gain_term = lin_back(grad_k, k_lin, k_factor, my_gk, dots[1][:, None])
    grad_lin = jnp.concatenate([grad_q_lin, grad_k_lin, grad_v], axis=1)

    def place(term):
        mine = jnp.arange(n_seq)[:, None] == seq_at
        return jnp.where(mine, term[None, :], 0.0).reshape(model_width)

    gain_terms = jnp.stack(
        [
            place(query_gain_term),
            place(key_gain_term),
            attn_gain_term,
            ffn_gain_term,
        ]
    )
    gain_terms = gain_terms.reshape(4, n_all, own_rows).transpose(1, 0, 2)
    gain_grads = jnp.sum(exchange(gain_terms, ALL), axis=0)

    def row_part(z_of, *earlier):
        rows = lax.dynamic_slice_in_dim(grad_lin, z_of * n_y * tok_count, n_y * tok_count)
        if earlier:
            rows = tie(rows, *earlier)
        return dot_right_t(rows, w_heads)

    grad_input = hidden_back + seq_sum(row_part, grad_w_down, grad_w_out)

    grad_heads = dot_left_t(x_row, grad_lin).astype(BF16)
    grad_heads = dp_sum(grad_heads)
    home_g = feed_home(tie(sum_g, home_d))
    home_u = feed_home(tie(sum_u, home_g, gain_grads, grad_w_out))
    grad_w_gate, grad_w_up = feed_rows(home_g), feed_rows(home_u)
    grad_heads = exchange(grad_heads.reshape(n_seq, own_rows, 3 * own_width), SEQ)
    grad_heads = grad_heads.reshape(n_seq, own_rows, 3, own_width).transpose(2, 1, 0, 3)
    grad_heads = grad_heads.reshape(3, own_rows, model_width).astype(F32)

    return (
        output[None],
        grad_input[None],
        grad_heads[0],
        grad_heads[1],
        grad_heads[2],
        grad_w_out,
        gain_grads[0],
        gain_grads[1],
        gain_grads[2],
        grad_w_gate,
        grad_w_up,
        grad_w_down,
        gain_grads[3],
    )


def plain_rotation(first_pos, tok_count):
    half_dim = HEAD_DIM // 2
    position = (first_pos + jnp.arange(tok_count)).astype(jnp.float32)
    inverse = jnp.exp(-(jnp.arange(half_dim).astype(jnp.float32) / half_dim) * math.log(ROPE_BASE))
    angles = position[:, None] * inverse[None, :]
    return (jnp.cos(angles)[None, :, None, :], jnp.sin(angles)[None, :, None, :])


def plain_rotate(array_in, cosine, sine_t, turn_sign):
    half_dim = array_in.shape[-1] // 2
    first_half = array_in[..., :half_dim]
    second_half = array_in[..., half_dim:]
    return jnp.concatenate(
        [
            first_half * cosine - turn_sign * second_half * sine_t,
            second_half * cosine + turn_sign * first_half * sine_t,
        ],
        axis=-1,
    )


def plain_body(
    inputs,
    doc_lengths,
    w_query,
    w_key,
    w_value,
    w_out,
    gain_query,
    gain_key,
    gain_attn,
    w_gate,
    w_up,
    w_down,
    gain_ffn,
    cotangent,
):
    row_count, tok_count, model_width = inputs.shape
    length = tok_count * lax.axis_size("seq")
    first_pos = lax.axis_index("seq") * tok_count
    score_scale = 1.0 / math.sqrt(HEAD_DIM)
    tokens = inputs.reshape(row_count * tok_count, model_width)

    def heads_first(array_in):
        return array_in.reshape(row_count, tok_count, HEADS, HEAD_DIM).transpose(2, 0, 1, 3)

    def heads_last(array_in):
        return array_in.transpose(1, 2, 0, 3).reshape(row_count * tok_count, HEADS * HEAD_DIM)

    full_q, full_k, full_v, full_o, full_gq, full_gk, full_ga = (
        lax.all_gather(w_query, ("dp", "seq"), axis=0, tiled=True),
        lax.all_gather(w_key, ("dp", "seq"), axis=0, tiled=True),
        lax.all_gather(w_value, ("dp", "seq"), axis=0, tiled=True),
        lax.all_gather(w_out, ("dp", "seq"), axis=0, tiled=True),
        lax.all_gather(gain_query, ("dp", "seq"), axis=0, tiled=True),
        lax.all_gather(gain_key, ("dp", "seq"), axis=0, tiled=True),
        lax.all_gather(gain_attn, ("dp", "seq"), axis=0, tiled=True),
    )
    cosine, sine_t = plain_rotation(first_pos, tok_count)
    q_lin = matmul(tokens, full_q)
    k_lin = matmul(tokens, full_k)
    v_lin = matmul(tokens, full_v)
    q_norm, q_factor = norm_apply(q_lin, full_gq.astype(jnp.float32))
    k_norm, k_factor = norm_apply(k_lin, full_gk.astype(jnp.float32))
    queries = (
        plain_rotate(q_norm.reshape(row_count, tok_count, HEADS, HEAD_DIM), cosine, sine_t, 1.0)
        .astype(jnp.bfloat16)
        .transpose(2, 0, 1, 3)
    )
    keys_mine = (
        plain_rotate(k_norm.reshape(row_count, tok_count, HEADS, HEAD_DIM), cosine, sine_t, 1.0)
        .astype(jnp.bfloat16)
        .transpose(2, 0, 1, 3)
    )
    values_mine = heads_first(v_lin.astype(jnp.bfloat16))
    keys_all, values_all = (
        lax.all_gather(keys_mine, "seq", axis=2, tiled=True),
        lax.all_gather(values_mine, "seq", axis=2, tiled=True),
    )
    doc_ends = jnp.cumsum(doc_lengths, axis=1)
    position = jnp.arange(length)
    doc_ids = jnp.sum((position[None, :, None] >= doc_ends[:, None, :]).astype(jnp.int32), axis=2)
    my_pos = first_pos + jnp.arange(tok_count)
    docs_mine = lax.dynamic_slice_in_dim(doc_ids, first_pos, tok_count, 1)
    allowed = (position[None, None, :] <= my_pos[None, :, None]) & (
        doc_ids[:, None, :] == docs_mine[:, :, None]
    )

    def scores_of(q_head, k_head):
        raw_scores = (
            jnp.einsum("rtd,rkd->rtk", q_head, k_head, preferred_element_type=jnp.float32)
            * score_scale
        )
        return jnp.where(allowed, raw_scores, MASK_FILL)

    def attend(head_item):
        q_head, k_head, v_head = head_item
        scores = scores_of(q_head, k_head)
        row_max = jnp.max(scores, axis=-1, keepdims=True)
        row_total = row_max + jnp.log(jnp.sum(jnp.exp(scores - row_max), axis=-1, keepdims=True))
        attn_probs = jnp.exp(scores - row_total).astype(jnp.bfloat16)
        head_out = jnp.einsum(
            "rtk,rkd->rtd", attn_probs, v_head, preferred_element_type=jnp.float32
        )
        return (head_out, row_total[..., 0])

    attn_mixed, totals = lax.map(attend, (queries, keys_all, values_all))
    attended = heads_last(attn_mixed.astype(jnp.bfloat16))
    branch = matmul(attended, full_o)
    branch_norm, branch_factor = norm_apply(branch, full_ga.astype(jnp.float32))
    hidden = tokens.astype(jnp.float32) + branch_norm
    hidden_low = hidden.astype(jnp.bfloat16)
    gate_full, up_full, down_full, ffn_gain_full = (
        lax.all_gather(w_gate, ("dp", "seq"), axis=0, tiled=True),
        lax.all_gather(w_up, ("dp", "seq"), axis=0, tiled=True),
        lax.all_gather(w_down, ("dp", "seq"), axis=1, tiled=True),
        lax.all_gather(gain_ffn, ("dp", "seq"), axis=0, tiled=True),
    )
    gate_act = matmul(hidden_low, gate_full)
    upward = matmul(hidden_low, up_full)
    gate_sig = jax.nn.sigmoid(gate_act)
    active = (gate_act * gate_sig * upward).astype(jnp.bfloat16)
    result = matmul(active, down_full)
    result_norm, result_factor = norm_apply(result, ffn_gain_full.astype(jnp.float32))
    output = (hidden + result_norm).astype(jnp.bfloat16).reshape(row_count, tok_count, model_width)
    grad_top = cotangent.reshape(row_count * tok_count, model_width).astype(jnp.float32)
    grad_result, ffn_gain_term = norm_back(
        result, result_factor, ffn_gain_full.astype(jnp.float32), grad_top
    )
    grad_result = grad_result.astype(jnp.bfloat16)
    grad_active = dot_right_t(grad_result, down_full)
    grad_gate = (grad_active * upward * gate_sig * (1.0 + gate_act * (1.0 - gate_sig))).astype(
        jnp.bfloat16
    )
    grad_up = (grad_active * gate_act * gate_sig).astype(jnp.bfloat16)
    grad_hidden = grad_top + dot_right_t(grad_gate, gate_full) + dot_right_t(grad_up, up_full)
    feedforward_grads = lax.psum_scatter(
        jnp.concatenate(
            [
                dot_left_t(hidden_low, grad_gate),
                dot_left_t(hidden_low, grad_up),
                dot_left_t(grad_result, active),
            ],
            axis=1,
        ),
        ("dp", "seq"),
        scatter_dimension=0,
        tiled=True,
    )
    grad_branch, attn_gain_term = norm_back(
        branch, branch_factor, full_ga.astype(jnp.float32), grad_hidden
    )
    grad_branch = grad_branch.astype(jnp.bfloat16)
    back_q, back_k, back_v, back_o, back_gq, back_gk = (
        lax.all_gather(w_query, ("dp", "seq"), axis=0, tiled=True),
        lax.all_gather(w_key, ("dp", "seq"), axis=0, tiled=True),
        lax.all_gather(w_value, ("dp", "seq"), axis=0, tiled=True),
        lax.all_gather(w_out, ("dp", "seq"), axis=0, tiled=True),
        lax.all_gather(gain_query, ("dp", "seq"), axis=0, tiled=True),
        lax.all_gather(gain_key, ("dp", "seq"), axis=0, tiled=True),
    )
    grad_attended = dot_right_t(grad_branch, back_o).astype(jnp.bfloat16)
    grad_w_out_term = dot_left_t(attended, grad_branch)
    grad_mixed = heads_first(grad_attended)

    def head_back(head_item):
        q_head, k_head, v_head, g_head, t_head = head_item
        prob_full = jnp.exp(scores_of(q_head, k_head) - t_head[..., None])
        grad_probs = jnp.einsum("rtd,rkd->rtk", g_head, v_head, preferred_element_type=jnp.float32)
        offsets = jnp.sum(prob_full * grad_probs, axis=-1, keepdims=True)
        grad_scores = (prob_full * (grad_probs - offsets)).astype(jnp.bfloat16)
        grad_q = (
            jnp.einsum("rtk,rkd->rtd", grad_scores, k_head, preferred_element_type=jnp.float32)
            * score_scale
        )
        grad_k = (
            jnp.einsum("rtk,rtd->rkd", grad_scores, q_head, preferred_element_type=jnp.float32)
            * score_scale
        )
        grad_v = jnp.einsum(
            "rtk,rtd->rkd",
            prob_full.astype(jnp.bfloat16),
            g_head,
            preferred_element_type=jnp.float32,
        )
        return (grad_q, grad_k, grad_v)

    grad_queries, key_terms, value_terms = lax.map(
        head_back, (queries, keys_all, values_all, grad_mixed, totals)
    )
    grad_keys, grad_values = (
        lax.psum_scatter(
            key_terms.astype(jnp.bfloat16), "seq", scatter_dimension=2, tiled=True
        ).astype(jnp.float32),
        lax.psum_scatter(
            value_terms.astype(jnp.bfloat16), "seq", scatter_dimension=2, tiled=True
        ).astype(jnp.float32),
    )
    grad_q_norm = plain_rotate(grad_queries.transpose(1, 2, 0, 3), cosine, sine_t, -1.0).reshape(
        row_count * tok_count, model_width
    )
    grad_k_norm = plain_rotate(grad_keys.transpose(1, 2, 0, 3), cosine, sine_t, -1.0).reshape(
        row_count * tok_count, model_width
    )
    grad_q_lin, query_gain_term = norm_back(
        q_lin, q_factor, back_gq.astype(jnp.float32), grad_q_norm
    )
    grad_k_lin, key_gain_term = norm_back(k_lin, k_factor, back_gk.astype(jnp.float32), grad_k_norm)
    grad_q_lin = grad_q_lin.astype(jnp.bfloat16)
    grad_k_lin = grad_k_lin.astype(jnp.bfloat16)
    grad_v_lin = heads_last(grad_values).astype(jnp.bfloat16)
    grad_input = (
        grad_hidden
        + dot_right_t(grad_q_lin, back_q)
        + dot_right_t(grad_k_lin, back_k)
        + dot_right_t(grad_v_lin, back_v)
    )
    attention_grads = (
        lax.psum_scatter(
            dot_left_t(tokens, grad_q_lin), ("dp", "seq"), scatter_dimension=0, tiled=True
        ),
        lax.psum_scatter(
            dot_left_t(tokens, grad_k_lin), ("dp", "seq"), scatter_dimension=0, tiled=True
        ),
        lax.psum_scatter(
            dot_left_t(tokens, grad_v_lin), ("dp", "seq"), scatter_dimension=0, tiled=True
        ),
        lax.psum_scatter(grad_w_out_term, ("dp", "seq"), scatter_dimension=0, tiled=True),
        lax.psum_scatter(query_gain_term, ("dp", "seq"), scatter_dimension=0, tiled=True),
        lax.psum_scatter(key_gain_term, ("dp", "seq"), scatter_dimension=0, tiled=True),
        lax.psum_scatter(attn_gain_term, ("dp", "seq"), scatter_dimension=0, tiled=True),
        lax.psum_scatter(ffn_gain_term, ("dp", "seq"), scatter_dimension=0, tiled=True),
    )
    feed_width = w_gate.shape[1]
    grad_w_gate = feedforward_grads[:, :feed_width]
    grad_w_up = feedforward_grads[:, feed_width : 2 * feed_width]
    grad_w_down = feedforward_grads[:, 2 * feed_width :].T
    return (
        output,
        grad_input.reshape(row_count, tok_count, model_width),
        attention_grads[0],
        attention_grads[1],
        attention_grads[2],
        attention_grads[3],
        attention_grads[4],
        attention_grads[5],
        attention_grads[6],
        grad_w_gate,
        grad_w_up,
        grad_w_down,
        attention_grads[7],
    )


def solution(mesh):
    n_dp, n_seq = mesh.shape["dp"], mesh.shape["seq"]
    if n_dp == 4 and n_seq % 2 == 0 and HEADS % n_seq == 0:
        grid = Mesh(mesh.devices.reshape(n_dp // 2, 2, n_seq // 2, 2), ALL)
        layer, dp, seq = body, DP, SEQ
    else:
        grid, layer, dp, seq = mesh, plain_body, ("dp",), ("seq",)
    rows = P(dp, seq, None)
    split = P(dp + seq, None)
    vector = P(dp + seq)
    down = P(None, dp + seq)
    return jax.shard_map(
        layer,
        mesh=grid,
        in_specs=(rows, P(dp, None))
        + (split,) * 4
        + (vector,) * 3
        + (split, split, down, vector, rows),
        out_specs=(rows, rows) + (split,) * 4 + (vector,) * 3 + (split, split, down, vector),
        check_vma=False,
    )
```
